32 devices in a mesh: dp: 4 (over z), chan: 8 (over y, x, core).
Axes of the slice: x: 2, y: 2, z: 4, core: 2. Of those that a mesh axis runs over, the one named last changes fastest.
Arguments:
- tokens: bfloat16 [3, 8192, 512], P(None, ('dp', 'chan')), may hold values from -6 to 6
- cotangent: bfloat16 [3, 8192, 512], P(None, ('dp', 'chan')), may hold values from -6 to 6
- lengths: int32 [3, 4], P(None, 'dp'), may hold values from 1024 to 2048, as said below
- norm_gain: bfloat16 [512], P(('dp', 'chan')), may hold values from 0.5 to 1.5
- log_step: float32 [512], P('chan'), may hold values from -6.9 to -2.3
- log_decay: float32 [512, 32], P('chan', 'dp'), may hold values from -1.5 to 0.5
- frequency: float32 [512, 32], P('chan', 'dp'), may hold values from 0 to 100
- readout_real: float32 [512, 32], P('chan', 'dp'), may hold values from -4 to 4
- readout_imaginary: float32 [512, 32], P('chan', 'dp'), may hold values from -4 to 4
- skip_gain: float32 [512], P('chan'), may hold values from -4 to 4
- out_weight: bfloat16 [512, 1024], P(('dp', 'chan')), may hold values from -0.25 to 0.25
- out_bias: bfloat16 [1024], P(('dp', 'chan')), may hold values from -3 to 3
- ffn_gain: bfloat16 [512], P(('dp', 'chan')), may hold values from 0.5 to 1.5
- in_weight: bfloat16 [512, 2048], P(('dp', 'chan')), may hold values from -0.25 to 0.25
- in_bias: bfloat16 [2048], P(('dp', 'chan')), may hold values from -3 to 3
- back_weight: bfloat16 [2048, 512], P(('dp', 'chan')), may hold values from -0.125 to 0.125
Outputs:
- block_out: bfloat16 [3, 8192, 512], P(None, ('dp', 'chan'))
- grad_tokens: bfloat16 [3, 8192, 512], P(None, ('dp', 'chan'))
- grad_norm_gain: float32 [512], P(('dp', 'chan'))
- grad_log_step: float32 [512], P('chan')
- grad_log_decay: float32 [512, 32], P('chan', 'dp')
- grad_frequency: float32 [512, 32], P('chan', 'dp')
- grad_readout_real: float32 [512, 32], P('chan', 'dp')
- grad_readout_imaginary: float32 [512, 32], P('chan', 'dp')
- grad_skip_gain: float32 [512], P('chan')
- grad_out_weight: float32 [512, 1024], P(('dp', 'chan'))
- grad_out_bias: float32 [1024], P(('dp', 'chan'))
- grad_ffn_gain: float32 [512], P(('dp', 'chan'))
- grad_in_weight: float32 [512, 2048], P(('dp', 'chan'))
- grad_in_bias: float32 [2048], P(('dp', 'chan'))
- grad_back_weight: float32 [2048, 512], P(('dp', 'chan'))
The draws below stay inside these ranges and needn't reach their ends.
Inputs may be any that keep to these rules, and one draw needn't show every extreme that they name: `lengths`: each entry is 2048 divided by a power of two; in every group some micro-batch has length 2048.
All inputs are finite; a program needn't handle non-finite values.
Results may differ from the reference program's by a relative error of at most 0.0088.
Values may be sent and summed in bfloat16 or wider, within the bound.
A program may use at most 320 MiB of HBM per device.

```python
import jax
import jax.numpy as jnp
from jax import lax

D = 512
FF = 2048
NH = 32
MB = 3
MINLEN = 1024
TOK_GROUP = 2048
GROUPS = 4
TOKENS = 8192


def draw_lengths(key, part):
    key = jax.random.fold_in(key, 11)
    deepest = (TOK_GROUP // MINLEN).bit_length() - 1
    halvings = jax.random.randint(jax.random.fold_in(key, 1), (MB, GROUPS), 0, deepest + 1)
    full_at = jax.random.randint(jax.random.fold_in(key, 2), (GROUPS,), 0, MB)
    batch_ids = jnp.arange(MB, dtype=jnp.int32)[:, None]
    group_ids = jnp.arange(GROUPS, dtype=jnp.int32)[None, :]
    halvings = jnp.where(batch_ids == full_at[None, :], 0, halvings)
    short_group = jax.random.randint(jax.random.fold_in(key, 3), (), 0, GROUPS)
    short_batch = (full_at[short_group] + 1 + jax.random.randint(jax.random.fold_in(key, 4), (), 0, MB - 1)) % MB
    halvings = jnp.where((batch_ids == short_batch) & (group_ids == short_group), deepest, halvings)
    return jnp.right_shift(jnp.full((MB, GROUPS), TOK_GROUP, jnp.int32), halvings.astype(jnp.int32))


def shard_levels(rng, extent, split, smallest, high):
    def one(position, parts):
        draws = jax.random.uniform(jax.random.fold_in(jax.random.fold_in(rng, 6), position), (parts,), jnp.float32, smallest / len(split), high / len(split))
        return jnp.repeat(jnp.exp(draws), extent[position] // parts).reshape((-1,) + (1,) * (len(extent) - position - 1))

    loudness = one(*split[0])
    for cut in split[1:]:
        loudness = loudness * one(*cut)
    return loudness


def noise(own_key, extent, scale, limit, cuts=(), held_as=jnp.bfloat16):
    drawn = scale * jax.random.normal(own_key, extent, jnp.float32)
    if cuts:
        drawn = drawn * shard_levels(own_key, extent, cuts, -0.22, 0.18)
    return jnp.clip(drawn, -limit, limit).astype(held_as)


def setup_inputs(seed: int = 0) -> dict:
    keys = jax.random.split(jax.random.key(seed), 17)
    return {
        "tokens": noise(keys[0], (MB, TOKENS, D), 1.0, 6.0, ((1, 32),)),
        "cotangent": noise(keys[1], (MB, TOKENS, D), 1.0, 6.0, ((1, 32),)),
        "lengths": draw_lengths(jax.random.fold_in(keys[16], 71), 0),
        "norm_gain": jnp.clip(1.0 + 0.1 * jax.random.normal(keys[3], (D,), jnp.float32), 0.5, 1.5).astype(jnp.bfloat16),
        "log_step": jnp.clip(-6.9 + 4.6000001430511475 * jax.random.uniform(keys[4], (D,), jnp.float32) ** shard_levels(keys[4], (D,), ((0, 8),), -0.2, 0.2), -6.9, -2.3),
        "log_decay": jnp.clip(-1.5 + 2.0 * jax.random.uniform(keys[5], (D, NH), jnp.float32) ** shard_levels(keys[5], (D, NH), ((0, 8), (1, 4)), -0.2, 0.2), -1.5, 0.5),
        "frequency": jnp.clip(100.0 * jax.random.uniform(keys[6], (D, NH), jnp.float32) ** shard_levels(keys[6], (D, NH), ((0, 8), (1, 4)), -0.2, 0.2), 0.0, 100.0),
        "readout_real": noise(keys[7], (D, NH), 0.5, 4.0, ((0, 8), (1, 4)), jnp.float32),
        "readout_imaginary": noise(keys[8], (D, NH), 0.5, 4.0, ((0, 8), (1, 4)), jnp.float32),
        "skip_gain": noise(keys[9], (D,), 1.0, 4.0, ((0, 8),), jnp.float32),
        "out_weight": noise(keys[10], (D, 2 * D), D ** -0.5, 0.25, ((0, 32),)),
        "out_bias": noise(keys[11], (2 * D,), 0.3, 3.0, ((0, 32),)),
        "ffn_gain": jnp.clip(1.0 + 0.1 * jax.random.normal(keys[12], (D,), jnp.float32), 0.5, 1.5).astype(jnp.bfloat16),
        "in_weight": noise(keys[13], (D, FF), D ** -0.5, 0.25, ((0, 32),)),
        "in_bias": noise(keys[14], (FF,), 0.3, 3.0, ((0, 32),)),
        "back_weight": noise(keys[15], (FF, D), FF ** -0.5, 0.125, ((0, 32),)),
    }


@jax.custom_vjp
def low(v):
    return lax.optimization_barrier(v.astype(jnp.bfloat16)).astype(jnp.float32)

@jax.custom_vjp
def low_back(v):
    return v

def low_keep(v):
    return (low(v), None)

def low_pass(kept, grad):
    return (grad,)

def back_keep(v):
    return (v, None)

def back_low(kept, grad):
    return (low(grad),)
low.defvjp(low_keep, low_pass)
low_back.defvjp(back_keep, back_low)

def layer_norm(values, gain_vector):
    average = lax.optimization_barrier(jnp.mean(values, axis=-1, keepdims=True))
    centred = values - average
    spread = lax.optimization_barrier(jnp.mean(centred * centred, axis=-1, keepdims=True))
    return centred * lax.rsqrt(spread + 1e-05) * gain_vector

def exact_gelu(values):
    return jax.nn.gelu(values, approximate=False)

def mode_powers(damping, rotation, offsets):
    shaped = offsets[..., None, None]
    magnitude = jnp.exp(shaped * damping)
    return (magnitude * jnp.cos(shaped * rotation), magnitude * jnp.sin(shaped * rotation))

def lower_toeplitz(kernel):
    block_size, channels = kernel.shape
    zero_part = jnp.zeros((block_size, channels), kernel.dtype)
    row_base = jnp.concatenate([kernel[0:1], zero_part, kernel[1:][::-1]], axis=0)
    tiled = jnp.broadcast_to(row_base[None], (block_size, 2 * block_size, channels))
    flat = tiled.reshape(2 * block_size * block_size, channels)[:block_size * (2 * block_size - 1)]
    return flat.reshape(block_size, 2 * block_size - 1, channels)[:, :block_size]

def state_mix(inputs, length, log_step, log_decay, frequency, readout_real, readout_imaginary, skip_gain):
    positions, channels = inputs.shape
    block_size = min(256, positions)
    blocks = positions // block_size
    highest = lax.Precision.HIGHEST
    step_size = jnp.exp(log_step)[:, None]
    real_rate = -jnp.exp(log_decay)
    damping = step_size * real_rate
    rotation = step_size * frequency
    shrink = jnp.exp(damping)
    above_real = shrink * jnp.cos(rotation) - 1.0
    above_imag = shrink * jnp.sin(rotation)
    modulus = real_rate * real_rate + frequency * frequency
    ratio_real = (above_real * real_rate + above_imag * frequency) / modulus
    ratio_imag = (above_imag * real_rate - above_real * frequency) / modulus
    weight_real = readout_real * ratio_real - readout_imaginary * ratio_imag
    weight_imag = readout_real * ratio_imag + readout_imaginary * ratio_real
    offsets = jnp.arange(block_size + 1).astype(jnp.float32)
    power_real, power_imag = mode_powers(damping, rotation, offsets)
    kernel = 2.0 * (lax.optimization_barrier(jnp.sum(power_real[:block_size] * weight_real, axis=-1)) - lax.optimization_barrier(jnp.sum(power_imag[:block_size] * weight_imag, axis=-1)))
    places = jnp.arange(block_size).astype(jnp.int32)
    distance = places[:, None] - places[None, :]
    inside = (distance >= 0) & (places[:, None] // length == places[None, :] // length)
    toeplitz = jnp.where(inside[:, :, None], lower_toeplitz(kernel), 0.0)
    shaped = inputs.reshape(blocks, block_size, channels)
    within = jnp.einsum('tsc,bsc->btc', toeplitz, shaped, precision=highest)
    reverse_real = power_real[:block_size][::-1]
    reverse_imag = power_imag[:block_size][::-1]
    state_real = jnp.einsum('bsc,scn->bcn', shaped, reverse_real, precision=highest)
    state_imag = jnp.einsum('bsc,scn->bcn', shaped, reverse_imag, precision=highest)
    block_ids = jnp.arange(blocks).astype(jnp.int32)
    sequence = block_ids * block_size // length
    block_gap = block_ids[:, None] - 1 - block_ids[None, :]
    linked = (block_gap >= 0) & (sequence[:, None] == sequence[None, :])
    hop_real, hop_imag = mode_powers(damping, rotation, (jnp.maximum(block_gap, 0) * block_size).astype(jnp.float32))
    hop_real = jnp.where(linked[:, :, None, None], hop_real, 0.0)
    hop_imag = jnp.where(linked[:, :, None, None], hop_imag, 0.0)
    carry_real = jnp.einsum('ijcn,jcn->icn', hop_real, state_real, precision=highest) - jnp.einsum('ijcn,jcn->icn', hop_imag, state_imag, precision=highest)
    carry_imag = jnp.einsum('ijcn,jcn->icn', hop_real, state_imag, precision=highest) + jnp.einsum('ijcn,jcn->icn', hop_imag, state_real, precision=highest)
    read_real = power_real[1:] * weight_real - power_imag[1:] * weight_imag
    read_imag = power_real[1:] * weight_imag + power_imag[1:] * weight_real
    across = 2.0 * (jnp.einsum('tcn,icn->itc', read_real, carry_real, precision=highest) - jnp.einsum('tcn,icn->itc', read_imag, carry_imag, precision=highest))
    return (within + across).reshape(positions, channels) + skip_gain * inputs

def block(lengths, tokens, norm_gain, log_step, log_decay, frequency, readout_real, readout_imaginary, skip_gain, out_weight, out_bias, ffn_gain, in_weight, in_bias, back_weight):
    highest = lax.Precision.HIGHEST
    features = tokens.shape[2]
    normed = low(low_back(layer_norm(tokens, norm_gain)))
    grouped = normed.reshape(MB * GROUPS, TOK_GROUP, features)
    group_lengths = lengths.reshape(MB * GROUPS)

    def one_group(group_pair):
        return state_mix(group_pair[0], group_pair[1], log_step, log_decay, frequency, readout_real, readout_imaginary, skip_gain)
    convolved = lax.map(jax.checkpoint(one_group), (grouped, group_lengths))
    activated = low(low_back(exact_gelu(convolved))).reshape(tokens.shape)
    project = low_back(jnp.einsum('mtd,df->mtf', activated, out_weight, precision=highest) + out_bias)
    middle = tokens + project[..., :features] * jax.nn.sigmoid(project[..., features:])
    second = low(layer_norm(middle, ffn_gain))
    before = low_back(jnp.einsum('mtd,df->mtf', second, in_weight, precision=highest) + in_bias)
    hidden = low(exact_gelu(before))
    return middle + jnp.einsum('mtf,fd->mtd', hidden, back_weight, precision=highest)

def reference(tokens, cotangent, lengths, norm_gain, log_step, log_decay, frequency, readout_real, readout_imaginary, skip_gain, out_weight, out_bias, ffn_gain, in_weight, in_bias, back_weight):
    params = (tokens, norm_gain, log_step, log_decay, frequency, readout_real, readout_imaginary, skip_gain, out_weight, out_bias, ffn_gain, in_weight, in_bias, back_weight)
    floats = tuple((argument_value.astype(jnp.float32) for argument_value in params))

    def forward(*values):
        return block(lengths, *values)
    result, pullback = jax.vjp(forward, *floats)
    gradients = pullback(cotangent.astype(jnp.float32))
    return (result.astype(jnp.bfloat16), gradients[0].astype(jnp.bfloat16), gradients[1], gradients[2], gradients[3], gradients[4], gradients[5], gradients[6], gradients[7], gradients[8], gradients[9], gradients[10], gradients[11], gradients[12], gradients[13])
```

```python
import functools
import jax
import jax.numpy as jnp
from jax import lax
from jax.experimental import pallas as pl
from jax.experimental.pallas import tpu as pltpu
from jax.sharding import PartitionSpec as P

SPAN = 128
PACK = 16
HI = lax.Precision.HIGHEST


def cmul(ar, ai, br, bi):
    return ar * br - ai * bi, ar * bi + ai * br


def mode_rows(ls, ld, fr, rr, ri):
    dt = jnp.exp(ls)
    a_r = -jnp.exp(ld)
    a_i = fr
    t_r, t_i = dt * a_r, dt * a_i
    mag = jnp.exp(t_r)
    l_r, l_i = mag * jnp.cos(t_i), mag * jnp.sin(t_i)
    mod = a_r * a_r + a_i * a_i
    u_r = l_r - 1.0
    q_r = (u_r * a_r + l_i * a_i) / mod
    q_i = (l_i * a_r - u_r * a_i) / mod
    w_r, w_i = cmul(rr, ri, q_r, q_i)
    return dict(dt=dt, a_r=a_r, a_i=a_i, t_r=t_r, t_i=t_i, l_r=l_r, l_i=l_i, mod=mod,
                q_r=q_r, q_i=q_i, w_r=w_r, w_i=w_i)


def mode_prelude(modes_ref, pw_ref):
    m = mode_rows(modes_ref[0], modes_ref[1], modes_ref[2], modes_ref[3], modes_ref[4])
    r, i = m["l_r"], m["l_i"]
    for k in range(8):
        pw_ref[2 * k] = r
        pw_ref[2 * k + 1] = i
        r, i = cmul(r, i, r, i)
    pw_ref[16] = 2.0 * m["w_r"]
    pw_ref[17] = 2.0 * m["w_i"]


def group_rows(pw_ref, g):
    rows = [pw_ref[k, pl.ds(g, 1), :] for k in range(18)]
    return [jnp.broadcast_to(x, (8, 128)) for x in rows]


def power_table(rows, reverse):
    sub = lax.broadcasted_iota(jnp.int32, (8, 128), 0)
    if reverse:
        sub = 7 - sub
        r, i = jnp.ones((8, 128), jnp.float32), jnp.zeros((8, 128), jnp.float32)
    else:
        r, i = rows[0], rows[1]
    for k in range(3):
        bit = ((sub >> k) & 1) == 1
        fr = jnp.where(bit, rows[2 * k], 1.0)
        fi = jnp.where(bit, rows[2 * k + 1], 0.0)
        r, i = cmul(r, i, fr, fi)
    parts = [(r, i)]
    for k in range(3, 7):
        more = [cmul(a, b, rows[2 * k], rows[2 * k + 1]) for a, b in parts]
        parts = more + parts if reverse else parts + more
    return (jnp.concatenate([p[0] for p in parts], 0), jnp.concatenate([p[1] for p in parts], 0))


def nt(a, b, **kw):
    return lax.dot_general(a, b, (((1,), (1,)), ((), ())), preferred_element_type=jnp.float32, **kw)


def tn(a, b, **kw):
    return lax.dot_general(a, b, (((0,), (0,)), ((), ())), preferred_element_type=jnp.float32, **kw)


def nn(a, b, **kw):
    return jnp.dot(a, b, preferred_element_type=jnp.float32, **kw)


def kernel_rows(rd_r, w_r):
    t = lax.broadcasted_iota(jnp.int32, (SPAN, 128), 0)
    src = jnp.where(t == SPAN - 1, jnp.concatenate([w_r] * 16, 0), rd_r)
    pick = (lax.broadcasted_iota(jnp.int32, (8, 128), 1) // 32
            == lax.broadcasted_iota(jnp.int32, (8, 128), 0)).astype(jnp.float32)
    return pltpu.roll(nt(pick, src, precision=HI), 1, 1)


def toeplitz(row):
    base = pltpu.roll(jnp.broadcast_to(row, (8, 128)), 0, 1, stride=1, stride_axis=0)
    parts = [base] + [pltpu.roll(base, 8 * v, 1) for v in range(1, 16)]
    whole = jnp.concatenate(parts, 0)
    s = lax.broadcasted_iota(jnp.int32, (SPAN, 128), 0)
    t = lax.broadcasted_iota(jnp.int32, (SPAN, 128), 1)
    return jnp.where(t >= s, whole, 0.0).astype(jnp.bfloat16)


def lag_sums(g):
    s = lax.broadcasted_iota(jnp.int32, (SPAN, 128), 0)
    t = lax.broadcasted_iota(jnp.int32, (SPAN, 128), 1)
    g = jnp.where(t >= s, g, 0.0)
    n = SPAN
    while n > 8:
        n //= 2
        g = g[:n] + pltpu.roll(g[n:], 128 - n, 1)
    for n in (4, 2, 1):
        g = g + pltpu.roll(pltpu.roll(g, 128 - n, 1), 8 - n, 0)
    return g[0:1]


def lane_owner(rows):
    return lax.broadcasted_iota(jnp.int32, (rows, 128), 1) // 32


def fold(stack, rows):
    width = stack.shape[1]
    own = (lax.broadcasted_iota(jnp.int32, (rows, width), 1) // 32) & 3
    out = stack[:rows]
    for k in range(1, 4):
        out = jnp.where(own == k, stack[k * rows:(k + 1) * rows], out)
    return out


def spread(packed, rows):
    width = packed.shape[1]
    own = (lax.broadcasted_iota(jnp.int32, (rows, width), 1) // 32) & 3
    return jnp.concatenate([jnp.where(own == k, packed, 0.0) for k in range(4)], 0)


def gelu_pair(v):
    half = 0.5 * (1.0 + lax.erf(v * 0.7071067811865476))
    return v * half, half + v * jnp.exp(-0.5 * v * v) * 0.3989422804014327


def block_rows(r):
    return pl.ds(pl.multiple_of(r * PACK, PACK), PACK)


def unpack(src_ref, q, xs, nj, mb, h, blocks, scale=None):
    def body(j, _):
        for m in range(mb):
            for k in range(h):
                x = src_ref[j, pl.ds(q * PACK, PACK), pl.ds((m * h + k) * 128, 128)]
                xs[block_rows(m * blocks + j * h + k), :] = x.astype(jnp.float32)
        return 0
    lax.fori_loop(0, nj, body, 0)


def forward_kernel(dims, modes_ref, skip_ref, keep_ref, u_ref, act_ref, slope_ref, carry_ref, pw_ref, xs, ys, sc):
    nj, chans, mb, h = dims
    blocks = nj * h
    rows = mb * blocks
    mode_prelude(modes_ref, pw_ref)

    def one_pack(q, _):
        unpack(u_ref, q, xs, nj, mb, h, blocks)

        def states(g, _):
            rws = group_rows(pw_ref, q * 4 + g)
            p_r, p_i = power_table(rws, True)
            back = (SPAN - 1 - lax.broadcasted_iota(jnp.int32, (SPAN, 128), 0)).astype(jnp.float32)
            table = jnp.concatenate([p_r, p_i, back * p_r, back * p_i], 1).astype(jnp.bfloat16)
            x = jnp.concatenate([xs[pl.ds(4 * g + k, rows, stride=PACK), :] for k in range(4)], 0).astype(jnp.bfloat16)
            s = fold(nn(x, table), rows)
            for a in range(4):
                for m in range(mb):
                    sc[a, pl.ds(g * mb + m, blocks, stride=PACK), :] = s[m * blocks:(m + 1) * blocks, a * 128:(a + 1) * 128]
            return 0
        lax.fori_loop(0, 4, states, 0)

        def rows_of(k):
            parts = [jnp.broadcast_to(pw_ref[k, pl.ds(q * 4 + g, 1), :], (mb, 128)) for g in range(4)]
            parts.append(jnp.zeros((PACK - 4 * mb, 128), jnp.float32))
            return jnp.concatenate(parts, 0)
        h_r, h_i = rows_of(14), rows_of(15)

        def step(i, c):
            at = pl.ds(pl.multiple_of(i * PACK, PACK), PACK)
            keep = keep_ref[i]
            c = [x * keep for x in c]
            s = [sc[a, at, :] for a in range(4)]
            for a in range(4):
                carry_ref[q, a, at, :] = c[a]
            z_r, z_i = cmul(c[0], c[1], h_r, h_i)
            d_r, d_i = cmul(c[2] + SPAN * c[0], c[3] + SPAN * c[1], h_r, h_i)
            return (z_r + s[0], z_i + s[1], d_r + s[2], d_i + s[3])
        zero = jnp.zeros((PACK, 128), jnp.float32)
        lax.fori_loop(0, blocks, step, (zero,) * 4)

        def outputs(g, _):
            rws = group_rows(pw_ref, q * 4 + g)
            e_r, e_i = power_table(rws, False)
            w_r, w_i = jnp.concatenate([rws[16]] * 16, 0), jnp.concatenate([rws[17]] * 16, 0)
            r_r, r_i = cmul(e_r, e_i, w_r, w_i)
            krow = kernel_rows(r_r, rws[16])
            table = jnp.concatenate([r_r, -r_i], 1).astype(jnp.bfloat16)
            c = jnp.concatenate([
                jnp.concatenate([carry_ref[q, a, pl.ds(g * mb + m, blocks, stride=PACK), :] for m in range(mb)], 0)
                for a in range(2)], 1)
            across = nt(spread(c, rows).astype(jnp.bfloat16), table)
            for k in range(4):
                x = xs[pl.ds(4 * g + k, rows, stride=PACK), :].astype(jnp.bfloat16)
                y = across[k * rows:(k + 1) * rows] + nn(x, toeplitz(krow[k:k + 1]))
                ys[pl.ds(4 * g + k, rows, stride=PACK), :] = y
            return 0
        lax.fori_loop(0, 4, outputs, 0)

        skip = skip_ref[pl.ds(pl.multiple_of(q * PACK, PACK), PACK), :]
        def finish(j, _):
            for m in range(mb):
                for k in range(h):
                    r = m * blocks + j * h + k
                    v = ys[block_rows(r), :] + skip * xs[block_rows(r), :]
                    a, d = gelu_pair(v)
                    act_ref[j, pl.ds(q * PACK, PACK), pl.ds((m * h + k) * 128, 128)] = a.astype(jnp.bfloat16)
                    slope_ref[q, r] = d
            return 0
        lax.fori_loop(0, nj, finish, 0)
        return 0
    lax.fori_loop(0, chans // PACK, one_pack, 0)


def backward_kernel(dims, modes_ref, skip_ref, keep_ref, u_ref, ga_ref, slope_ref, carry_ref, gn_ref, zw_ref, pw_ref, xs, gy, gx, sc):
    nj, chans, mb, h = dims
    blocks = nj * h
    rows = mb * blocks
    mode_prelude(modes_ref, pw_ref)

    def one_pack(q, _):
        unpack(u_ref, q, xs, nj, mb, h, blocks)
        def start(j, _):
            for m in range(mb):
                for k in range(h):
                    r = m * blocks + j * h + k
                    x = ga_ref[j, pl.ds(q * PACK, PACK), pl.ds((m * h + k) * 128, 128)]
                    gy[block_rows(r), :] = x.astype(jnp.float32) * slope_ref[q, r]
            return 0
        lax.fori_loop(0, nj, start, 0)

        def states(g, _):
            gg = q * 4 + g
            rws = group_rows(pw_ref, gg)
            e_r, e_i = power_table(rws, False)
            ahead = (1 + lax.broadcasted_iota(jnp.int32, (SPAN, 128), 0)).astype(jnp.float32)
            table = jnp.concatenate([e_r, e_i, ahead * e_r, ahead * e_i], 1).astype(jnp.bfloat16)
            ups = [gy[pl.ds(4 * g + k, rows, stride=PACK), :].astype(jnp.bfloat16) for k in range(4)]
            lag = []
            for k in range(4):
                x = xs[pl.ds(4 * g + k, rows, stride=PACK), :].astype(jnp.bfloat16)
                lag.append(lag_sums(tn(x, ups[k])))
            lag = jnp.concatenate(lag + [jnp.zeros((4, 128), jnp.float32)], 0)
            own8 = lax.broadcasted_iota(jnp.int32, (8, 128), 1) // 32 == lax.broadcasted_iota(jnp.int32, (8, 128), 0)
            lag0 = jnp.sum(jnp.where(own8, jnp.broadcast_to(lag[:, 0:1], (8, 128)), 0.0), axis=0, keepdims=True)
            lane = lax.broadcasted_iota(jnp.int32, (8, 128), 1)
            later = jnp.where(lane == 127, 0.0, pltpu.roll(lag, 127, 1))
            top = later.astype(jnp.bfloat16)
            low = (later - top.astype(jnp.float32)).astype(jnp.bfloat16)
            stack = jnp.concatenate(ups + [top, low], 0)
            s = nn(stack, table)
            near = s[4 * rows:4 * rows + 8] + s[4 * rows + 8:]
            own = jnp.concatenate([own8] * 4, 1)
            near = jnp.sum(jnp.where(own, near, 0.0), axis=0, keepdims=True)
            zw_ref[0, pl.ds(gg, 1), :] = near[:, 0:128] + lag0
            for a in range(1, 4):
                zw_ref[a, pl.ds(gg, 1), :] = near[:, a * 128:(a + 1) * 128]
            zw_ref[4, pl.ds(gg, 1), :] = lag0
            s = fold(s[:4 * rows], rows)
            for a in range(4):
                for m in range(mb):
                    sc[a, pl.ds(g * mb + m, blocks, stride=PACK), :] = s[m * blocks:(m + 1) * blocks, a * 128:(a + 1) * 128]
            return 0
        lax.fori_loop(0, 4, states, 0)

        def rows_of(k):
            parts = [jnp.broadcast_to(pw_ref[k, pl.ds(q * 4 + g, 1), :], (mb, 128)) for g in range(4)]
            parts.append(jnp.zeros((PACK - 4 * mb, 128), jnp.float32))
            return jnp.concatenate(parts, 0)
        h_r, h_i = rows_of(14), rows_of(15)

        def step(n, c):
            i = blocks - 1 - n
            at = pl.ds(pl.multiple_of(i * PACK, PACK), PACK)
            a_r, a_i, z_r, z_i, w_r, w_i = c
            q_ = [sc[a, at, :] for a in range(4)]
            f = [carry_ref[q, a, at, :] for a in range(4)]
            d = cmul(q_[0], q_[1], f[0], f[1])
            e1 = cmul(q_[2], q_[3], f[0], f[1])
            e2 = cmul(q_[0], q_[1], f[2], f[3])
            sc[0, at, :] = a_r
            sc[1, at, :] = a_i
            keep = keep_ref[i]
            n_r, n_i = cmul(a_r, a_i, h_r, h_i)
            return ((n_r + q_[0]) * keep, (n_i + q_[1]) * keep, z_r + d[0], z_i + d[1], w_r + e1[0] + e2[0], w_i + e1[1] + e2[1])
        zero = jnp.zeros((PACK, 128), jnp.float32)
        out = lax.fori_loop(0, blocks, step, (zero,) * 6)
        for a in range(4):
            for g in range(4):
                add = jnp.sum(out[2 + a][g * mb:(g + 1) * mb], axis=0, keepdims=True)
                zw_ref[a, pl.ds(q * 4 + g, 1), :] += add

        def outputs(g, _):
            rws = group_rows(pw_ref, q * 4 + g)
            e_r, e_i = power_table(rws, False)
            w_r, w_i = jnp.concatenate([rws[16]] * 16, 0), jnp.concatenate([rws[17]] * 16, 0)
            r_r = e_r * w_r - e_i * w_i
            krow = kernel_rows(r_r, rws[16])
            p_r, p_i = power_table(rws, True)
            r_r, r_i = cmul(p_r, p_i, w_r, w_i)
            table = jnp.concatenate([r_r, -r_i], 1).astype(jnp.bfloat16)
            c = jnp.concatenate([
                jnp.concatenate([sc[a, pl.ds(g * mb + m, blocks, stride=PACK), :] for m in range(mb)], 0)
                for a in range(2)], 1)
            across = nt(spread(c, rows).astype(jnp.bfloat16), table)
            for k in range(4):
                up = gy[pl.ds(4 * g + k, rows, stride=PACK), :].astype(jnp.bfloat16)
                y = across[k * rows:(k + 1) * rows] + nt(up, toeplitz(krow[k:k + 1]))
                gx[pl.ds(4 * g + k, rows, stride=PACK), :] = y
            return 0
        lax.fori_loop(0, 4, outputs, 0)

        skip = skip_ref[pl.ds(pl.multiple_of(q * PACK, PACK), PACK), :]
        def finish(j, _):
            for m in range(mb):
                for k in range(h):
                    r = m * blocks + j * h + k
                    v = gx[block_rows(r), :] + skip * gy[block_rows(r), :]
                    gn_ref[j, pl.ds(q * PACK, PACK), pl.ds((m * h + k) * 128, 128)] = v.astype(jnp.bfloat16)
            return 0
        lax.fori_loop(0, nj, finish, 0)
        return 0
    lax.fori_loop(0, chans // PACK, one_pack, 0)


def ssm_forward(modes, skip, keep, u, mb):
    nj, chans, width = u.shape
    h = width // mb // 128
    blocks = nj * h
    rows = mb * blocks
    packs = chans // PACK
    f32 = jnp.float32
    return pl.pallas_call(
        functools.partial(forward_kernel, (nj, chans, mb, h)),
        out_shape=(
            jax.ShapeDtypeStruct(u.shape, jnp.bfloat16),
            jax.ShapeDtypeStruct((packs, rows, PACK, 128), f32),
            jax.ShapeDtypeStruct((packs, 4, blocks * PACK, 128), f32),
        ),
        scratch_shapes=[
            pltpu.VMEM((18, modes.shape[1], 128), f32),
            pltpu.VMEM((rows * PACK, 128), f32),
            pltpu.VMEM((rows * PACK, 128), f32),
            pltpu.VMEM((4, blocks * PACK, 128), f32),
        ],
        compiler_params=pltpu.CompilerParams(vmem_limit_bytes=50 << 20),
        name="ssm_forward",
    )(modes, skip, keep, u)


def ssm_backward(modes, skip, keep, u, ga, slope, carry, mb):
    nj, chans, width = u.shape
    h = width // mb // 128
    blocks = nj * h
    rows = mb * blocks
    f32 = jnp.float32
    return pl.pallas_call(
        functools.partial(backward_kernel, (nj, chans, mb, h)),
        out_shape=(
            jax.ShapeDtypeStruct(u.shape, jnp.bfloat16),
            jax.ShapeDtypeStruct((5, modes.shape[1], 128), f32),
        ),
        scratch_shapes=[
            pltpu.VMEM((18, modes.shape[1], 128), f32),
            pltpu.VMEM((rows * PACK, 128), f32),
            pltpu.VMEM((rows * PACK, 128), f32),
            pltpu.VMEM((rows * PACK, 128), f32),
            pltpu.VMEM((4, blocks * PACK, 128), f32),
        ],
        compiler_params=pltpu.CompilerParams(vmem_limit_bytes=50 << 20),
        name="ssm_backward",
    )(modes, skip, keep, u, ga, slope, carry)


def mode_gradients(modes, zw):
    m = mode_rows(*modes)
    z_r, z_i, v_r, v_i = zw[0], zw[1], zw[2], zw[3]
    rr, ri = modes[3], modes[4]
    g_rr = 2.0 * (z_r * m["q_r"] - z_i * m["q_i"])
    g_ri = -2.0 * (z_r * m["q_i"] + z_i * m["q_r"])
    k_r, k_i = cmul(rr, ri, m["a_r"] / m["mod"], -m["a_i"] / m["mod"])
    s_r, s_i = cmul(k_r, k_i, m["l_r"], m["l_i"])
    h1 = cmul(z_r, z_i, s_r, s_i)
    h2 = cmul(m["w_r"], m["w_i"], v_r, v_i)
    h_r, h_i = h1[0] + h2[0], h1[1] + h2[1]
    zc = cmul(z_r, z_i, m["w_r"], m["w_i"])
    za = cmul(zc[0], zc[1], m["a_r"] / m["mod"], -m["a_i"] / m["mod"])
    j_r, j_i = h_r * m["dt"] - za[0], h_i * m["dt"] - za[1]
    g_ls = 2.0 * (h_r * m["t_r"] - h_i * m["t_i"])
    return g_ls, 2.0 * m["a_r"] * j_r, -2.0 * j_i, g_rr, g_ri


def keep_rows(lengths, blocks, mb):
    at = jnp.arange(blocks, dtype=jnp.int32)[:, None] * SPAN
    keep = (at % lengths[None, :] != 0).astype(jnp.float32)
    rows = jnp.concatenate([keep] * 4 + [jnp.zeros((blocks, PACK - 4 * mb), jnp.float32)], 1)
    return jnp.broadcast_to(rows[:, :, None], (blocks, PACK, 128))


def mode_stack(log_step, ld, fr, rr, ri):
    nh = ld.shape[1]
    ls = jnp.broadcast_to(log_step[:, None], ld.shape)
    return jnp.stack([x.reshape(-1, 128) for x in (ls, ld, fr, rr, ri)])


def layer_norm(values, gain_vector):
    average = jnp.mean(values, axis=-1, keepdims=True)
    centred = values - average
    spread = jnp.mean(centred * centred, axis=-1, keepdims=True)
    return centred * lax.rsqrt(spread + 1e-05) * gain_vector


def exact_gelu(values):
    return jax.nn.gelu(values, approximate=False)


def gate_mix(project):
    features = project.shape[1] // 2
    return project[:, :features] * jax.nn.sigmoid(project[:, features:])


def on_device(
    tokens, cotangent, lengths, norm_gain, log_step, log_decay, frequency, readout_real, readout_imaginary,
    skip_gain, out_weight, out_bias, ffn_gain, in_weight, in_bias, back_weight,
):
    both = ("dp", "chan")
    mb, rows, feats = tokens.shape
    chans = log_step.shape[0]
    nj = feats // chans
    groups = log_decay.shape[1]
    f32, bf16 = jnp.float32, jnp.bfloat16
    shards = lax.axis_size("dp") * nj

    small = jnp.concatenate([out_bias, norm_gain, ffn_gain, in_bias])
    small = lax.all_gather(small, both, axis=0, tiled=False).astype(f32)
    cuts = (out_bias.shape[0], norm_gain.shape[0], ffn_gain.shape[0], in_bias.shape[0])
    at = [sum(cuts[:k]) for k in range(5)]
    b_out, gain_one, gain_two, b_in = (small[:, at[k]:at[k + 1]].reshape(-1) for k in range(4))
    four = jnp.stack([log_decay, frequency, readout_real, readout_imaginary])
    four = lax.all_gather(four, "dp", axis=2, tiled=True)
    w_out = lax.all_gather(out_weight, both, axis=0, tiled=True)
    w_in = lax.all_gather(in_weight, both, axis=0, tiled=True)
    w_back = lax.all_gather(back_weight, both, axis=0, tiled=True)

    rows_all = tokens.reshape(mb * rows, feats).astype(f32)
    normed, norm_pull = jax.vjp(layer_norm, rows_all, gain_one)
    sent = normed.astype(bf16).T.reshape(nj, chans, mb * rows)
    u = lax.all_to_all(sent, "chan", split_axis=0, concat_axis=0, tiled=True)

    modes = mode_stack(log_step, *four)
    skip = jnp.broadcast_to(skip_gain[:, None], (chans, 128))
    keep = keep_rows(lengths[:, 0], nj * rows // SPAN, mb)
    act, slope, carry = ssm_forward(modes, skip, keep, u, mb)
    act_t = lax.all_to_all(act, "chan", split_axis=0, concat_axis=0, tiled=True).reshape(feats, mb * rows)

    project = tn(act_t, w_out) + b_out
    gated, gate_pull = jax.vjp(gate_mix, project)
    middle = rows_all + gated
    second_float, second_pull = jax.vjp(layer_norm, middle, gain_two)
    second = second_float.astype(bf16)
    before = nn(second, w_in) + b_in
    hidden_float, hidden_pull = jax.vjp(exact_gelu, before)
    hidden = hidden_float.astype(bf16)
    block_out = (middle + nn(hidden, w_back)).astype(bf16)
    upstream = cotangent.reshape(mb * rows, feats)
    grad_back = tn(hidden, upstream)
    grad_before = hidden_pull(nt(upstream, w_back))[0].astype(bf16)
    grad_in = tn(second, grad_before)
    grad_in_bias = jnp.sum(grad_before.astype(f32), axis=0)
    grad_middle, grad_gain_two = second_pull(nt(grad_before, w_in))
    grad_middle = grad_middle + upstream.astype(f32)
    grad_project = gate_pull(grad_middle)[0].astype(bf16)
    grad_out = nn(act_t, grad_project)
    grad_out_bias = jnp.sum(grad_project.astype(f32), axis=0)
    grad_act = nt(w_out, grad_project).astype(bf16).reshape(nj, chans, mb * rows)
    ga = lax.all_to_all(grad_act, "chan", split_axis=0, concat_axis=0, tiled=True)

    gn, zw = ssm_backward(modes, skip, keep, u, ga, slope, carry, mb)
    row_grad = lax.all_to_all(gn, "chan", split_axis=0, concat_axis=0, tiled=True).reshape(feats, mb * rows).T
    grad_rows, grad_gain_one = norm_pull(row_grad.astype(f32))
    grad_tokens = (grad_rows + grad_middle).astype(bf16)

    zw = lax.psum(zw, "dp")
    g_ls, g_ld, g_fr, g_rr, g_ri = (x.reshape(chans, -1) for x in mode_gradients(modes, zw))
    first = lax.axis_index("dp") * groups
    own = [lax.dynamic_slice_in_dim(x, first, groups, 1) for x in (g_ld, g_fr, g_rr, g_ri)]
    g_skip = zw[4].reshape(chans, -1)[:, 0]

    def scatter(x):
        return lax.psum_scatter(x, both, scatter_dimension=0, tiled=True)
    vec = jnp.concatenate([x.reshape(shards, -1) for x in (grad_out_bias, grad_gain_one, grad_gain_two, grad_in_bias)], 1)
    vec = scatter(vec)[0]
    g_bo, g_g1, g_g2, g_bi = (vec[at[k]:at[k + 1]] for k in range(4))
    return (
        block_out.reshape(tokens.shape), grad_tokens.reshape(tokens.shape), g_g1, jnp.sum(g_ls, 1), *own, g_skip,
        scatter(grad_out.astype(bf16)).astype(f32), g_bo, g_g2, scatter(grad_in.astype(bf16)).astype(f32), g_bi, scatter(grad_back.astype(bf16)).astype(f32),
    )


def solution(mesh):
    both = ("dp", "chan")
    rows, row, vec, chan, mode = P(None, both, None), P(both, None), P(both), P("chan"), P("chan", "dp")
    return jax.shard_map(
        on_device, mesh=mesh,
        in_specs=(rows, rows, P(None, "dp"), vec, chan, mode, mode, mode, mode, chan, row, vec, vec, row, vec, row),
        out_specs=(rows, rows, vec, chan, mode, mode, mode, mode, chan, row, vec, vec, row, vec, row),
        check_vma=False,
    )
```

```python
import functools
import jax
import jax.numpy as jnp
from jax import lax
from jax.experimental import pallas as pl
from jax.experimental.pallas import tpu as pltpu
from jax.sharding import PartitionSpec as P

SPAN = 128
PACK = 16
HI = lax.Precision.HIGHEST


def cmul(ar, ai, br, bi):
    return ar * br - ai * bi, ar * bi + ai * br


def mode_rows(ls, ld, fr, rr, ri):
    dt = jnp.exp(ls)
    a_r = -jnp.exp(ld)
    a_i = fr
    t_r, t_i = dt * a_r, dt * a_i
    mag = jnp.exp(t_r)
    l_r, l_i = mag * jnp.cos(t_i), mag * jnp.sin(t_i)
    mod = a_r * a_r + a_i * a_i
    u_r = l_r - 1.0
    q_r = (u_r * a_r + l_i * a_i) / mod
    q_i = (l_i * a_r - u_r * a_i) / mod
    w_r, w_i = cmul(rr, ri, q_r, q_i)
    return dict(dt=dt, a_r=a_r, a_i=a_i, t_r=t_r, t_i=t_i, l_r=l_r, l_i=l_i, mod=mod,
                q_r=q_r, q_i=q_i, w_r=w_r, w_i=w_i)


def mode_prelude(modes_ref, pw_ref):
    m = mode_rows(modes_ref[0], modes_ref[1], modes_ref[2], modes_ref[3], modes_ref[4])
    r, i = m["l_r"], m["l_i"]
    for k in range(8):
        pw_ref[2 * k] = r
        pw_ref[2 * k + 1] = i
        r, i = cmul(r, i, r, i)
    pw_ref[16] = 2.0 * m["w_r"]
    pw_ref[17] = 2.0 * m["w_i"]


def group_rows(pw_ref, g):
    rows = [pw_ref[k, pl.ds(g, 1), :] for k in range(18)]
    return [jnp.broadcast_to(x, (8, 128)) for x in rows]


def power_table(rows, reverse):
    sub = lax.broadcasted_iota(jnp.int32, (8, 128), 0)
    if reverse:
        sub = 7 - sub
        r, i = jnp.ones((8, 128), jnp.float32), jnp.zeros((8, 128), jnp.float32)
    else:
        r, i = rows[0], rows[1]
    for k in range(3):
        bit = ((sub >> k) & 1) == 1
        fr = jnp.where(bit, rows[2 * k], 1.0)
        fi = jnp.where(bit, rows[2 * k + 1], 0.0)
        r, i = cmul(r, i, fr, fi)
    parts = [(r, i)]
    for k in range(3, 7):
        more = [cmul(a, b, rows[2 * k], rows[2 * k + 1]) for a, b in parts]
        parts = more + parts if reverse else parts + more
    return (jnp.concatenate([p[0] for p in parts], 0), jnp.concatenate([p[1] for p in parts], 0))


def nt(a, b, **kw):
    return lax.dot_general(a, b, (((1,), (1,)), ((), ())), preferred_element_type=jnp.float32, **kw)


def tn(a, b, **kw):
    return lax.dot_general(a, b, (((0,), (0,)), ((), ())), preferred_element_type=jnp.float32, **kw)


def nn(a, b, **kw):
    return jnp.dot(a, b, preferred_element_type=jnp.float32, **kw)


def kernel_rows(rd_r, w_r):
    t = lax.broadcasted_iota(jnp.int32, (SPAN, 128), 0)
    src = jnp.where(t == SPAN - 1, jnp.concatenate([w_r] * 16, 0), rd_r)
    pick = (lax.broadcasted_iota(jnp.int32, (8, 128), 1) // 32
            == lax.broadcasted_iota(jnp.int32, (8, 128), 0)).astype(jnp.float32)
    return pltpu.roll(nt(pick, src, precision=HI), 1, 1)


def toeplitz(row):
    base = pltpu.roll(jnp.broadcast_to(row, (8, 128)), 0, 1, stride=1, stride_axis=0)
    parts = [base] + [pltpu.roll(base, 8 * v, 1) for v in range(1, 16)]
    whole = jnp.concatenate(parts, 0)
    s = lax.broadcasted_iota(jnp.int32, (SPAN, 128), 0)
    t = lax.broadcasted_iota(jnp.int32, (SPAN, 128), 1)
    return jnp.where(t >= s, whole, 0.0).astype(jnp.bfloat16)


def lag_sums(g):
    s = lax.broadcasted_iota(jnp.int32, (SPAN, 128), 0)
    t = lax.broadcasted_iota(jnp.int32, (SPAN, 128), 1)
    g = jnp.where(t >= s, g, 0.0)
    n = SPAN
    while n > 8:
        n //= 2
        g = g[:n] + pltpu.roll(g[n:], 128 - n, 1)
    for n in (4, 2, 1):
        g = g + pltpu.roll(pltpu.roll(g, 128 - n, 1), 8 - n, 0)
    return g[0:1]


def lane_owner(rows):
    return lax.broadcasted_iota(jnp.int32, (rows, 128), 1) // 32


def fold(stack, rows):
    width = stack.shape[1]
    own = (lax.broadcasted_iota(jnp.int32, (rows, width), 1) // 32) & 3
    out = stack[:rows]
    for k in range(1, 4):
        out = jnp.where(own == k, stack[k * rows:(k + 1) * rows], out)
    return out


def spread(packed, rows):
    width = packed.shape[1]
    own = (lax.broadcasted_iota(jnp.int32, (rows, width), 1) // 32) & 3
    return jnp.concatenate([jnp.where(own == k, packed, 0.0) for k in range(4)], 0)


def gelu_pair(v):
    half = 0.5 * (1.0 + lax.erf(v * 0.7071067811865476))
    return v * half, half + v * jnp.exp(-0.5 * v * v) * 0.3989422804014327


def block_rows(r):
    return pl.ds(pl.multiple_of(r * PACK, PACK), PACK)


def unpack(src_ref, q, xs, nj, mb, h, blocks, scale=None):
    def body(j, _):
        for m in range(mb):
            for k in range(h):
                x = src_ref[j, block_rows(q), pl.ds((m * h + k) * 128, 128)]
                xs[block_rows(m * blocks + j * h + k), :] = x.astype(jnp.float32)
        return 0
    lax.fori_loop(0, nj, body, 0)


def rows_of(pw_ref, k, q, mb):
    parts = [jnp.broadcast_to(pw_ref[k, pl.ds(q * 4 + g, 1), :], (mb, 128)) for g in range(4)]
    parts.append(jnp.zeros((PACK - 4 * mb, 128), jnp.float32))
    return jnp.concatenate(parts, 0)


def forward_pack(dims, q, skip_ref, keep_ref, u_ref, act_ref, slope_ref, carry_ref, pw_ref, xs, ys, sc):
    nj, chans, mb, h = dims
    blocks = nj * h
    rows = mb * blocks
    unpack(u_ref, q, xs, nj, mb, h, blocks)

    def states(g, _):
        rws = group_rows(pw_ref, q * 4 + g)
        p_r, p_i = power_table(rws, True)
        back = (SPAN - 1 - lax.broadcasted_iota(jnp.int32, (SPAN, 128), 0)).astype(jnp.float32)
        table = jnp.concatenate([p_r, p_i, back * p_r, back * p_i], 1).astype(jnp.bfloat16)
        x = jnp.concatenate([xs[pl.ds(4 * g + k, rows, stride=PACK), :] for k in range(4)], 0).astype(jnp.bfloat16)
        s = fold(nn(x, table), rows)
        for a in range(4):
            for m in range(mb):
                sc[a, pl.ds(g * mb + m, blocks, stride=PACK), :] = s[m * blocks:(m + 1) * blocks, a * 128:(a + 1) * 128]
        return 0
    lax.fori_loop(0, 4, states, 0, unroll=2)
    h_r, h_i = rows_of(pw_ref, 14, q, mb), rows_of(pw_ref, 15, q, mb)

    def step(i, c):
        at = block_rows(i)
        keep = keep_ref[i]
        c = [x * keep for x in c]
        s = [sc[a, at, :] for a in range(4)]
        for a in range(4):
            carry_ref[q, a, at, :] = c[a]
        z_r, z_i = cmul(c[0], c[1], h_r, h_i)
        d_r, d_i = cmul(c[2] + SPAN * c[0], c[3] + SPAN * c[1], h_r, h_i)
        return (z_r + s[0], z_i + s[1], d_r + s[2], d_i + s[3])
    zero = jnp.zeros((PACK, 128), jnp.float32)
    lax.fori_loop(0, blocks, step, (zero,) * 4)

    def outputs(g, _):
        rws = group_rows(pw_ref, q * 4 + g)
        e_r, e_i = power_table(rws, False)
        w_r, w_i = jnp.concatenate([rws[16]] * 16, 0), jnp.concatenate([rws[17]] * 16, 0)
        r_r, r_i = cmul(e_r, e_i, w_r, w_i)
        krow = kernel_rows(r_r, rws[16])
        table = jnp.concatenate([r_r, -r_i], 1).astype(jnp.bfloat16)
        c = jnp.concatenate([
            jnp.concatenate([carry_ref[q, a, pl.ds(g * mb + m, blocks, stride=PACK), :] for m in range(mb)], 0)
            for a in range(2)], 1)
        across = nt(spread(c, rows).astype(jnp.bfloat16), table)
        for k in range(4):
            x = xs[pl.ds(4 * g + k, rows, stride=PACK), :].astype(jnp.bfloat16)
            y = across[k * rows:(k + 1) * rows] + nn(x, toeplitz(krow[k:k + 1]))
            ys[pl.ds(4 * g + k, rows, stride=PACK), :] = y
        return 0
    lax.fori_loop(0, 4, outputs, 0, unroll=2)
    skip = skip_ref[block_rows(q), :]

    def finish(j, _):
        for m in range(mb):
            for k in range(h):
                r = m * blocks + j * h + k
                v = ys[block_rows(r), :] + skip * xs[block_rows(r), :]
                a, d = gelu_pair(v)
                act_ref[j, block_rows(q), pl.ds((m * h + k) * 128, 128)] = a.astype(jnp.bfloat16)
                slope_ref[q, block_rows(r), :] = d
        return 0
    lax.fori_loop(0, nj, finish, 0)


def backward_pack(dims, q, skip_ref, keep_ref, u_ref, ga_ref, slope_ref, carry_ref, gn_ref, zw_ref, pw_ref, xs, gy, gx, sc):
    nj, chans, mb, h = dims
    blocks = nj * h
    rows = mb * blocks
    unpack(u_ref, q, xs, nj, mb, h, blocks)
    def start(j, _):
        for m in range(mb):
            for k in range(h):
                r = m * blocks + j * h + k
                x = ga_ref[j, block_rows(q), pl.ds((m * h + k) * 128, 128)]
                gy[block_rows(r), :] = x.astype(jnp.float32) * slope_ref[q, block_rows(r), :]
        return 0
    lax.fori_loop(0, nj, start, 0)

    def states(g, _):
        gg = q * 4 + g
        rws = group_rows(pw_ref, gg)
        e_r, e_i = power_table(rws, False)
        ahead = (1 + lax.broadcasted_iota(jnp.int32, (SPAN, 128), 0)).astype(jnp.float32)
        table = jnp.concatenate([e_r, e_i, ahead * e_r, ahead * e_i], 1).astype(jnp.bfloat16)
        ups = [gy[pl.ds(4 * g + k, rows, stride=PACK), :].astype(jnp.bfloat16) for k in range(4)]
        lag = []
        for k in range(4):
            x = xs[pl.ds(4 * g + k, rows, stride=PACK), :].astype(jnp.bfloat16)
            lag.append(lag_sums(tn(x, ups[k])))
        lag = jnp.concatenate(lag + [jnp.zeros((4, 128), jnp.float32)], 0)
        own8 = lax.broadcasted_iota(jnp.int32, (8, 128), 1) // 32 == lax.broadcasted_iota(jnp.int32, (8, 128), 0)
        lag0 = jnp.sum(jnp.where(own8, jnp.broadcast_to(lag[:, 0:1], (8, 128)), 0.0), axis=0, keepdims=True)
        lane = lax.broadcasted_iota(jnp.int32, (8, 128), 1)
        later = jnp.where(lane == 127, 0.0, pltpu.roll(lag, 127, 1))
        top = later.astype(jnp.bfloat16)
        low = (later - top.astype(jnp.float32)).astype(jnp.bfloat16)
        stack = jnp.concatenate(ups + [top, low], 0)
        s = nn(stack, table)
        near = s[4 * rows:4 * rows + 8] + s[4 * rows + 8:]
        own = jnp.concatenate([own8] * 4, 1)
        near = jnp.sum(jnp.where(own, near, 0.0), axis=0, keepdims=True)
        zw_ref[0, pl.ds(gg, 1), :] = near[:, 0:128] + lag0
        for a in range(1, 4):
            zw_ref[a, pl.ds(gg, 1), :] = near[:, a * 128:(a + 1) * 128]
        zw_ref[4, pl.ds(gg, 1), :] = lag0
        s = fold(s[:4 * rows], rows)
        for a in range(4):
            for m in range(mb):
                sc[a, pl.ds(g * mb + m, blocks, stride=PACK), :] = s[m * blocks:(m + 1) * blocks, a * 128:(a + 1) * 128]
        return 0
    lax.fori_loop(0, 4, states, 0, unroll=2)

    h_r, h_i = rows_of(pw_ref, 14, q, mb), rows_of(pw_ref, 15, q, mb)

    def step(n, c):
        i = blocks - 1 - n
        at = block_rows(i)
        a_r, a_i, z_r, z_i, w_r, w_i = c
        q_ = [sc[a, at, :] for a in range(4)]
        f = [carry_ref[q, a, at, :] for a in range(4)]
        d = cmul(q_[0], q_[1], f[0], f[1])
        e1 = cmul(q_[2], q_[3], f[0], f[1])
        e2 = cmul(q_[0], q_[1], f[2], f[3])
        sc[0, at, :] = a_r
        sc[1, at, :] = a_i
        keep = keep_ref[i]
        n_r, n_i = cmul(a_r, a_i, h_r, h_i)
        return ((n_r + q_[0]) * keep, (n_i + q_[1]) * keep, z_r + d[0], z_i + d[1], w_r + e1[0] + e2[0], w_i + e1[1] + e2[1])
    zero = jnp.zeros((PACK, 128), jnp.float32)
    out = lax.fori_loop(0, blocks, step, (zero,) * 6)
    for a in range(4):
        for g in range(4):
            add = jnp.sum(out[2 + a][g * mb:(g + 1) * mb], axis=0, keepdims=True)
            zw_ref[a, pl.ds(q * 4 + g, 1), :] += add

    def outputs(g, _):
        rws = group_rows(pw_ref, q * 4 + g)
        e_r, e_i = power_table(rws, False)
        w_r, w_i = jnp.concatenate([rws[16]] * 16, 0), jnp.concatenate([rws[17]] * 16, 0)
        r_r = e_r * w_r - e_i * w_i
        krow = kernel_rows(r_r, rws[16])
        p_r, p_i = power_table(rws, True)
        r_r, r_i = cmul(p_r, p_i, w_r, w_i)
        table = jnp.concatenate([r_r, -r_i], 1).astype(jnp.bfloat16)
        c = jnp.concatenate([
            jnp.concatenate([sc[a, pl.ds(g * mb + m, blocks, stride=PACK), :] for m in range(mb)], 0)
            for a in range(2)], 1)
        across = nt(spread(c, rows).astype(jnp.bfloat16), table)
        for k in range(4):
            up = gy[pl.ds(4 * g + k, rows, stride=PACK), :].astype(jnp.bfloat16)
            y = across[k * rows:(k + 1) * rows] + nt(up, toeplitz(krow[k:k + 1]))
            gx[pl.ds(4 * g + k, rows, stride=PACK), :] = y
        return 0
    lax.fori_loop(0, 4, outputs, 0, unroll=2)

    skip = skip_ref[block_rows(q), :]
    def finish(j, _):
        for m in range(mb):
            for k in range(h):
                r = m * blocks + j * h + k
                v = gx[block_rows(r), :] + skip * gy[block_rows(r), :]
                gn_ref[j, block_rows(q), pl.ds((m * h + k) * 128, 128)] = v.astype(jnp.bfloat16)
        return 0
    lax.fori_loop(0, nj, finish, 0)


def backward_kernel(dims, modes_ref, skip_ref, keep_ref, u_ref, ga_ref, slope_ref, carry_ref, gn_ref, zw_ref, pw_ref, xs, gy, gx, sc):
    mode_prelude(modes_ref, pw_ref)
    sc[...] = jnp.zeros(sc.shape, jnp.float32)

    def one(q, _):
        backward_pack(dims, q, skip_ref, keep_ref, u_ref, ga_ref, slope_ref, carry_ref, gn_ref, zw_ref, pw_ref, xs, gy, gx, sc)
        return 0
    lax.fori_loop(0, dims[1] // PACK, one, 0)


def ssm_backward(modes, skip, keep, u, ga, slope, carry, mb):
    nj, chans, width = u.shape
    h = width // mb // 128
    blocks = nj * h
    rows = mb * blocks
    f32 = jnp.float32
    return pl.pallas_call(
        functools.partial(backward_kernel, (nj, chans, mb, h)),
        out_shape=(
            jax.ShapeDtypeStruct(u.shape, jnp.bfloat16),
            jax.ShapeDtypeStruct((5, modes.shape[1], 128), f32),
        ),
        scratch_shapes=[
            pltpu.VMEM((18, modes.shape[1], 128), f32),
            pltpu.VMEM((rows * PACK, 128), f32),
            pltpu.VMEM((rows * PACK, 128), f32),
            pltpu.VMEM((rows * PACK, 128), f32),
            pltpu.VMEM((4, blocks * PACK, 128), f32),
        ],
        compiler_params=pltpu.CompilerParams(vmem_limit_bytes=50 << 20),
        name="ssm_backward",
    )(modes, skip, keep, u, ga, slope, carry)


def mode_gradients(modes, zw):
    m = mode_rows(*modes)
    z_r, z_i, v_r, v_i = zw[0], zw[1], zw[2], zw[3]
    rr, ri = modes[3], modes[4]
    g_rr = 2.0 * (z_r * m["q_r"] - z_i * m["q_i"])
    g_ri = -2.0 * (z_r * m["q_i"] + z_i * m["q_r"])
    k_r, k_i = cmul(rr, ri, m["a_r"] / m["mod"], -m["a_i"] / m["mod"])
    s_r, s_i = cmul(k_r, k_i, m["l_r"], m["l_i"])
    h1 = cmul(z_r, z_i, s_r, s_i)
    h2 = cmul(m["w_r"], m["w_i"], v_r, v_i)
    h_r, h_i = h1[0] + h2[0], h1[1] + h2[1]
    zc = cmul(z_r, z_i, m["w_r"], m["w_i"])
    za = cmul(zc[0], zc[1], m["a_r"] / m["mod"], -m["a_i"] / m["mod"])
    j_r, j_i = h_r * m["dt"] - za[0], h_i * m["dt"] - za[1]
    g_ls = 2.0 * (h_r * m["t_r"] - h_i * m["t_i"])
    return g_ls, 2.0 * m["a_r"] * j_r, -2.0 * j_i, g_rr, g_ri


def keep_rows(lengths, blocks, mb):
    at = jnp.arange(blocks, dtype=jnp.int32)[:, None] * SPAN
    keep = (at % lengths[None, :] != 0).astype(jnp.float32)
    rows = jnp.concatenate([keep] * 4 + [jnp.zeros((blocks, PACK - 4 * mb), jnp.float32)], 1)
    return jnp.broadcast_to(rows[:, :, None], (blocks, PACK, 128))


def mode_stack(log_step, ld, fr, rr, ri):
    nh = ld.shape[1]
    ls = jnp.broadcast_to(log_step[:, None], ld.shape)
    return jnp.stack([x.reshape(-1, 128) for x in (ls, ld, fr, rr, ri)])


MESH = pl.DeviceIdType.MESH


def layer_stats(v):
    average = jnp.mean(v, axis=-1, keepdims=True)
    centred = v - average
    spread = jnp.mean(centred * centred, axis=-1, keepdims=True)
    return centred, lax.rsqrt(spread + 1e-05)


def peers(count, me):
    return [lax.rem(me + k, count) for k in range(1, count)]


def greet(n_dp, n_chan, d, c):
    barrier = pltpu.get_barrier_semaphore()
    for p in peers(n_dp, d):
        pl.semaphore_signal(barrier, inc=1, device_id=(p, c), device_id_type=MESH)
    for p in peers(n_chan, c):
        pl.semaphore_signal(barrier, inc=1, device_id=(d, p), device_id_type=MESH)
    pl.semaphore_wait(barrier, n_dp + n_chan - 2)


def send(src, dst, send_sem, recv_sem, to):
    copy = pltpu.make_async_remote_copy(src_ref=src, dst_ref=dst, send_sem=send_sem, recv_sem=recv_sem, device_id=to, device_id_type=MESH)
    copy.start()
    return copy


def exchange_start(box, sems, axis_count, me, to):
    for p in peers(axis_count, me):
        send(box.at[me], box.at[me], sems.at[0], sems.at[1], to(p))


def exchange_wait(box, sems, axis_count, to):
    if axis_count > 1:
        whole = box.at[pl.ds(0, axis_count - 1)]
        pltpu.make_async_remote_copy(src_ref=whole, dst_ref=whole, send_sem=sems.at[0], recv_sem=sems.at[1], device_id=to, device_id_type=MESH).wait()


class Spread:
    def __init__(self, wholes, sems, d, c):
        self.wholes, self.sems = wholes, sems
        self.d, self.c = d, c
        self.a, self.b, self.core = c // 4, lax.rem(c // 2, 2), lax.rem(c, 2)
        self.used = 0
        self.open = []

    def chan(self, a, b, core):
        return (self.d, a * 4 + b * 2 + core)

    def put(self, ref, to):
        n = self.used
        self.used += 1
        return send(ref, ref, self.sems.at[0, n], self.sems.at[1, n], to)

    def halves(self, w):
        cols = w.shape[-1] // 2
        return pl.ds(0, cols), pl.ds(cols, cols)

    def along_dp(self, owns, n_dp):
        a, b, core, d = self.a, self.b, self.core, self.d
        self.step = []
        for own, w in zip(owns, self.wholes):
            w[d, a, b, core] = own[...]
        for w in self.wholes:
            for p in peers(n_dp, d):
                self.step.append(self.put(w.at[d, a, b, core], (p, self.c)))

    def arrived(self):
        for copy in self.step:
            copy.wait_recv()
        self.open += self.step
        self.step = []

    def first_hop(self):
        a, b, core = self.a, self.b, self.core
        self.arrived()
        for w in self.wholes:
            low, high = self.halves(w)
            self.step.append(self.put(w.at[:, a, b, core, :, low], self.chan(a, 1 - b, core)))
            self.step.append(self.put(w.at[:, a, b, core, :, high], self.chan(1 - a, b, core)))
        self.side = [self.put(w.at[:, a, b, core], self.chan(a, b, 1 - core)) for w in self.wholes]

    def second_hop(self):
        a, b, core = self.a, self.b, self.core
        self.arrived()
        for w in self.wholes:
            low, high = self.halves(w)
            self.step.append(self.put(w.at[:, a, :, core, :, low], self.chan(1 - a, b, core)))
            self.step.append(self.put(w.at[:, :, b, core, :, high], self.chan(a, 1 - b, core)))
        other = self.chan(a, b, 1 - core)
        for w in self.wholes:
            low, high = self.halves(w)
            self.side.append(self.put(w.at[:, a, 1 - b, core, :, low], other))
            self.side.append(self.put(w.at[:, 1 - a, b, core, :, high], other))

    def last_hop(self):
        a, b, core = self.a, self.b, self.core
        self.arrived()
        other = self.chan(a, b, 1 - core)
        for w in self.wholes:
            low, high = self.halves(w)
            self.side.append(self.put(w.at[:, 1 - a, :, core, :, low], other))
            self.side.append(self.put(w.at[:, :, 1 - b, core, :, high], other))

    def finish(self):
        for copy in self.side:
            copy.wait_recv()
        for copy in self.open + self.side:
            copy.wait_send()


def entry_kernel(dims, n_dp, direct, *refs):
    (nj, chans, mb, h) = dims
    refs = list(refs)
    tokens_ref, vec_ref, modes_ref, skip_ref, keep_ref = refs[:5]
    del refs[:5]
    owns = [refs.pop(0) for _ in range(3)] if direct else []
    u_ref, act_ref, slope_ref, carry_ref, vec_out, modes_out = refs[:6]
    del refs[:6]
    wholes = [refs.pop(0) for _ in range(3)] if direct else []
    snd, out, vec_dp, vec_chan, modes_dp, pw, xs, ys, sc = refs[:9]
    del refs[:9]
    vec_sems, modes_sems, in_sems, out_sems = refs[:4]
    del refs[:4]
    d, c = lax.axis_index("dp"), lax.axis_index("chan")
    packs = chans // PACK
    width = tokens_ref.shape[0]
    t = width // mb
    feats = nj * chans

    greet(n_dp, nj, d, c)
    vec_dp[d] = vec_ref[...]
    modes_dp[d] = modes_ref[pl.ds(1, 4)]
    exchange_start(vec_dp, vec_sems.at[0], n_dp, d, lambda p: (p, c))
    exchange_start(modes_dp, modes_sems, n_dp, d, lambda p: (p, c))
    if direct:
        spread = Spread(wholes, refs[0], d, c)
        spread.along_dp(owns, n_dp)
    exchange_wait(vec_dp, vec_sems.at[0], n_dp, (d, c))
    vec_chan[c] = sum(vec_dp[k] for k in range(n_dp))
    exchange_start(vec_chan, vec_sems.at[1], nj, c, lambda p: (d, p))
    exchange_wait(modes_dp, modes_sems, n_dp, (d, c))
    modes_out[0] = modes_ref[0]
    modes_out[pl.ds(1, 4)] = sum(modes_dp[k] for k in range(n_dp))
    mode_prelude(modes_out, pw)
    sc[...] = jnp.zeros(sc.shape, jnp.float32)
    exchange_wait(vec_chan, vec_sems.at[1], nj, (d, c))
    vec_out[...] = sum(vec_chan[k] for k in range(nj))
    gain = jnp.concatenate([vec_out[8 + k:9 + k, :] for k in range(feats // 128)], 1)

    def normalize(m, _):
        at = pl.ds(pl.multiple_of(m * t, t), t)
        centred, scale = layer_stats(tokens_ref[at, :].astype(jnp.float32))
        normed = (centred * scale * gain).T.astype(jnp.bfloat16)
        snd[:, :, at] = normed.reshape(nj, chans, t)
        return 0
    lax.fori_loop(0, mb, normalize, 0)

    def share(box, where, sems, q):
        for p in peers(nj, c):
            send(box.at[p, block_rows(q)], where.at[c, block_rows(q)], sems.at[0, q], sems.at[1, q], (d, p))
        where[c, block_rows(q), :] = box[c, block_rows(q), :]

    def settle(where, sems, q):
        whole = where.at[pl.ds(0, nj - 1), block_rows(q)]
        pltpu.make_async_remote_copy(src_ref=whole, dst_ref=whole, send_sem=sems.at[0, q], recv_sem=sems.at[1, q], device_id=(d, c), device_id_type=MESH).wait()

    for q in range(packs):
        share(snd, u_ref, in_sems, q)
    for q in range(packs):
        settle(u_ref, in_sems, q)
        forward_pack(dims, q, skip_ref, keep_ref, u_ref, out, slope_ref, carry_ref, pw, xs, ys, sc)
        share(out, act_ref, out_sems, q)
        if direct:
            if q == 0:
                spread.first_hop()
            if q == 1:
                spread.second_hop()
            if q == 3:
                spread.last_hop()
    for q in range(packs):
        settle(act_ref, out_sems, q)
    if direct:
        spread.finish()


def entry(tokens, vec, modes, skip, keep, weights, mb, n_dp, nj):
    width, feats = tokens.shape
    chans = feats // nj
    t = width // mb
    h = t // SPAN
    blocks = nj * h
    rows = mb * blocks
    packs = chans // PACK
    groups = modes.shape[1]
    f32, bf16 = jnp.float32, jnp.bfloat16
    direct = nj == 8 and packs == 4 and all(w.shape[0] % 16 == 0 for w in weights)
    owns = list(weights) if direct else []
    shapes = [
        jax.ShapeDtypeStruct((nj, chans, width), bf16),
        jax.ShapeDtypeStruct((nj, chans, width), bf16),
        jax.ShapeDtypeStruct((packs, rows * PACK, 128), f32),
        jax.ShapeDtypeStruct((packs, 4, blocks * PACK, 128), f32),
        jax.ShapeDtypeStruct(vec.shape, f32),
        jax.ShapeDtypeStruct(modes.shape, f32),
    ] + [jax.ShapeDtypeStruct((n_dp, 2, 2, 2) + w.shape, bf16) for w in owns]
    dma = pltpu.SemaphoreType.DMA
    scratch = [
        pltpu.VMEM((nj, chans, width), bf16),
        pltpu.VMEM((nj, chans, width), bf16),
        pltpu.VMEM((n_dp,) + vec.shape, f32),
        pltpu.VMEM((nj,) + vec.shape, f32),
        pltpu.VMEM((n_dp, 4) + modes.shape[1:], f32),
        pltpu.VMEM((18, groups, 128), f32),
        pltpu.VMEM((rows * PACK, 128), f32),
        pltpu.VMEM((rows * PACK, 128), f32),
        pltpu.VMEM((4, blocks * PACK, 128), f32),
        dma((2, 2)), dma((2,)), dma((2, packs)), dma((2, packs)),
    ]
    if direct:
        scratch.append(dma((2, 48)))
    vmem = pl.BlockSpec(memory_space=pltpu.VMEM)
    outs = pl.pallas_call(
        functools.partial(entry_kernel, (nj, chans, mb, h), n_dp, direct),
        out_shape=shapes,
        in_specs=[vmem] * (5 + len(owns)),
        out_specs=[vmem] * len(shapes),
        scratch_shapes=scratch,
        compiler_params=pltpu.CompilerParams(collective_id=0, has_side_effects=True, vmem_limit_bytes=56 << 20),
        name="entry",
    )(tokens, vec, modes, skip, keep, *owns)
    u, act, slope, carry, vec, modes = outs[:6]
    wholes = [w.reshape(-1, w.shape[-1]) for w in outs[6:]]
    if not direct:
        wholes = [lax.all_gather(w, ("dp", "chan"), axis=0, tiled=True) for w in weights]
    return u, act.reshape(feats, width), slope, carry, vec, modes, wholes


def layer_norm(values, gain_vector):
    average = jnp.mean(values, axis=-1, keepdims=True)
    centred = values - average
    spread = jnp.mean(centred * centred, axis=-1, keepdims=True)
    return centred * lax.rsqrt(spread + 1e-05) * gain_vector


def exact_gelu(values):
    return jax.nn.gelu(values, approximate=False)


def gate_mix(project):
    features = project.shape[1] // 2
    return project[:, :features] * jax.nn.sigmoid(project[:, features:])


def on_device(
    tokens, cotangent, lengths, norm_gain, log_step, log_decay, frequency, readout_real, readout_imaginary,
    skip_gain, out_weight, out_bias, ffn_gain, in_weight, in_bias, back_weight,
):
    both = ("dp", "chan")
    mb, rows, feats = tokens.shape
    chans = log_step.shape[0]
    nj = feats // chans
    groups = log_decay.shape[1]
    f32, bf16 = jnp.float32, jnp.bfloat16
    shards = lax.axis_size("dp") * nj

    place = lax.axis_index("dp") * nj + lax.axis_index("chan")
    def placed(x):
        return lax.dynamic_update_slice(jnp.zeros((shards * x.shape[0],), f32), x.astype(f32), (place * x.shape[0],))
    vec = jnp.concatenate([placed(x) for x in (out_bias, norm_gain, ffn_gain, in_bias)]).reshape(-1, 128)
    cuts = (out_bias.shape[0], norm_gain.shape[0], ffn_gain.shape[0], in_bias.shape[0])
    at = [sum(cuts[:k]) for k in range(5)]
    n_dp = lax.axis_size("dp")
    mine = jnp.arange(groups * n_dp) // groups == lax.axis_index("dp")
    modes = [jnp.broadcast_to(log_step[:, None], (chans, groups * n_dp))]
    modes += [jnp.where(mine, jnp.tile(x, (1, n_dp)), 0.0) for x in (log_decay, frequency, readout_real, readout_imaginary)]
    modes = jnp.stack([x.reshape(-1, 128) for x in modes])
    skip = jnp.broadcast_to(skip_gain[:, None], (chans, 128))
    keep = keep_rows(lengths[:, 0], nj * rows // SPAN, mb)
    u, act_t, slope, carry, vec, modes, (w_out, w_in, w_back) = entry(
        tokens.reshape(mb * rows, feats), vec, modes, skip, keep, (out_weight, in_weight, back_weight), mb, n_dp, nj)
    vec = vec.reshape(-1)
    b_out, gain_one, gain_two, b_in = (vec[shards * at[k]:shards * at[k + 1]] for k in range(4))

    rows_all = tokens.reshape(mb * rows, feats).astype(f32)
    normed, norm_pull = jax.vjp(layer_norm, rows_all, gain_one)
    project = tn(act_t, w_out) + b_out
    gated, gate_pull = jax.vjp(gate_mix, project)
    middle = rows_all + gated
    second_float, second_pull = jax.vjp(layer_norm, middle, gain_two)
    second = second_float.astype(bf16)
    before = nn(second, w_in) + b_in
    hidden_float, hidden_pull = jax.vjp(exact_gelu, before)
    hidden = hidden_float.astype(bf16)
    block_out = (middle + nn(hidden, w_back)).astype(bf16)
    upstream = cotangent.reshape(mb * rows, feats)
    grad_back = tn(hidden, upstream)
    grad_before = hidden_pull(nt(upstream, w_back))[0].astype(bf16)
    grad_in = tn(second, grad_before)
    grad_in_bias = jnp.sum(grad_before.astype(f32), axis=0)
    grad_middle, grad_gain_two = second_pull(nt(grad_before, w_in))
    grad_middle = grad_middle + upstream.astype(f32)
    grad_project = gate_pull(grad_middle)[0].astype(bf16)
    grad_out = nn(act_t, grad_project)
    grad_out_bias = jnp.sum(grad_project.astype(f32), axis=0)
    grad_act = nt(w_out, grad_project).astype(bf16).reshape(nj, chans, mb * rows)
    ga = lax.all_to_all(grad_act, "chan", split_axis=0, concat_axis=0, tiled=True)

    gn, zw = ssm_backward(modes, skip, keep, u, ga, slope, carry, mb)
    row_grad = lax.all_to_all(gn, "chan", split_axis=0, concat_axis=0, tiled=True).reshape(feats, mb * rows).T
    grad_rows, grad_gain_one = norm_pull(row_grad.astype(f32))
    grad_tokens = (grad_rows + grad_middle).astype(bf16)

    zw = lax.psum(zw, "dp")
    g_ls, g_ld, g_fr, g_rr, g_ri = (x.reshape(chans, -1) for x in mode_gradients(modes, zw))
    first = lax.axis_index("dp") * groups
    own = [lax.dynamic_slice_in_dim(x, first, groups, 1) for x in (g_ld, g_fr, g_rr, g_ri)]
    g_skip = zw[4].reshape(chans, -1)[:, 0]

    def scatter(x):
        return lax.psum_scatter(x, both, scatter_dimension=0, tiled=True)
    vec = jnp.concatenate([x.reshape(shards, -1) for x in (grad_out_bias, grad_gain_one, grad_gain_two, grad_in_bias)], 1)
    vec = scatter(vec)[0]
    g_bo, g_g1, g_g2, g_bi = (vec[at[k]:at[k + 1]] for k in range(4))
    return (
        block_out.reshape(tokens.shape), grad_tokens.reshape(tokens.shape), g_g1, jnp.sum(g_ls, 1), *own, g_skip,
        scatter(grad_out.astype(bf16)).astype(f32), g_bo, g_g2, scatter(grad_in.astype(bf16)).astype(f32), g_bi, scatter(grad_back.astype(bf16)).astype(f32),
    )


def solution(mesh):
    both = ("dp", "chan")
    rows, row, vec, chan, mode = P(None, both, None), P(both, None), P(both), P("chan"), P("chan", "dp")
    return jax.shard_map(
        on_device, mesh=mesh,
        in_specs=(rows, rows, P(None, "dp"), vec, chan, mode, mode, mode, mode, chan, row, vec, vec, row, vec, row),
        out_specs=(rows, rows, vec, chan, mode, mode, mode, mode, chan, row, vec, vec, row, vec, row),
        check_vma=False,
    )
```

```python
import functools
import jax
import jax.numpy as jnp
from jax import lax
from jax.experimental import pallas as pl
from jax.experimental.pallas import tpu as pltpu
from jax.sharding import PartitionSpec as P

SPAN = 128
PACK = 16
HI = lax.Precision.HIGHEST


def cmul(ar, ai, br, bi):
    return ar * br - ai * bi, ar * bi + ai * br


def mode_rows(ls, ld, fr, rr, ri):
    dt = jnp.exp(ls)
    a_r = -jnp.exp(ld)
    a_i = fr
    t_r, t_i = dt * a_r, dt * a_i
    mag = jnp.exp(t_r)
    l_r, l_i = mag * jnp.cos(t_i), mag * jnp.sin(t_i)
    mod = a_r * a_r + a_i * a_i
    u_r = l_r - 1.0
    q_r = (u_r * a_r + l_i * a_i) / mod
    q_i = (l_i * a_r - u_r * a_i) / mod
    w_r, w_i = cmul(rr, ri, q_r, q_i)
    return dict(dt=dt, a_r=a_r, a_i=a_i, t_r=t_r, t_i=t_i, l_r=l_r, l_i=l_i, mod=mod,
                q_r=q_r, q_i=q_i, w_r=w_r, w_i=w_i)


def mode_prelude(modes_ref, pw_ref):
    m = mode_rows(modes_ref[0], modes_ref[1], modes_ref[2], modes_ref[3], modes_ref[4])
    r, i = m["l_r"], m["l_i"]
    for k in range(8):
        pw_ref[2 * k] = r
        pw_ref[2 * k + 1] = i
        r, i = cmul(r, i, r, i)
    pw_ref[16] = 2.0 * m["w_r"]
    pw_ref[17] = 2.0 * m["w_i"]


def group_rows(pw_ref, g):
    rows = [pw_ref[k, pl.ds(g, 1), :] for k in range(18)]
    return [jnp.broadcast_to(x, (8, 128)) for x in rows]


def power_table(rows, reverse):
    sub = lax.broadcasted_iota(jnp.int32, (8, 128), 0)
    if reverse:
        sub = 7 - sub
        r, i = jnp.ones((8, 128), jnp.float32), jnp.zeros((8, 128), jnp.float32)
    else:
        r, i = rows[0], rows[1]
    for k in range(3):
        bit = ((sub >> k) & 1) == 1
        fr = jnp.where(bit, rows[2 * k], 1.0)
        fi = jnp.where(bit, rows[2 * k + 1], 0.0)
        r, i = cmul(r, i, fr, fi)
    parts = [(r, i)]
    for k in range(3, 7):
        more = [cmul(a, b, rows[2 * k], rows[2 * k + 1]) for a, b in parts]
        parts = more + parts if reverse else parts + more
    return (jnp.concatenate([p[0] for p in parts], 0), jnp.concatenate([p[1] for p in parts], 0))


def nt(a, b, **kw):
    return lax.dot_general(a, b, (((1,), (1,)), ((), ())), preferred_element_type=jnp.float32, **kw)


def tn(a, b, **kw):
    return lax.dot_general(a, b, (((0,), (0,)), ((), ())), preferred_element_type=jnp.float32, **kw)


def nn(a, b, **kw):
    return jnp.dot(a, b, preferred_element_type=jnp.float32, **kw)


def kernel_rows(rd_r, w_r):
    t = lax.broadcasted_iota(jnp.int32, (SPAN, 128), 0)
    src = jnp.where(t == SPAN - 1, jnp.concatenate([w_r] * 16, 0), rd_r)
    pick = (lax.broadcasted_iota(jnp.int32, (8, 128), 1) // 32
            == lax.broadcasted_iota(jnp.int32, (8, 128), 0)).astype(jnp.float32)
    return pltpu.roll(nt(pick, src, precision=HI), 1, 1)


def toeplitz(row):
    base = pltpu.roll(jnp.broadcast_to(row, (8, 128)), 0, 1, stride=1, stride_axis=0)
    parts = [base] + [pltpu.roll(base, 8 * v, 1) for v in range(1, 16)]
    whole = jnp.concatenate(parts, 0)
    s = lax.broadcasted_iota(jnp.int32, (SPAN, 128), 0)
    t = lax.broadcasted_iota(jnp.int32, (SPAN, 128), 1)
    return jnp.where(t >= s, whole, 0.0).astype(jnp.bfloat16)


def lag_sums(g):
    s = lax.broadcasted_iota(jnp.int32, (SPAN, 128), 0)
    t = lax.broadcasted_iota(jnp.int32, (SPAN, 128), 1)
    g = jnp.where(t >= s, g, 0.0)
    n = SPAN
    while n > 8:
        n //= 2
        g = g[:n] + pltpu.roll(g[n:], 128 - n, 1)
    for n in (4, 2, 1):
        g = g + pltpu.roll(pltpu.roll(g, 128 - n, 1), 8 - n, 0)
    return g[0:1]


def lane_owner(rows):
    return lax.broadcasted_iota(jnp.int32, (rows, 128), 1) // 32


def fold(stack, rows):
    width = stack.shape[1]
    own = (lax.broadcasted_iota(jnp.int32, (rows, width), 1) // 32) & 3
    out = stack[:rows]
    for k in range(1, 4):
        out = jnp.where(own == k, stack[k * rows:(k + 1) * rows], out)
    return out


def spread(packed, rows):
    width = packed.shape[1]
    own = (lax.broadcasted_iota(jnp.int32, (rows, width), 1) // 32) & 3
    return jnp.concatenate([jnp.where(own == k, packed, 0.0) for k in range(4)], 0)


def gelu_pair(v):
    half = 0.5 * (1.0 + lax.erf(v * 0.7071067811865476))
    return v * half, half + v * jnp.exp(-0.5 * v * v) * 0.3989422804014327


def block_rows(r):
    return pl.ds(pl.multiple_of(r * PACK, PACK), PACK)


def unpack(src_ref, q, xs, nj, mb, h, blocks, scale=None):
    def body(j, _):
        for m in range(mb):
            for k in range(h):
                x = src_ref[j, block_rows(q), pl.ds((m * h + k) * 128, 128)]
                xs[block_rows(m * blocks + j * h + k), :] = x.astype(jnp.float32)
        return 0
    lax.fori_loop(0, nj, body, 0)


def rows_of(pw_ref, k, q, mb):
    parts = [jnp.broadcast_to(pw_ref[k, pl.ds(q * 4 + g, 1), :], (mb, 128)) for g in range(4)]
    parts.append(jnp.zeros((PACK - 4 * mb, 128), jnp.float32))
    return jnp.concatenate(parts, 0)


def forward_pack(dims, q, skip_ref, keep_ref, u_ref, act_ref, slope_ref, carry_ref, pw_ref, xs, ys, sc):
    nj, chans, mb, h = dims
    blocks = nj * h
    rows = mb * blocks
    unpack(u_ref, q, xs, nj, mb, h, blocks)

    def states(g, _):
        rws = group_rows(pw_ref, q * 4 + g)
        p_r, p_i = power_table(rws, True)
        back = (SPAN - 1 - lax.broadcasted_iota(jnp.int32, (SPAN, 128), 0)).astype(jnp.float32)
        table = jnp.concatenate([p_r, p_i, back * p_r, back * p_i], 1).astype(jnp.bfloat16)
        x = jnp.concatenate([xs[pl.ds(4 * g + k, rows, stride=PACK), :] for k in range(4)], 0).astype(jnp.bfloat16)
        s = fold(nn(x, table), rows)
        for a in range(4):
            for m in range(mb):
                sc[a, pl.ds(g * mb + m, blocks, stride=PACK), :] = s[m * blocks:(m + 1) * blocks, a * 128:(a + 1) * 128]
        return 0
    lax.fori_loop(0, 4, states, 0, unroll=2)
    h_r, h_i = rows_of(pw_ref, 14, q, mb), rows_of(pw_ref, 15, q, mb)

    def step(i, c):
        at = block_rows(i)
        keep = keep_ref[i]
        c = [x * keep for x in c]
        s = [sc[a, at, :] for a in range(4)]
        for a in range(4):
            carry_ref[q, a, at, :] = c[a]
        z_r, z_i = cmul(c[0], c[1], h_r, h_i)
        d_r, d_i = cmul(c[2] + SPAN * c[0], c[3] + SPAN * c[1], h_r, h_i)
        return (z_r + s[0], z_i + s[1], d_r + s[2], d_i + s[3])
    zero = jnp.zeros((PACK, 128), jnp.float32)
    lax.fori_loop(0, blocks, step, (zero,) * 4)

    def outputs(g, _):
        rws = group_rows(pw_ref, q * 4 + g)
        e_r, e_i = power_table(rws, False)
        w_r, w_i = jnp.concatenate([rws[16]] * 16, 0), jnp.concatenate([rws[17]] * 16, 0)
        r_r, r_i = cmul(e_r, e_i, w_r, w_i)
        krow = kernel_rows(r_r, rws[16])
        table = jnp.concatenate([r_r, -r_i], 1).astype(jnp.bfloat16)
        c = jnp.concatenate([
            jnp.concatenate([carry_ref[q, a, pl.ds(g * mb + m, blocks, stride=PACK), :] for m in range(mb)], 0)
            for a in range(2)], 1)
        across = nt(spread(c, rows).astype(jnp.bfloat16), table)
        for k in range(4):
            x = xs[pl.ds(4 * g + k, rows, stride=PACK), :].astype(jnp.bfloat16)
            y = across[k * rows:(k + 1) * rows] + nn(x, toeplitz(krow[k:k + 1]))
            ys[pl.ds(4 * g + k, rows, stride=PACK), :] = y
        return 0
    lax.fori_loop(0, 4, outputs, 0, unroll=2)
    skip = skip_ref[block_rows(q), :]

    def finish(j, _):
        for m in range(mb):
            for k in range(h):
                r = m * blocks + j * h + k
                v = ys[block_rows(r), :] + skip * xs[block_rows(r), :]
                a, d = gelu_pair(v)
                act_ref[j, block_rows(q), pl.ds((m * h + k) * 128, 128)] = a.astype(jnp.bfloat16)
                slope_ref[q, block_rows(r), :] = d
        return 0
    lax.fori_loop(0, nj, finish, 0)


def backward_pack(dims, q, skip_ref, keep_ref, u_ref, ga_ref, slope_ref, carry_ref, gn_ref, zw_ref, pw_ref, xs, gy, gx, sc):
    nj, chans, mb, h = dims
    blocks = nj * h
    rows = mb * blocks
    unpack(u_ref, q, xs, nj, mb, h, blocks)
    def start(j, _):
        for m in range(mb):
            for k in range(h):
                r = m * blocks + j * h + k
                x = ga_ref[j, block_rows(q), pl.ds((m * h + k) * 128, 128)]
                gy[block_rows(r), :] = x.astype(jnp.float32) * slope_ref[q, block_rows(r), :]
        return 0
    lax.fori_loop(0, nj, start, 0)

    def states(g, _):
        gg = q * 4 + g
        rws = group_rows(pw_ref, gg)
        e_r, e_i = power_table(rws, False)
        ahead = (1 + lax.broadcasted_iota(jnp.int32, (SPAN, 128), 0)).astype(jnp.float32)
        table = jnp.concatenate([e_r, e_i, ahead * e_r, ahead * e_i], 1).astype(jnp.bfloat16)
        ups = [gy[pl.ds(4 * g + k, rows, stride=PACK), :].astype(jnp.bfloat16) for k in range(4)]
        lag = []
        for k in range(4):
            x = xs[pl.ds(4 * g + k, rows, stride=PACK), :].astype(jnp.bfloat16)
            lag.append(lag_sums(tn(x, ups[k])))
        lag = jnp.concatenate(lag + [jnp.zeros((4, 128), jnp.float32)], 0)
        own8 = lax.broadcasted_iota(jnp.int32, (8, 128), 1) // 32 == lax.broadcasted_iota(jnp.int32, (8, 128), 0)
        lag0 = jnp.sum(jnp.where(own8, jnp.broadcast_to(lag[:, 0:1], (8, 128)), 0.0), axis=0, keepdims=True)
        lane = lax.broadcasted_iota(jnp.int32, (8, 128), 1)
        later = jnp.where(lane == 127, 0.0, pltpu.roll(lag, 127, 1))
        top = later.astype(jnp.bfloat16)
        low = (later - top.astype(jnp.float32)).astype(jnp.bfloat16)
        stack = jnp.concatenate(ups + [top, low], 0)
        s = nn(stack, table)
        near = s[4 * rows:4 * rows + 8] + s[4 * rows + 8:]
        own = jnp.concatenate([own8] * 4, 1)
        near = jnp.sum(jnp.where(own, near, 0.0), axis=0, keepdims=True)
        zw_ref[0, pl.ds(gg, 1), :] = near[:, 0:128] + lag0
        for a in range(1, 4):
            zw_ref[a, pl.ds(gg, 1), :] = near[:, a * 128:(a + 1) * 128]
        zw_ref[4, pl.ds(gg, 1), :] = lag0
        s = fold(s[:4 * rows], rows)
        for a in range(4):
            for m in range(mb):
                sc[a, pl.ds(g * mb + m, blocks, stride=PACK), :] = s[m * blocks:(m + 1) * blocks, a * 128:(a + 1) * 128]
        return 0
    lax.fori_loop(0, 4, states, 0, unroll=2)

    h_r, h_i = rows_of(pw_ref, 14, q, mb), rows_of(pw_ref, 15, q, mb)

    def step(n, c):
        i = blocks - 1 - n
        at = block_rows(i)
        a_r, a_i, z_r, z_i, w_r, w_i = c
        q_ = [sc[a, at, :] for a in range(4)]
        f = [carry_ref[q, a, at, :] for a in range(4)]
        d = cmul(q_[0], q_[1], f[0], f[1])
        e1 = cmul(q_[2], q_[3], f[0], f[1])
        e2 = cmul(q_[0], q_[1], f[2], f[3])
        sc[0, at, :] = a_r
        sc[1, at, :] = a_i
        keep = keep_ref[i]
        n_r, n_i = cmul(a_r, a_i, h_r, h_i)
        return ((n_r + q_[0]) * keep, (n_i + q_[1]) * keep, z_r + d[0], z_i + d[1], w_r + e1[0] + e2[0], w_i + e1[1] + e2[1])
    zero = jnp.zeros((PACK, 128), jnp.float32)
    out = lax.fori_loop(0, blocks, step, (zero,) * 6)
    for a in range(4):
        for g in range(4):
            add = jnp.sum(out[2 + a][g * mb:(g + 1) * mb], axis=0, keepdims=True)
            zw_ref[a, pl.ds(q * 4 + g, 1), :] += add

    def outputs(g, _):
        rws = group_rows(pw_ref, q * 4 + g)
        e_r, e_i = power_table(rws, False)
        w_r, w_i = jnp.concatenate([rws[16]] * 16, 0), jnp.concatenate([rws[17]] * 16, 0)
        r_r = e_r * w_r - e_i * w_i
        krow = kernel_rows(r_r, rws[16])
        p_r, p_i = power_table(rws, True)
        r_r, r_i = cmul(p_r, p_i, w_r, w_i)
        table = jnp.concatenate([r_r, -r_i], 1).astype(jnp.bfloat16)
        c = jnp.concatenate([
            jnp.concatenate([sc[a, pl.ds(g * mb + m, blocks, stride=PACK), :] for m in range(mb)], 0)
            for a in range(2)], 1)
        across = nt(spread(c, rows).astype(jnp.bfloat16), table)
        for k in range(4):
            up = gy[pl.ds(4 * g + k, rows, stride=PACK), :].astype(jnp.bfloat16)
            y = across[k * rows:(k + 1) * rows] + nt(up, toeplitz(krow[k:k + 1]))
            gx[pl.ds(4 * g + k, rows, stride=PACK), :] = y
        return 0
    lax.fori_loop(0, 4, outputs, 0, unroll=2)

    skip = skip_ref[block_rows(q), :]
    def finish(j, _):
        for m in range(mb):
            for k in range(h):
                r = m * blocks + j * h + k
                v = gx[block_rows(r), :] + skip * gy[block_rows(r), :]
                gn_ref[j, block_rows(q), pl.ds((m * h + k) * 128, 128)] = v.astype(jnp.bfloat16)
        return 0
    lax.fori_loop(0, nj, finish, 0)


def mode_gradients(modes, zw):
    m = mode_rows(*modes)
    z_r, z_i, v_r, v_i = zw[0], zw[1], zw[2], zw[3]
    rr, ri = modes[3], modes[4]
    g_rr = 2.0 * (z_r * m["q_r"] - z_i * m["q_i"])
    g_ri = -2.0 * (z_r * m["q_i"] + z_i * m["q_r"])
    k_r, k_i = cmul(rr, ri, m["a_r"] / m["mod"], -m["a_i"] / m["mod"])
    s_r, s_i = cmul(k_r, k_i, m["l_r"], m["l_i"])
    h1 = cmul(z_r, z_i, s_r, s_i)
    h2 = cmul(m["w_r"], m["w_i"], v_r, v_i)
    h_r, h_i = h1[0] + h2[0], h1[1] + h2[1]
    zc = cmul(z_r, z_i, m["w_r"], m["w_i"])
    za = cmul(zc[0], zc[1], m["a_r"] / m["mod"], -m["a_i"] / m["mod"])
    j_r, j_i = h_r * m["dt"] - za[0], h_i * m["dt"] - za[1]
    g_ls = 2.0 * (h_r * m["t_r"] - h_i * m["t_i"])
    return g_ls, 2.0 * m["a_r"] * j_r, -2.0 * j_i, g_rr, g_ri


def keep_rows(lengths, blocks, mb):
    at = jnp.arange(blocks, dtype=jnp.int32)[:, None] * SPAN
    keep = (at % lengths[None, :] != 0).astype(jnp.float32)
    rows = jnp.concatenate([keep] * 4 + [jnp.zeros((blocks, PACK - 4 * mb), jnp.float32)], 1)
    return jnp.broadcast_to(rows[:, :, None], (blocks, PACK, 128))


MESH = pl.DeviceIdType.MESH
F32, BF16 = jnp.float32, jnp.bfloat16


def layer_stats(v):
    average = jnp.mean(v, axis=-1, keepdims=True)
    centred = v - average
    spread = jnp.mean(centred * centred, axis=-1, keepdims=True)
    scale = lax.rsqrt(spread + 1e-05)
    return centred * scale, scale


def layer_back(q, n, scale):
    return scale * (q - jnp.mean(q, axis=-1, keepdims=True) - n * jnp.mean(q * n, axis=-1, keepdims=True))


def column_sum(x):
    return jnp.sum(x, axis=0, keepdims=True)


def peers(count, me):
    return [lax.rem(me + k, count) for k in range(1, count)]


def greet(n_dp, n_chan, d, c):
    barrier = pltpu.get_barrier_semaphore()
    for p in peers(n_dp, d):
        pl.semaphore_signal(barrier, inc=1, device_id=(p, c), device_id_type=MESH)
    for p in peers(n_chan, c):
        pl.semaphore_signal(barrier, inc=1, device_id=(d, p), device_id_type=MESH)
    pl.semaphore_wait(barrier, n_dp + n_chan - 2)


def send(src, dst, send_sem, recv_sem, to):
    copy = pltpu.make_async_remote_copy(src_ref=src, dst_ref=dst, send_sem=send_sem, recv_sem=recv_sem, device_id=to, device_id_type=MESH)
    copy.start()
    return copy


def exchange_start(box, sems, count, me, to):
    for p in peers(count, me):
        send(box.at[me], box.at[me], sems.at[0], sems.at[1], to(p))


def exchange_wait(box, sems, count, here):
    whole = box.at[pl.ds(0, count - 1)]
    pltpu.make_async_remote_copy(src_ref=whole, dst_ref=whole, send_sem=sems.at[0], recv_sem=sems.at[1], device_id=here, device_id_type=MESH).wait()


class Copies:
    def __init__(self, sems):
        self.sems = sems
        self.used = 0
        self.unsent = []

    def put(self, src, dst, to):
        n = self.used
        self.used += 1
        copy = send(src, dst, self.sems.at[0, n], self.sems.at[1, n], to)
        self.unsent.append(copy)
        return copy

    def finish(self):
        for copy in self.unsent:
            copy.wait_send()


def arrive(copies):
    for copy in copies:
        copy.wait_recv()


class Place:
    def __init__(self, d, c):
        self.d, self.c = d, c
        self.a, self.b, self.core = c // 4, lax.rem(c // 2, 2), lax.rem(c, 2)

    def at(self, a, b, core):
        return (self.d, a * 4 + b * 2 + core)

    @property
    def over_a(self):
        return self.at(1 - self.a, self.b, self.core)

    @property
    def over_b(self):
        return self.at(self.a, 1 - self.b, self.core)

    @property
    def twin(self):
        return self.at(self.a, self.b, 1 - self.core)


def halves(w):
    cols = w.shape[-1] // 2
    return pl.ds(0, cols), pl.ds(cols, cols)


class Gather:
    def __init__(self, wholes, copies, here):
        self.wholes, self.copies, self.here = wholes, copies, here
        self.side = []

    def along_dp(self, owns, n_dp):
        i = self.here
        for own, w in zip(owns, self.wholes):
            w[i.d, i.a, i.b, i.core] = own[...]
        self.step = []
        for w in self.wholes:
            ref = w.at[i.d, i.a, i.b, i.core]
            self.step += [self.copies.put(ref, ref, (p, i.c)) for p in peers(n_dp, i.d)]

    def same(self, ref, to):
        return self.copies.put(ref, ref, to)

    def first_hop(self):
        i = self.here
        arrive(self.step)
        self.step = []
        for w in self.wholes:
            low, high = halves(w)
            self.step.append(self.same(w.at[:, i.a, i.b, i.core, :, low], i.over_b))
            self.step.append(self.same(w.at[:, i.a, i.b, i.core, :, high], i.over_a))
        self.side += [self.same(w.at[:, i.a, i.b, i.core], i.twin) for w in self.wholes]

    def second_hop(self):
        i = self.here
        arrive(self.step)
        self.step = []
        for w in self.wholes:
            low, high = halves(w)
            self.step.append(self.same(w.at[:, i.a, :, i.core, :, low], i.over_a))
            self.step.append(self.same(w.at[:, :, i.b, i.core, :, high], i.over_b))
        for w in self.wholes:
            low, high = halves(w)
            self.side.append(self.same(w.at[:, i.a, 1 - i.b, i.core, :, low], i.twin))
            self.side.append(self.same(w.at[:, 1 - i.a, i.b, i.core, :, high], i.twin))

    def last_hop(self):
        i = self.here
        arrive(self.step)
        for w in self.wholes:
            low, high = halves(w)
            self.side.append(self.same(w.at[:, 1 - i.a, :, i.core, :, low], i.twin))
            self.side.append(self.same(w.at[:, :, 1 - i.b, i.core, :, high], i.twin))

    def finish(self):
        arrive(self.side)


class Scatter:
    def __init__(self, grads, boxes, copies, here):
        self.grads, self.copies, self.here = grads, copies, here
        self.twins, self.lows, self.highs, self.low2s, self.high2s, self.lasts = boxes
        self.first = []
        self.step = []

    def to_twin(self, k):
        i = self.here
        self.first.append(self.copies.put(self.grads[k].at[:, :, :, 1 - i.core], self.twins[k], i.twin))

    def add_twin(self):
        i = self.here
        arrive(self.first)
        for g, t in zip(self.grads, self.twins):
            def add(n, _):
                for a in range(2):
                    for b in range(2):
                        t[n, a, b] = (t[n, a, b].astype(F32) + g[n, a, b, i.core].astype(F32)).astype(BF16)
                return 0
            lax.fori_loop(0, t.shape[0], add, 0)
        for t, low_box, high_box in zip(self.twins, self.lows, self.highs):
            low, high = halves(t)
            self.step.append(self.copies.put(t.at[:, 1 - i.a, :, :, low], low_box, i.over_a))
            self.step.append(self.copies.put(t.at[:, :, 1 - i.b, :, high], high_box, i.over_b))

    def add_first(self):
        i = self.here
        arrive(self.step)
        self.step = []
        for t, low_box, high_box in zip(self.twins, self.lows, self.highs):
            low, high = halves(t)
            def add(n, _):
                for k in range(2):
                    low_box[n, k] = (low_box[n, k].astype(F32) + t[n, i.a, k, :, low].astype(F32)).astype(BF16)
                    high_box[n, k] = (high_box[n, k].astype(F32) + t[n, k, i.b, :, high].astype(F32)).astype(BF16)
                return 0
            lax.fori_loop(0, t.shape[0], add, 0)
        for low_box, high_box, low2, high2 in zip(self.lows, self.highs, self.low2s, self.high2s):
            self.step.append(self.copies.put(low_box.at[:, 1 - i.b], low2, i.over_b))
            self.step.append(self.copies.put(high_box.at[:, 1 - i.a], high2, i.over_a))

    def add_second(self, n_dp):
        i = self.here
        arrive(self.step)
        self.step = []
        for low_box, high_box, low2, high2, last in zip(self.lows, self.highs, self.low2s, self.high2s, self.lasts):
            low, high = halves(last)
            for n in range(n_dp):
                low2[n] = (low2[n].astype(F32) + low_box[n, i.b].astype(F32)).astype(BF16)
                high2[n] = (high2[n].astype(F32) + high_box[n, i.a].astype(F32)).astype(BF16)
            for p in peers(n_dp, i.d):
                self.step.append(self.copies.put(low2.at[p], last.at[i.d, :, low], (p, i.c)))
                self.step.append(self.copies.put(high2.at[p], last.at[i.d, :, high], (p, i.c)))

    def finish(self, outs, n_dp):
        i = self.here
        arrive(self.step)
        for low2, high2, last, out in zip(self.low2s, self.high2s, self.lasts, outs):
            low, high = halves(last)
            for cut, box in ((low, low2), (high, high2)):
                total = box[i.d].astype(F32)
                for p in peers(n_dp, i.d):
                    total = total + last[p, :, cut].astype(F32)
                out[:, cut] = total


def wide(vec_ref, first, count):
    return jnp.concatenate([vec_ref[first + k:first + k + 1, :] for k in range(count)], 1)


def add_wide(vec_ref, first, row):
    for k in range(row.shape[1] // 128):
        vec_ref[first + k:first + k + 1, :] += row[:, k * 128:(k + 1) * 128]


def flat(x):
    return x.reshape(-1, x.shape[-1])


def dense_rows(m, t, tokens, cot, act, wholes, vec, block_out, second, hidden, gb, gp, gm, snd, sums, nj, chans):
    w_out, w_in, w_back = wholes
    at = pl.ds(pl.multiple_of(m * t, t), t)
    feats = nj * chans
    ff = w_in.shape[-1]
    tile = ff // 4
    x = tokens[at, :].astype(F32)
    project = tn(act[:, :, at].reshape(feats, t), flat(w_out[...])) + wide(vec, 0, 2 * feats // 128)
    gate = jax.nn.sigmoid(project[:, feats:])
    gated = project[:, :feats] * gate
    middle = x + gated
    n, scale = layer_stats(middle)
    gain = wide(vec, 12, feats // 128)
    after = (n * gain).astype(BF16)
    second[at, :] = after
    up = cot[at, :]
    total = middle
    back = jnp.zeros((t, feats), F32)
    for f in range(4):
        cols = slice(f * tile, (f + 1) * tile)
        w = flat(w_in[:, :, :, :, :, cols])
        before = nn(after, w) + wide(vec, 16 + f * tile // 128, tile // 128)
        high, slope = gelu_pair(before)
        high = high.astype(BF16)
        hidden[at, cols] = high
        wb = flat(w_back[f])
        low = (slope * nt(up, wb)).astype(BF16)
        gb[at, cols] = low
        add_wide(sums, 16 + f * tile // 128, column_sum(low.astype(F32)))
        total = total + nn(high, wb)
        back = back + nt(low, w)
    block_out[at, :] = total.astype(BF16)
    add_wide(sums, 12, column_sum(back * n))
    grad = up.astype(F32) + layer_back(back * gain, n, scale)
    gm[at, :] = grad
    first = (grad * gate).astype(BF16)
    last = (grad * gated * (1.0 - gate)).astype(BF16)
    gp[at, :feats] = first
    gp[at, feats:] = last
    add_wide(sums, 0, column_sum(first.astype(F32)))
    add_wide(sums, feats // 128, column_sum(last.astype(F32)))
    both = jnp.concatenate([first, last], 1)
    snd[:, :, at] = nt(flat(w_out[...]), both).astype(BF16).reshape(nj, chans, t)


def weight_grads(act, gp, second, gb, hidden, cot, grads, nj, scatter):
    g_out, g_in, g_back = grads
    def shaped(x, g):
        return x.astype(BF16).reshape(g.shape[1:])
    def back(n, _):
        size = hidden.shape[1] // 4
        g_back[n] = shaped(tn(hidden[:, pl.ds(pl.multiple_of(n * size, size), size)], cot[...]), g_back)
        return 0
    lax.fori_loop(0, 4, back, 0)
    if scatter:
        scatter.to_twin(2)
    def inner(n, _):
        size = second.shape[1] // 4
        g_in[n] = shaped(tn(second[:, pl.ds(pl.multiple_of(n * size, size), size)], gb[...]), g_in)
        return 0
    lax.fori_loop(0, 4, inner, 0)
    if scatter:
        scatter.to_twin(1)
    def outer(n, _):
        g_out[n] = shaped(nn(flat(act[pl.ds(n * (nj // 4), nj // 4)]), gp[...]), g_out)
        return 0
    lax.fori_loop(0, 4, outer, 0)
    if scatter:
        scatter.to_twin(0)


def whole_kernel(dims, n_dp, direct, *refs):
    nj, chans, mb, h = dims
    refs = list(refs)
    def take(n):
        out = refs[:n]
        del refs[:n]
        return out
    tokens, cot, vec_own, modes_own, skip, keep = take(6)
    given = take(3)
    block_out, grad_tokens, mode_out, vec_out = take(4)
    results = take(3)
    u, snd, act, out, ga, gn, slope, carry = take(8)
    second, hidden, gb, gp, gm = take(5)
    vec_dp, vec_chan, modes_dp, zw_dp, modes, vec, sums = take(7)
    pw, xs, ys, gy, sc = take(5)
    box_sems, in_sems, out_sems, back_sems, gn_sems = take(5)
    d, c = lax.axis_index("dp"), lax.axis_index("chan")
    here = (d, c)
    packs = chans // PACK
    t = tokens.shape[0] // mb
    feats = nj * chans
    over_dp, over_chan = (lambda p: (p, c)), (lambda p: (d, p))
    if direct:
        wholes, grads = take(3), take(3)
        boxes = [take(3) for _ in range(6)]
        place = Place(d, c)
        gather_copies, scatter_copies = Copies(refs[0]), Copies(refs[1])
        gather = Gather(wholes, gather_copies, place)
        scatter = Scatter(grads, boxes, scatter_copies, place)
    else:
        wholes, grads, scatter = given, results, None

    greet(n_dp, nj, d, c)
    vec_dp[d] = vec_own[...]
    modes_dp[d] = modes_own[pl.ds(1, 4)]
    exchange_start(vec_dp, box_sems.at[0], n_dp, d, over_dp)
    exchange_start(modes_dp, box_sems.at[1], n_dp, d, over_dp)
    if direct:
        gather.along_dp(given, n_dp)
    sums[...] = jnp.zeros(sums.shape, F32)
    sc[...] = jnp.zeros(sc.shape, F32)
    exchange_wait(vec_dp, box_sems.at[0], n_dp, here)
    vec_chan[c] = sum(vec_dp[k] for k in range(n_dp))
    exchange_start(vec_chan, box_sems.at[2], nj, c, over_chan)
    exchange_wait(modes_dp, box_sems.at[1], n_dp, here)
    modes[0] = modes_own[0]
    modes[pl.ds(1, 4)] = sum(modes_dp[k] for k in range(n_dp))
    mode_prelude(modes, pw)
    exchange_wait(vec_chan, box_sems.at[2], nj, here)
    vec[...] = sum(vec_chan[k] for k in range(nj))
    gain = wide(vec, 8, feats // 128)

    def normalize(m, _):
        at = pl.ds(pl.multiple_of(m * t, t), t)
        n, _scale = layer_stats(tokens[at, :].astype(F32))
        snd[:, :, at] = (n * gain).T.astype(BF16).reshape(nj, chans, t)
        return 0
    lax.fori_loop(0, mb, normalize, 0)

    def share(box, where, sems, q):
        for p in peers(nj, c):
            send(box.at[p, block_rows(q)], where.at[c, block_rows(q)], sems.at[0, q], sems.at[1, q], (d, p))
        where[c, block_rows(q), :] = box[c, block_rows(q), :]

    def settle(where, sems, q):
        whole = where.at[pl.ds(0, nj - 1), block_rows(q)]
        pltpu.make_async_remote_copy(src_ref=whole, dst_ref=whole, send_sem=sems.at[0, q], recv_sem=sems.at[1, q], device_id=here, device_id_type=MESH).wait()

    for q in range(packs):
        share(snd, u, in_sems, q)
    for q in range(packs):
        settle(u, in_sems, q)
        forward_pack(dims, q, skip, keep, u, out, slope, carry, pw, xs, ys, sc)
        share(out, act, out_sems, q)
        if direct:
            if q == 0:
                gather.first_hop()
            if q == 1:
                gather.second_hop()
            if q == 3:
                gather.last_hop()
    for q in range(packs):
        settle(act, out_sems, q)
    if direct:
        gather.finish()

    for m in range(mb):
        dense_rows(m, t, tokens, cot, act, wholes, vec, block_out, second, hidden, gb, gp, gm, snd, sums, nj, chans)
        at = pl.ds(m * t, t)
        for p in peers(nj, c):
            send(snd.at[p, :, at], ga.at[c, :, at], back_sems.at[0, m], back_sems.at[1, m], (d, p))
        ga[c, :, at] = snd[c, :, at]
    weight_grads(act, gp, second, gb, hidden, cot, grads, nj, scatter)
    for m in range(mb):
        whole = ga.at[pl.ds(0, nj - 1), :, pl.ds(m * t, t)]
        pltpu.make_async_remote_copy(src_ref=whole, dst_ref=whole, send_sem=back_sems.at[0, m], recv_sem=back_sems.at[1, m], device_id=here, device_id_type=MESH).wait()

    for q in range(packs):
        backward_pack(dims, q, skip, keep, u, ga, slope, carry, out, zw_dp.at[d], pw, xs, gy, ys, sc)
        share(out, gn, gn_sems, q)
        if direct:
            if q == 0:
                scatter.add_twin()
            if q == 2:
                scatter.add_first()
            if q == 3:
                scatter.add_second(n_dp)
    exchange_start(zw_dp, box_sems.at[3], n_dp, d, over_dp)
    for q in range(packs):
        settle(gn, gn_sems, q)

    def finish_rows(m, _):
        at = pl.ds(pl.multiple_of(m * t, t), t)
        n, scale = layer_stats(tokens[at, :].astype(F32))
        grad = gn[:, :, at].reshape(feats, t).astype(F32).T
        add_wide(sums, 8, column_sum(grad * n))
        grad_tokens[at, :] = (gm[at, :] + layer_back(grad * gain, n, scale)).astype(BF16)
        return 0
    lax.fori_loop(0, mb, finish_rows, 0)

    vec_chan[c] = sums[...]
    exchange_start(vec_chan, box_sems.at[4], nj, c, over_chan)
    exchange_wait(zw_dp, box_sems.at[3], n_dp, here)
    zw = [sum(zw_dp[k, a] for k in range(n_dp)) for a in range(5)]
    for k, x in enumerate(mode_gradients([modes[a] for a in range(5)], zw)):
        mode_out[k] = x
    mode_out[5] = zw[4]
    exchange_wait(vec_chan, box_sems.at[4], nj, here)
    vec_dp[d] = sum(vec_chan[k] for k in range(nj))
    exchange_start(vec_dp, box_sems.at[5], n_dp, d, over_dp)
    if direct:
        scatter.finish(results, n_dp)
    exchange_wait(vec_dp, box_sems.at[5], n_dp, here)
    vec_out[...] = sum(vec_dp[k] for k in range(n_dp))
    if direct:
        gather_copies.finish()
        scatter_copies.finish()


def whole(tokens, cot, vec, modes, skip, keep, weights, mb, n_dp, nj):
    width, feats = tokens.shape
    chans = feats // nj
    t = width // mb
    h = t // SPAN
    blocks = nj * h
    rows = mb * blocks
    packs = chans // PACK
    groups = modes.shape[1]
    direct = nj == 8 and n_dp == 4 and packs == 4 and all(w.shape[0] % 16 == 0 for w in weights)
    if not direct:
        weights = [lax.all_gather(w, ("dp", "chan"), axis=0, tiled=True) for w in weights]
        weights = [w.reshape(4, 2, 2, 2, -1, w.shape[1]) for w in weights]
    per = [w.shape[-2:] for w in weights]
    full = [(4, 2, 2, 2) + p for p in per]
    ff = per[1][1]
    shape = jax.ShapeDtypeStruct
    shapes = [
        shape((width, feats), BF16), shape((width, feats), BF16), shape((6,) + modes.shape[1:], F32), shape(vec.shape, F32),
    ] + ([shape(p, F32) for p in per] if direct else [shape(f, BF16) for f in full])
    dma, vm = pltpu.SemaphoreType.DMA, pltpu.VMEM
    scratch = [vm((nj, chans, width), BF16)] * 6 + [
        vm((packs, rows * PACK, 128), F32),
        vm((packs, 4, blocks * PACK, 128), F32),
        vm((width, feats), BF16), vm((width, ff), BF16), vm((width, ff), BF16), vm((width, 2 * feats), BF16), vm((width, feats), F32),
        vm((n_dp,) + vec.shape, F32), vm((nj,) + vec.shape, F32), vm((n_dp, 4) + modes.shape[1:], F32),
        vm((n_dp, 5) + modes.shape[1:], F32), vm(modes.shape, F32), vm(vec.shape, F32), vm(vec.shape, F32),
        vm((18, groups, 128), F32),
        vm((rows * PACK, 128), F32), vm((rows * PACK, 128), F32), vm((rows * PACK, 128), F32),
        vm((4, blocks * PACK, 128), F32),
        dma((6, 2)), dma((2, packs)), dma((2, packs)), dma((2, mb)), dma((2, packs)),
    ]
    if direct:
        scratch += [vm(f, BF16) for f in full] * 2
        half = [(r, k // 2) for r, k in per]
        scratch += [vm((4, 2, 2) + p, BF16) for p in per]
        scratch += [vm((4, 2) + p, BF16) for p in half] * 2
        scratch += [vm((4,) + p, BF16) for p in half] * 2
        scratch += [vm((4,) + p, BF16) for p in per]
        scratch += [dma((2, 36)), dma((2, 33))]
    vmem = pl.BlockSpec(memory_space=pltpu.VMEM)
    outs = pl.pallas_call(
        functools.partial(whole_kernel, (nj, chans, mb, h), n_dp, direct),
        out_shape=shapes,
        in_specs=[vmem] * 9,
        out_specs=[vmem] * 7,
        scratch_shapes=scratch,
        compiler_params=pltpu.CompilerParams(collective_id=0, has_side_effects=True, vmem_limit_bytes=60 << 20),
        name="whole",
    )(tokens, cot, vec, modes, skip, keep, *weights)
    grads = outs[4:]
    if not direct:
        grads = [lax.psum_scatter(g.reshape(-1, g.shape[-1]).astype(F32), ("dp", "chan"), scatter_dimension=0, tiled=True) for g in grads]
    return outs[:4], grads


def on_device(
    tokens, cotangent, lengths, norm_gain, log_step, log_decay, frequency, readout_real, readout_imaginary,
    skip_gain, out_weight, out_bias, ffn_gain, in_weight, in_bias, back_weight,
):
    mb, rows, feats = tokens.shape
    chans, groups = log_decay.shape
    nj, n_dp = lax.axis_size("chan"), lax.axis_size("dp")
    shards = n_dp * nj
    place = lax.axis_index("dp") * nj + lax.axis_index("chan")
    vectors = (out_bias, norm_gain, ffn_gain, in_bias)

    def placed(x):
        return lax.dynamic_update_slice(jnp.zeros((shards * x.shape[0],), F32), x.astype(F32), (place * x.shape[0],))
    vec = jnp.concatenate([placed(x) for x in vectors]).reshape(-1, 128)
    mine = jnp.arange(groups * n_dp) // groups == lax.axis_index("dp")
    modes = [jnp.broadcast_to(log_step[:, None], (chans, groups * n_dp))]
    modes += [jnp.where(mine, jnp.tile(x, (1, n_dp)), 0.0) for x in (log_decay, frequency, readout_real, readout_imaginary)]
    modes = jnp.stack([x.reshape(-1, 128) for x in modes])
    skip = jnp.broadcast_to(skip_gain[:, None], (chans, 128))
    keep = keep_rows(lengths[:, 0], nj * rows // SPAN, mb)
    (block_out, grad_tokens, mode_grads, vec), (g_out, g_in, g_back) = whole(
        tokens.reshape(mb * rows, feats), cotangent.reshape(mb * rows, feats), vec, modes, skip, keep,
        (out_weight, in_weight, back_weight), mb, n_dp, nj)
    g_ls, g_ld, g_fr, g_rr, g_ri, g_skip = (x.reshape(chans, -1) for x in mode_grads)
    first = lax.axis_index("dp") * groups
    own = [lax.dynamic_slice_in_dim(x, first, groups, 1) for x in (g_ld, g_fr, g_rr, g_ri)]
    vec = vec.reshape(-1)
    cuts, start = [], 0
    for x in vectors:
        cuts.append(lax.dynamic_slice_in_dim(vec, start + place * x.shape[0], x.shape[0], 0))
        start += shards * x.shape[0]
    g_bo, g_g1, g_g2, g_bi = cuts
    return (
        block_out.reshape(tokens.shape), grad_tokens.reshape(tokens.shape), g_g1, jnp.sum(g_ls, 1), *own, g_skip[:, 0],
        g_out, g_bo, g_g2, g_in, g_bi, g_back,
    )


def solution(mesh):
    both = ("dp", "chan")
    rows, row, vec, chan, mode = P(None, both, None), P(both, None), P(both), P("chan"), P("chan", "dp")
    return jax.shard_map(
        on_device, mesh=mesh,
        in_specs=(rows, rows, P(None, "dp"), vec, chan, mode, mode, mode, mode, chan, row, vec, vec, row, vec, row),
        out_specs=(rows, rows, vec, chan, mode, mode, mode, mode, chan, row, vec, vec, row, vec, row),
        check_vma=False,
    )
```

```python
import functools
import jax
import jax.numpy as jnp
from jax import lax
from jax.experimental import pallas as pl
from jax.experimental.pallas import tpu as pltpu
from jax.sharding import PartitionSpec as P

SPAN = 128
PACK = 16
HI = lax.Precision.HIGHEST


def keep_row(span, i):
    return jnp.where((span & (i * SPAN)) == 0, 0.0, 1.0)


def cmul(ar, ai, br, bi):
    return ar * br - ai * bi, ar * bi + ai * br


def mode_rows(ls, ld, fr, rr, ri):
    dt = jnp.exp(ls)
    a_r = -jnp.exp(ld)
    a_i = fr
    t_r, t_i = dt * a_r, dt * a_i
    mag = jnp.exp(t_r)
    l_r, l_i = mag * jnp.cos(t_i), mag * jnp.sin(t_i)
    mod = a_r * a_r + a_i * a_i
    u_r = l_r - 1.0
    q_r = (u_r * a_r + l_i * a_i) / mod
    q_i = (l_i * a_r - u_r * a_i) / mod
    w_r, w_i = cmul(rr, ri, q_r, q_i)
    return dict(dt=dt, a_r=a_r, a_i=a_i, t_r=t_r, t_i=t_i, l_r=l_r, l_i=l_i, mod=mod,
                q_r=q_r, q_i=q_i, w_r=w_r, w_i=w_i)


def mode_prelude(modes_ref, pw_ref):
    m = mode_rows(modes_ref[0], modes_ref[1], modes_ref[2], modes_ref[3], modes_ref[4])
    r, i = m["l_r"], m["l_i"]
    for k in range(8):
        pw_ref[2 * k] = r
        pw_ref[2 * k + 1] = i
        r, i = cmul(r, i, r, i)
    pw_ref[16] = 2.0 * m["w_r"]
    pw_ref[17] = 2.0 * m["w_i"]


def group_rows(pw_ref, g):
    rows = [pw_ref[k, pl.ds(g, 1), :] for k in range(18)]
    return [jnp.broadcast_to(x, (8, 128)) for x in rows]


def power_table(rows, reverse):
    sub = lax.broadcasted_iota(jnp.int32, (8, 128), 0)
    if reverse:
        sub = 7 - sub
        r, i = jnp.ones((8, 128), jnp.float32), jnp.zeros((8, 128), jnp.float32)
    else:
        r, i = rows[0], rows[1]
    for k in range(3):
        bit = ((sub >> k) & 1) == 1
        fr = jnp.where(bit, rows[2 * k], 1.0)
        fi = jnp.where(bit, rows[2 * k + 1], 0.0)
        r, i = cmul(r, i, fr, fi)
    parts = [(r, i)]
    for k in range(3, 7):
        more = [cmul(a, b, rows[2 * k], rows[2 * k + 1]) for a, b in parts]
        parts = more + parts if reverse else parts + more
    return (jnp.concatenate([p[0] for p in parts], 0), jnp.concatenate([p[1] for p in parts], 0))


def nt(a, b, **kw):
    return lax.dot_general(a, b, (((1,), (1,)), ((), ())), preferred_element_type=jnp.float32, **kw)


def tn(a, b, **kw):
    return lax.dot_general(a, b, (((0,), (0,)), ((), ())), preferred_element_type=jnp.float32, **kw)


def nn(a, b, **kw):
    return jnp.dot(a, b, preferred_element_type=jnp.float32, **kw)


def kernel_rows(rd_r, w_r):
    t = lax.broadcasted_iota(jnp.int32, (SPAN, 128), 0)
    src = jnp.where(t == SPAN - 1, jnp.concatenate([w_r] * 16, 0), rd_r)
    pick = (lax.broadcasted_iota(jnp.int32, (8, 128), 1) // 32
            == lax.broadcasted_iota(jnp.int32, (8, 128), 0)).astype(jnp.float32)
    return pltpu.roll(nt(pick, src, precision=HI), 1, 1)


def toeplitz(row):
    base = pltpu.roll(jnp.broadcast_to(row, (8, 128)), 0, 1, stride=1, stride_axis=0)
    parts = [base] + [pltpu.roll(base, 8 * v, 1) for v in range(1, 16)]
    whole = jnp.concatenate(parts, 0)
    s = lax.broadcasted_iota(jnp.int32, (SPAN, 128), 0)
    t = lax.broadcasted_iota(jnp.int32, (SPAN, 128), 1)
    return jnp.where(t >= s, whole, 0.0).astype(jnp.bfloat16)


def lag_sums(g):
    s = lax.broadcasted_iota(jnp.int32, (SPAN, 128), 0)
    t = lax.broadcasted_iota(jnp.int32, (SPAN, 128), 1)
    g = jnp.where(t >= s, g, 0.0)
    n = SPAN
    while n > 8:
        n //= 2
        g = g[:n] + pltpu.roll(g[n:], 128 - n, 1)
    for n in (4, 2, 1):
        g = g + pltpu.roll(pltpu.roll(g, 128 - n, 1), 8 - n, 0)
    return g[0:1]


def lane_owner(rows):
    return lax.broadcasted_iota(jnp.int32, (rows, 128), 1) // 32


def fold(stack, rows):
    width = stack.shape[1]
    own = (lax.broadcasted_iota(jnp.int32, (rows, width), 1) // 32) & 3
    out = stack[:rows]
    for k in range(1, 4):
        out = jnp.where(own == k, stack[k * rows:(k + 1) * rows], out)
    return out


def spread(packed, rows):
    width = packed.shape[1]
    own = (lax.broadcasted_iota(jnp.int32, (rows, width), 1) // 32) & 3
    return jnp.concatenate([jnp.where(own == k, packed, 0.0) for k in range(4)], 0)


def gelu_pair(v):
    half = 0.5 * (1.0 + lax.erf(v * 0.7071067811865476))
    return v * half, half + v * jnp.exp(-0.5 * v * v) * 0.3989422804014327


def block_rows(r):
    return pl.ds(pl.multiple_of(r * PACK, PACK), PACK)


def unpack(src_ref, q, xs, nj, mb, h, blocks, gain):
    def body(j, _):
        for m in range(mb):
            for k in range(h):
                x = src_ref[j, block_rows(q), pl.ds((m * h + k) * 128, 128)]
                xs[block_rows(m * blocks + j * h + k), :] = x.astype(jnp.float32) * gain
        return 0
    lax.fori_loop(0, nj, body, 0)


def rows_of(pw_ref, k, q, mb):
    parts = [jnp.broadcast_to(pw_ref[k, pl.ds(q * 4 + g, 1), :], (mb, 128)) for g in range(4)]
    parts.append(jnp.zeros((PACK - 4 * mb, 128), jnp.float32))
    return jnp.concatenate(parts, 0)


def forward_pack(dims, q, skip_ref, gain_ref, span, u_ref, act_ref, slope_ref, carry_ref, pw_ref, xs, ys, sc):
    nj, chans, mb, h = dims
    blocks = nj * h
    rows = mb * blocks
    unpack(u_ref, q, xs, nj, mb, h, blocks, gain_ref[block_rows(q), :])

    def states(g, _):
        rws = group_rows(pw_ref, q * 4 + g)
        p_r, p_i = power_table(rws, True)
        back = (SPAN - 1 - lax.broadcasted_iota(jnp.int32, (SPAN, 128), 0)).astype(jnp.float32)
        table = jnp.concatenate([p_r, p_i, back * p_r, back * p_i], 1).astype(jnp.bfloat16)
        x = jnp.concatenate([xs[pl.ds(4 * g + k, rows, stride=PACK), :] for k in range(4)], 0).astype(jnp.bfloat16)
        s = fold(nn(x, table), rows)
        for a in range(4):
            for m in range(mb):
                sc[a, pl.ds(g * mb + m, blocks, stride=PACK), :] = s[m * blocks:(m + 1) * blocks, a * 128:(a + 1) * 128]
        return 0
    lax.fori_loop(0, 4, states, 0, unroll=2)
    h_r, h_i = rows_of(pw_ref, 14, q, mb), rows_of(pw_ref, 15, q, mb)

    def step(i, c):
        at = block_rows(i)
        keep = keep_row(span, i)
        c = [x * keep for x in c]
        s = [sc[a, at, :] for a in range(4)]
        for a in range(4):
            carry_ref[q, a, at, :] = c[a]
        z_r, z_i = cmul(c[0], c[1], h_r, h_i)
        d_r, d_i = cmul(c[2] + SPAN * c[0], c[3] + SPAN * c[1], h_r, h_i)
        return (z_r + s[0], z_i + s[1], d_r + s[2], d_i + s[3])
    zero = jnp.zeros((PACK, 128), jnp.float32)
    lax.fori_loop(0, blocks, step, (zero,) * 4)

    def outputs(g, _):
        rws = group_rows(pw_ref, q * 4 + g)
        e_r, e_i = power_table(rws, False)
        w_r, w_i = jnp.concatenate([rws[16]] * 16, 0), jnp.concatenate([rws[17]] * 16, 0)
        r_r, r_i = cmul(e_r, e_i, w_r, w_i)
        krow = kernel_rows(r_r, rws[16])
        table = jnp.concatenate([r_r, -r_i], 1).astype(jnp.bfloat16)
        c = jnp.concatenate([
            jnp.concatenate([carry_ref[q, a, pl.ds(g * mb + m, blocks, stride=PACK), :] for m in range(mb)], 0)
            for a in range(2)], 1)
        across = nt(spread(c, rows).astype(jnp.bfloat16), table)
        for k in range(4):
            x = xs[pl.ds(4 * g + k, rows, stride=PACK), :].astype(jnp.bfloat16)
            y = across[k * rows:(k + 1) * rows] + nn(x, toeplitz(krow[k:k + 1]))
            ys[pl.ds(4 * g + k, rows, stride=PACK), :] = y
        return 0
    lax.fori_loop(0, 4, outputs, 0, unroll=2)
    skip = skip_ref[block_rows(q), :]

    def finish(j, _):
        for m in range(mb):
            for k in range(h):
                r = m * blocks + j * h + k
                v = ys[block_rows(r), :] + skip * xs[block_rows(r), :]
                a, d = gelu_pair(v)
                act_ref[j, block_rows(q), pl.ds((m * h + k) * 128, 128)] = a.astype(jnp.bfloat16)
                slope_ref[q, block_rows(r), :] = d
        return 0
    lax.fori_loop(0, nj, finish, 0)


def backward_pack(dims, q, skip_ref, gain_ref, span, u_ref, ga_ref, slope_ref, carry_ref, gn_ref, zw_ref, ng_ref, pw_ref, xs, gy, gx, sc):
    nj, chans, mb, h = dims
    blocks = nj * h
    rows = mb * blocks
    unpack(u_ref, q, xs, nj, mb, h, blocks, gain_ref[block_rows(q), :])
    def start(j, _):
        for m in range(mb):
            for k in range(h):
                r = m * blocks + j * h + k
                x = ga_ref[j, block_rows(q), pl.ds((m * h + k) * 128, 128)]
                gy[block_rows(r), :] = x.astype(jnp.float32) * slope_ref[q, block_rows(r), :]
        return 0
    lax.fori_loop(0, nj, start, 0)

    def states(g, _):
        gg = q * 4 + g
        rws = group_rows(pw_ref, gg)
        e_r, e_i = power_table(rws, False)
        ahead = (1 + lax.broadcasted_iota(jnp.int32, (SPAN, 128), 0)).astype(jnp.float32)
        table = jnp.concatenate([e_r, e_i, ahead * e_r, ahead * e_i], 1).astype(jnp.bfloat16)
        ups = [gy[pl.ds(4 * g + k, rows, stride=PACK), :].astype(jnp.bfloat16) for k in range(4)]
        lag = []
        for k in range(4):
            x = xs[pl.ds(4 * g + k, rows, stride=PACK), :].astype(jnp.bfloat16)
            lag.append(lag_sums(tn(x, ups[k])))
        lag = jnp.concatenate(lag + [jnp.zeros((4, 128), jnp.float32)], 0)
        own8 = lax.broadcasted_iota(jnp.int32, (8, 128), 1) // 32 == lax.broadcasted_iota(jnp.int32, (8, 128), 0)
        lag0 = jnp.sum(jnp.where(own8, jnp.broadcast_to(lag[:, 0:1], (8, 128)), 0.0), axis=0, keepdims=True)
        lane = lax.broadcasted_iota(jnp.int32, (8, 128), 1)
        later = jnp.where(lane == 127, 0.0, pltpu.roll(lag, 127, 1))
        top = later.astype(jnp.bfloat16)
        low = (later - top.astype(jnp.float32)).astype(jnp.bfloat16)
        stack = jnp.concatenate(ups + [top, low], 0)
        s = nn(stack, table)
        near = s[4 * rows:4 * rows + 8] + s[4 * rows + 8:]
        own = jnp.concatenate([own8] * 4, 1)
        near = jnp.sum(jnp.where(own, near, 0.0), axis=0, keepdims=True)
        zw_ref[0, pl.ds(gg, 1), :] = near[:, 0:128] + lag0
        for a in range(1, 4):
            zw_ref[a, pl.ds(gg, 1), :] = near[:, a * 128:(a + 1) * 128]
        zw_ref[4, pl.ds(gg, 1), :] = lag0
        s = fold(s[:4 * rows], rows)
        for a in range(4):
            for m in range(mb):
                sc[a, pl.ds(g * mb + m, blocks, stride=PACK), :] = s[m * blocks:(m + 1) * blocks, a * 128:(a + 1) * 128]
        return 0
    lax.fori_loop(0, 4, states, 0, unroll=2)

    h_r, h_i = rows_of(pw_ref, 14, q, mb), rows_of(pw_ref, 15, q, mb)

    def step(n, c):
        i = blocks - 1 - n
        at = block_rows(i)
        a_r, a_i, z_r, z_i, w_r, w_i = c
        q_ = [sc[a, at, :] for a in range(4)]
        f = [carry_ref[q, a, at, :] for a in range(4)]
        d = cmul(q_[0], q_[1], f[0], f[1])
        e1 = cmul(q_[2], q_[3], f[0], f[1])
        e2 = cmul(q_[0], q_[1], f[2], f[3])
        sc[0, at, :] = a_r
        sc[1, at, :] = a_i
        keep = keep_row(span, i)
        n_r, n_i = cmul(a_r, a_i, h_r, h_i)
        return ((n_r + q_[0]) * keep, (n_i + q_[1]) * keep, z_r + d[0], z_i + d[1], w_r + e1[0] + e2[0], w_i + e1[1] + e2[1])
    zero = jnp.zeros((PACK, 128), jnp.float32)
    out = lax.fori_loop(0, blocks, step, (zero,) * 6)
    for a in range(4):
        for g in range(4):
            add = jnp.sum(out[2 + a][g * mb:(g + 1) * mb], axis=0, keepdims=True)
            zw_ref[a, pl.ds(q * 4 + g, 1), :] += add

    def outputs(g, _):
        rws = group_rows(pw_ref, q * 4 + g)
        e_r, e_i = power_table(rws, False)
        w_r, w_i = jnp.concatenate([rws[16]] * 16, 0), jnp.concatenate([rws[17]] * 16, 0)
        r_r = e_r * w_r - e_i * w_i
        krow = kernel_rows(r_r, rws[16])
        p_r, p_i = power_table(rws, True)
        r_r, r_i = cmul(p_r, p_i, w_r, w_i)
        table = jnp.concatenate([r_r, -r_i], 1).astype(jnp.bfloat16)
        c = jnp.concatenate([
            jnp.concatenate([sc[a, pl.ds(g * mb + m, blocks, stride=PACK), :] for m in range(mb)], 0)
            for a in range(2)], 1)
        across = nt(spread(c, rows).astype(jnp.bfloat16), table)
        for k in range(4):
            up = gy[pl.ds(4 * g + k, rows, stride=PACK), :].astype(jnp.bfloat16)
            y = across[k * rows:(k + 1) * rows] + nt(up, toeplitz(krow[k:k + 1]))
            gx[pl.ds(4 * g + k, rows, stride=PACK), :] = y
        return 0
    lax.fori_loop(0, 4, outputs, 0, unroll=2)

    skip = skip_ref[block_rows(q), :]
    def finish(j, total):
        for m in range(mb):
            for k in range(h):
                r = m * blocks + j * h + k
                v = (gx[block_rows(r), :] + skip * gy[block_rows(r), :]).astype(jnp.bfloat16)
                cols = pl.ds((m * h + k) * 128, 128)
                gn_ref[j, block_rows(q), cols] = v
                total = total + v.astype(jnp.float32) * u_ref[j, block_rows(q), cols].astype(jnp.float32)
        return total
    ng_ref[block_rows(q), :] = lax.fori_loop(0, nj, finish, jnp.zeros((PACK, 128), jnp.float32))


def mode_gradients(modes, zw):
    m = mode_rows(*modes)
    z_r, z_i, v_r, v_i = zw[0], zw[1], zw[2], zw[3]
    rr, ri = modes[3], modes[4]
    g_rr = 2.0 * (z_r * m["q_r"] - z_i * m["q_i"])
    g_ri = -2.0 * (z_r * m["q_i"] + z_i * m["q_r"])
    k_r, k_i = cmul(rr, ri, m["a_r"] / m["mod"], -m["a_i"] / m["mod"])
    s_r, s_i = cmul(k_r, k_i, m["l_r"], m["l_i"])
    h1 = cmul(z_r, z_i, s_r, s_i)
    h2 = cmul(m["w_r"], m["w_i"], v_r, v_i)
    h_r, h_i = h1[0] + h2[0], h1[1] + h2[1]
    zc = cmul(z_r, z_i, m["w_r"], m["w_i"])
    za = cmul(zc[0], zc[1], m["a_r"] / m["mod"], -m["a_i"] / m["mod"])
    j_r, j_i = h_r * m["dt"] - za[0], h_i * m["dt"] - za[1]
    g_ls = 2.0 * (h_r * m["t_r"] - h_i * m["t_i"])
    return g_ls, 2.0 * m["a_r"] * j_r, -2.0 * j_i, g_rr, g_ri


def keep_rows(lengths, blocks, mb):
    at = jnp.arange(blocks, dtype=jnp.int32)[:, None] * SPAN
    keep = (at % lengths[None, :] != 0).astype(jnp.float32)
    rows = jnp.concatenate([keep] * 4 + [jnp.zeros((blocks, PACK - 4 * mb), jnp.float32)], 1)
    return jnp.broadcast_to(rows[:, :, None], (blocks, PACK, 128))


MESH = pl.DeviceIdType.MESH
F32, BF16 = jnp.float32, jnp.bfloat16


def layer_stats(v):
    average = jnp.mean(v, axis=-1, keepdims=True)
    centred = v - average
    spread = jnp.mean(centred * centred, axis=-1, keepdims=True)
    scale = lax.rsqrt(spread + 1e-05)
    return centred * scale, scale


def layer_back(q, n, scale):
    return scale * (q - jnp.mean(q, axis=-1, keepdims=True) - n * jnp.mean(q * n, axis=-1, keepdims=True))


def column_sum(x):
    return jnp.sum(x, axis=0, keepdims=True)


def peers(count, me):
    return [lax.rem(me + k, count) for k in range(1, count)]


def greet(n_dp, n_chan, d, c):
    barrier = pltpu.get_barrier_semaphore()
    for p in peers(n_dp, d):
        pl.semaphore_signal(barrier, inc=1, device_id=(p, c), device_id_type=MESH)
    for p in peers(n_chan, c):
        pl.semaphore_signal(barrier, inc=1, device_id=(d, p), device_id_type=MESH)
    pl.semaphore_wait(barrier, n_dp + n_chan - 2)


def send(src, dst, send_sem, recv_sem, to):
    copy = pltpu.make_async_remote_copy(src_ref=src, dst_ref=dst, send_sem=send_sem, recv_sem=recv_sem, device_id=to, device_id_type=MESH)
    copy.start()
    return copy


def settle(whole, send_sem, recv_sem, here):
    pltpu.make_async_remote_copy(src_ref=whole, dst_ref=whole, send_sem=send_sem, recv_sem=recv_sem, device_id=here, device_id_type=MESH).wait()


class Exchange:
    def __init__(self, box, sems, count, me, to, here):
        self.box, self.sems, self.count, self.me, self.to, self.here = box, sems, count, me, to, here

    def start(self):
        for p in peers(self.count, self.me):
            send(self.box.at[self.me], self.box.at[self.me], self.sems.at[0], self.sems.at[1], self.to(p))

    def wait(self):
        settle(self.box.at[pl.ds(0, self.count - 1)], self.sems.at[0], self.sems.at[1], self.here)

    def total(self):
        return sum(self.box[k] for k in range(self.count))


class Copies:
    def __init__(self, sems):
        self.sems = sems
        self.used = 0
        self.unsent = []

    def put(self, src, dst, to):
        n = self.used
        self.used += 1
        copy = send(src, dst, self.sems.at[0, n], self.sems.at[1, n], to)
        self.unsent.append(copy)
        return copy

    def finish(self):
        for copy in self.unsent:
            copy.wait_send()


def arrive(copies):
    for copy in copies:
        copy.wait_recv()


class Place:
    def __init__(self, d, c):
        self.d, self.c = d, c
        self.a, self.b, self.core = c // 4, lax.rem(c // 2, 2), lax.rem(c, 2)

    def at(self, a, b, core):
        return (self.d, a * 4 + b * 2 + core)

    @property
    def over_a(self):
        return self.at(1 - self.a, self.b, self.core)

    @property
    def over_b(self):
        return self.at(self.a, 1 - self.b, self.core)

    @property
    def twin(self):
        return self.at(self.a, self.b, 1 - self.core)


def halves(w):
    cols = w.shape[-1] // 2
    return pl.ds(0, cols), pl.ds(cols, cols)


class Gather:
    def __init__(self, owns, wholes, copies, here):
        self.owns, self.wholes, self.copies, self.here = owns, wholes, copies, here
        self.side = []

    def same(self, ref, to):
        return self.copies.put(ref, ref, to)

    def along_dp(self, n_dp):
        i = self.here
        self.step = []
        for own, w in zip(self.owns, self.wholes):
            w[i.d, i.a, i.b, i.core] = own[...]
            ref = w.at[i.d, i.a, i.b, i.core]
            self.step += [self.same(ref, (p, i.c)) for p in peers(n_dp, i.d)]

    def first_hop(self):
        i = self.here
        arrive(self.step)
        self.step = []
        for w in self.wholes:
            low, high = halves(w)
            self.step.append(self.same(w.at[:, i.a, i.b, i.core, :, low], i.over_b))
            self.step.append(self.same(w.at[:, i.a, i.b, i.core, :, high], i.over_a))
        self.side += [self.same(w.at[:, i.a, i.b, i.core], i.twin) for w in self.wholes]

    def second_hop(self):
        i = self.here
        arrive(self.step)
        self.step = []
        for w in self.wholes:
            low, high = halves(w)
            self.step.append(self.same(w.at[:, i.a, :, i.core, :, low], i.over_a))
            self.step.append(self.same(w.at[:, :, i.b, i.core, :, high], i.over_b))
        for w in self.wholes:
            low, high = halves(w)
            self.side.append(self.same(w.at[:, i.a, 1 - i.b, i.core, :, low], i.twin))
            self.side.append(self.same(w.at[:, 1 - i.a, i.b, i.core, :, high], i.twin))

    def last_hop(self):
        i = self.here
        arrive(self.step)
        for w in self.wholes:
            low, high = halves(w)
            self.side.append(self.same(w.at[:, 1 - i.a, :, i.core, :, low], i.twin))
            self.side.append(self.same(w.at[:, :, 1 - i.b, i.core, :, high], i.twin))

    def finish(self):
        arrive(self.side)


class Scatter:
    def __init__(self, grads, boxes, copies, here):
        self.grads, self.copies, self.here = grads, copies, here
        self.twins, self.lows, self.highs, self.low2s, self.high2s, self.lasts = boxes
        self.first = []
        self.step = []

    def to_twin(self, k):
        i = self.here
        self.first.append(self.copies.put(self.grads[k].at[:, :, :, 1 - i.core], self.twins[k], i.twin))

    def add_twin(self):
        i = self.here
        arrive(self.first)
        for g, t in zip(self.grads, self.twins):
            def add(n, _):
                for a in range(2):
                    for b in range(2):
                        t[n, a, b] = (t[n, a, b].astype(F32) + g[n, a, b, i.core].astype(F32)).astype(BF16)
                return 0
            lax.fori_loop(0, t.shape[0], add, 0)
        for t, low_box, high_box in zip(self.twins, self.lows, self.highs):
            low, high = halves(t)
            self.step.append(self.copies.put(t.at[:, 1 - i.a, :, :, low], low_box, i.over_a))
            self.step.append(self.copies.put(t.at[:, :, 1 - i.b, :, high], high_box, i.over_b))

    def add_first(self):
        i = self.here
        arrive(self.step)
        self.step = []
        for t, low_box, high_box in zip(self.twins, self.lows, self.highs):
            low, high = halves(t)
            def add(n, _):
                for k in range(2):
                    low_box[n, k] = (low_box[n, k].astype(F32) + t[n, i.a, k, :, low].astype(F32)).astype(BF16)
                    high_box[n, k] = (high_box[n, k].astype(F32) + t[n, k, i.b, :, high].astype(F32)).astype(BF16)
                return 0
            lax.fori_loop(0, t.shape[0], add, 0)
        for low_box, high_box, low2, high2 in zip(self.lows, self.highs, self.low2s, self.high2s):
            self.step.append(self.copies.put(low_box.at[:, 1 - i.b], low2, i.over_b))
            self.step.append(self.copies.put(high_box.at[:, 1 - i.a], high2, i.over_a))

    def add_second(self, n_dp):
        i = self.here
        arrive(self.step)
        self.step = []
        for low_box, high_box, low2, high2, last in zip(self.lows, self.highs, self.low2s, self.high2s, self.lasts):
            low, high = halves(last)
            for n in range(n_dp):
                low2[n] = (low2[n].astype(F32) + low_box[n, i.b].astype(F32)).astype(BF16)
                high2[n] = (high2[n].astype(F32) + high_box[n, i.a].astype(F32)).astype(BF16)
            for p in peers(n_dp, i.d):
                self.step.append(self.copies.put(low2.at[p], last.at[i.d, :, low], (p, i.c)))
                self.step.append(self.copies.put(high2.at[p], last.at[i.d, :, high], (p, i.c)))

    def finish(self, outs, n_dp):
        i = self.here
        arrive(self.step)
        for low2, high2, last, out in zip(self.low2s, self.high2s, self.lasts, outs):
            low, high = halves(last)
            for cut, box in ((low, low2), (high, high2)):
                total = box[i.d].astype(F32)
                for p in peers(n_dp, i.d):
                    total = total + last[p, :, cut].astype(F32)
                out[:, cut] = total


def wide(vec_ref, first, count):
    return jnp.concatenate([vec_ref[first + k:first + k + 1, :] for k in range(count)], 1)


def add_wide(vec_ref, first, row):
    for k in range(row.shape[1] // 128):
        vec_ref[first + k:first + k + 1, :] += row[:, k * 128:(k + 1) * 128]


def put_own(vec_ref, first, own, shard, shards):
    size = own.shape[1]
    rows = size * shards // 128
    while own.shape[1] < 128:
        own = jnp.concatenate([own, own], 1)
    index = 128 * lax.broadcasted_iota(jnp.int32, (rows, 128), 0) + lax.broadcasted_iota(jnp.int32, (rows, 128), 1)
    inside = (index >= shard * size) & (index < (shard + 1) * size)
    vec_ref[first:first + rows, :] = jnp.where(inside, jnp.broadcast_to(own, (rows, 128)), 0.0)


def pick_own(vec_ref, first, size, shard):
    start = shard * size
    row = vec_ref[pl.ds(first + start // 128, 1), :]
    row = pltpu.roll(jnp.broadcast_to(row, (8, 128)), lax.rem(128 - lax.rem(start, 128), 128), 1)
    return row[0:1, :size]


def to_column(row):
    return jnp.broadcast_to(row, (128, row.shape[1])).T


def padded(x, lanes=128):
    if x.shape[1] == lanes:
        return x
    return jnp.concatenate([x, jnp.zeros((x.shape[0], lanes - x.shape[1]), x.dtype)], 1)


def lane_pick(groups, k):
    lane = lax.broadcasted_iota(jnp.int32, (groups, 128), 1)
    return (lane == 4 * lax.broadcasted_iota(jnp.int32, (groups, 128), 0) + k).astype(F32)


def spread_modes(rows, modes):
    groups = modes.shape[1]
    for k in range(4):
        part = nt(lane_pick(groups, k), rows, precision=HI)
        for a in range(modes.shape[0]):
            modes[a, :, k * 32:(k + 1) * 32] = part[:, a * 32:(a + 1) * 32]


def collect_modes(arrays):
    groups = arrays[0].shape[0]
    total = None
    for k in range(4):
        part = jnp.concatenate([x[:, k * 32:(k + 1) * 32] for x in arrays], 1)
        part = tn(part, lane_pick(groups, k), precision=HI)
        total = part if total is None else total + part
    return total


def flat(x):
    return x.reshape(-1, x.shape[-1])


def row_block(m, t):
    return pl.ds(pl.multiple_of(m * t, t), t)


def dense_up(m, t, tokens, act, w_out, w_in, vec, keeps):
    middle, gate_ref, gated_ref, second, hidden, slopes = keeps
    at = row_block(m, t)
    feats = tokens.shape[1]
    tile = w_in.shape[-1] // 4
    project = tn(act[:, :, at].reshape(feats, t), flat(w_out[...])) + wide(vec, 0, 2 * feats // 128)
    gate = jax.nn.sigmoid(project[:, feats:])
    gated = project[:, :feats] * gate
    total = tokens[at, :].astype(F32) + gated
    gate_ref[at, :] = gate
    gated_ref[at, :] = gated
    middle[at, :] = total
    n, _scale = layer_stats(total)
    after = (n * wide(vec, 12, feats // 128)).astype(BF16)
    second[at, :] = after
    for f in range(4):
        cols = slice(f * tile, (f + 1) * tile)
        before = nn(after, flat(w_in[:, :, :, :, :, cols])) + wide(vec, 16 + f * tile // 128, tile // 128)
        high, slope = gelu_pair(before)
        hidden[at, cols] = high.astype(BF16)
        slopes[at, cols] = slope


def dense_down(m, t, cot, wholes, vec, block_out, keeps, gb, gp, snd, sums):
    w_out, w_in, w_back = wholes
    middle, gate_ref, gated_ref, second, hidden, slopes = keeps
    at = row_block(m, t)
    feats = cot.shape[1]
    tile = w_in.shape[-1] // 4
    up = cot[at, :]
    total = middle[at, :]
    n, scale = layer_stats(total)
    gain = wide(vec, 12, feats // 128)
    back = jnp.zeros((t, feats), F32)
    for f in range(4):
        cols = slice(f * tile, (f + 1) * tile)
        wb = flat(w_back[f])
        low = (slopes[at, cols] * nt(up, wb)).astype(BF16)
        gb[at, cols] = low
        add_wide(sums, 16 + f * tile // 128, column_sum(low.astype(F32)))
        total = total + nn(hidden[at, cols], wb)
        back = back + nt(low, flat(w_in[:, :, :, :, :, cols]))
    block_out[at, :] = total.astype(BF16)
    add_wide(sums, 12, column_sum(back * n))
    grad = up.astype(F32) + layer_back(back * gain, n, scale)
    middle[at, :] = grad
    gate = gate_ref[at, :]
    first = (grad * gate).astype(BF16)
    last = (grad * gated_ref[at, :] * (1.0 - gate)).astype(BF16)
    gp[at, :feats] = first
    gp[at, feats:] = last
    add_wide(sums, 0, column_sum(first.astype(F32)))
    add_wide(sums, feats // 128, column_sum(last.astype(F32)))
    both = jnp.concatenate([first, last], 1)
    snd[:, :, at] = nt(flat(w_out[...]), both).astype(BF16).reshape(snd.shape[:2] + (t,))


def shaped(x, g):
    return x.astype(BF16).reshape(g.shape[1:])


def outer_products(left, right, g):
    size = left.shape[1] // 4
    def one(n, _):
        g[n] = shaped(tn(left[:, row_block(n, size)], right[...]), g)
        return 0
    lax.fori_loop(0, 4, one, 0)


def whole_kernel(dims, n_dp, direct, *refs):
    nj, chans, mb, h = dims
    refs = list(refs)
    def take(n):
        out = refs[:n]
        del refs[:n]
        return out
    tokens, cot, lengths, log_step, skip_row, *mode_parts = take(9)
    vectors = take(4)
    given = take(3)
    block_out, grad_tokens = take(2)
    g_step, g_skip, *g_modes = take(6)
    g_vectors = take(4)
    results = take(3)
    u, snd, act, out, ga, gn, slope, carry = take(8)
    second, hidden, gb, gp = take(4)
    keeps = take(4)
    middle = keeps[0]
    keeps = keeps[:3] + [second, hidden] + keeps[3:]
    vec_dp, vec_chan, vec2_dp, vec2_chan, modes_dp, zw_dp, ng_dp, ng_chan = take(8)
    modes, vec, sums, skip, gain, mode_rows_box = take(6)
    pw, xs, ys, gy, sc = take(5)
    box_sems, in_sems, out_sems, back_sems, gn_sems = take(5)
    d, c = lax.axis_index("dp"), lax.axis_index("chan")
    here = (d, c)
    shards, shard = n_dp * nj, d * nj + c
    packs = chans // PACK
    groups = modes.shape[1]
    width = tokens.shape[0]
    t = width // mb
    feats = nj * chans
    over_dp, over_chan = (lambda p: (p, c)), (lambda p: (d, p))

    def along_dp(box, n):
        return Exchange(box, box_sems.at[n], n_dp, d, over_dp, here)

    def along_chan(box, n):
        return Exchange(box, box_sems.at[n], nj, c, over_chan, here)
    vec_first, vec_second = along_dp(vec_dp, 0), along_chan(vec_chan, 1)
    modes_all = along_dp(modes_dp, 2)
    sums_first, sums_second = along_chan(vec2_chan, 3), along_dp(vec2_dp, 4)
    zw_all, ng_first, ng_second = along_dp(zw_dp, 5), along_dp(ng_dp, 6), along_chan(ng_chan, 7)
    if direct:
        wholes, grads = take(3), take(3)
        boxes = [take(3) for _ in range(6)]
        place = Place(d, c)
        gather_copies, scatter_copies = Copies(refs[0]), Copies(refs[1])
        early = Gather(given[:2], wholes[:2], gather_copies, place)
        late = Gather(given[2:], wholes[2:], gather_copies, place)
        rest = Scatter(grads[:2], [b[:2] for b in boxes], scatter_copies, place)
        ahead = Scatter(grads[2:], [b[2:] for b in boxes], scatter_copies, place)
    else:
        wholes, grads = given, results
    g_out, g_in, g_back = grads

    for k, (own, first) in enumerate(zip(vectors, (0, 8, 12, 16))):
        put_own(vec_dp.at[d], first, own[...].astype(F32), shard, shards)
    for a in range(4):
        modes_dp[d, a] = padded(mode_parts[a][...])
    greet(n_dp, nj, d, c)
    vec_first.start()
    modes_all.start()
    if direct:
        early.along_dp(n_dp)
        late.along_dp(n_dp)

    def normalize(m, _):
        at = row_block(m, t)
        n, _scale = layer_stats(tokens[at, :].astype(F32))
        snd[:, :, at] = n.T.astype(BF16).reshape(nj, chans, t)
        return 0
    lax.fori_loop(0, mb, normalize, 0)

    def share(box, where, sems, q):
        for p in peers(nj, c):
            send(box.at[p, block_rows(q)], where.at[c, block_rows(q)], sems.at[0, q], sems.at[1, q], (d, p))
        where[c, block_rows(q), :] = box[c, block_rows(q), :]

    def shared(where, sems, q):
        settle(where.at[pl.ds(0, nj - 1), block_rows(q)], sems.at[0, q], sems.at[1, q], here)

    for q in range(packs):
        share(snd, u, in_sems, q)
    sums[...] = jnp.zeros(sums.shape, F32)
    sc[...] = jnp.zeros(sc.shape, F32)
    skip[...] = to_column(skip_row[...])
    long = lengths[...] - 1
    row = lax.broadcasted_iota(jnp.int32, (PACK, 128), 0)
    span = jnp.zeros((PACK, 128), jnp.int32)
    for m in range(mb):
        span = jnp.where(lax.rem(row, mb) == m, jnp.broadcast_to(long[:, m:m + 1], (PACK, 128)), span)
    vec_first.wait()
    vec_chan[c] = vec_first.total()
    vec_second.start()
    modes_all.wait()
    kinds = [jnp.broadcast_to(padded(log_step[...]), (32, 128))]
    kinds += [jnp.concatenate([modes_dp[p, a] for p in range(n_dp)], 0) for a in range(4)]
    spread_modes(jnp.concatenate(kinds, 0), modes)
    mode_prelude(modes, pw)
    vec_second.wait()
    vec[...] = vec_second.total()
    for k in range(nj):
        @pl.when(c == k)
        def _():
            first = k * chans
            row = vec[8 + first // 128:9 + first // 128, :]
            gain[...] = to_column(row[:, first % 128:first % 128 + chans])
    if direct:
        early.first_hop()

    for q in range(packs):
        shared(u, in_sems, q)
        forward_pack(dims, q, skip, gain, span, u, out, slope, carry, pw, xs, ys, sc)
        share(out, act, out_sems, q)
        if direct:
            if q == 0:
                early.second_hop()
                late.first_hop()
            if q == 2:
                early.last_hop()
            if q == 3:
                late.second_hop()
    for q in range(packs):
        shared(act, out_sems, q)
    if direct:
        early.finish()

    def rows_up(m, _):
        dense_up(m, t, tokens, act, wholes[0], wholes[1], vec, keeps)
        return 0
    lax.fori_loop(0, mb, rows_up, 0)
    if direct:
        late.last_hop()
    outer_products(hidden, cot, g_back)
    if direct:
        ahead.to_twin(0)
        late.finish()
    for m in range(mb):
        dense_down(m, t, cot, wholes, vec, block_out, keeps, gb, gp, snd, sums)
        at = pl.ds(m * t, t)
        for p in peers(nj, c):
            send(snd.at[p, :, at], ga.at[c, :, at], back_sems.at[0, m], back_sems.at[1, m], (d, p))
        ga[c, :, at] = snd[c, :, at]
        if direct and m == 0:
            ahead.add_twin()
    vec2_chan[c] = sums[...]
    sums_first.start()
    outer_products(second, gb, g_in)
    if direct:
        rest.to_twin(1)
    def outer(n, _):
        g_out[n] = shaped(nn(flat(act[pl.ds(n * (nj // 4), nj // 4)]), gp[...]), g_out)
        return 0
    lax.fori_loop(0, 4, outer, 0)
    if direct:
        rest.to_twin(0)
        ahead.add_first()
    for m in range(mb):
        settle(ga.at[pl.ds(0, nj - 1), :, pl.ds(m * t, t)], back_sems.at[0, m], back_sems.at[1, m], here)
    if direct:
        rest.add_twin()

    for q in range(packs):
        backward_pack(dims, q, skip, gain, span, u, ga, slope, carry, out, zw_dp.at[d], ng_dp.at[d], pw, xs, gy, ys, sc)
        share(out, gn, gn_sems, q)
        if q == 0:
            sums_first.wait()
            vec2_dp[d] = sums_first.total()
            sums_second.start()
        if direct:
            if q == 0:
                ahead.add_second(n_dp)
            if q == 1:
                rest.add_first()
            if q == 2:
                rest.add_second(n_dp)
    zw_all.start()
    ng_first.start()
    sums_second.wait()
    sums[...] = sums_second.total()
    for k, (first, own) in enumerate(zip((0, 8, 12, 16), g_vectors)):
        if k != 1:
            own[...] = pick_own(sums, first, own.shape[1], shard)
    ng_first.wait()
    ng_chan[c, 0:1, :] = padded(column_sum(ng_first.total().T))
    ng_chan[c, 1:8, :] = jnp.zeros((7, 128), F32)
    ng_second.start()
    if direct:
        ahead.finish(results[2:], n_dp)
        rest.finish(results[:2], n_dp)
    zw_all.wait()
    zw = [sum(zw_dp[k, a] for k in range(n_dp)) for a in range(5)]
    found = list(mode_gradients([modes[a] for a in range(5)], zw)) + [zw[4]]
    mode_rows_box[...] = collect_modes(found)
    g_step[...] = column_sum(mode_rows_box[0:32, :])[:, :chans]
    g_skip[...] = mode_rows_box[160:161, :chans]
    for a in range(4):
        each = g_modes[a].shape[0]
        g_modes[a][...] = mode_rows_box[pl.ds(32 * (a + 1) + d * each, each), :chans]
    for q in range(packs):
        shared(gn, gn_sems, q)
    wide_gain = wide(vec, 8, feats // 128)

    def finish_rows(m, _):
        at = row_block(m, t)
        n, scale = layer_stats(tokens[at, :].astype(F32))
        grad = gn[:, :, at].reshape(feats, t).astype(F32).T
        grad_tokens[at, :] = (middle[at, :] + layer_back(grad * wide_gain, n, scale)).astype(BF16)
        return 0
    lax.fori_loop(0, mb, finish_rows, 0)
    ng_second.wait()
    size = g_vectors[1].shape[1]
    start = shard * size
    row = ng_chan[start // chans]
    g_vectors[1][...] = pltpu.roll(row, lax.rem(128 - lax.rem(start, chans), 128), 1)[0:1, :size]
    if direct:
        gather_copies.finish()
        scatter_copies.finish()


def whole(tokens, cot, lengths, log_step, skip, mode_parts, vectors, weights, mb, n_dp, nj):
    width, feats = tokens.shape
    chans = feats // nj
    t = width // mb
    h = t // SPAN
    blocks = nj * h
    rows = mb * blocks
    packs = chans // PACK
    groups = chans // 4
    direct = nj == 8 and n_dp == 4 and packs == 4 and all(w.shape[0] % 16 == 0 for w in weights)
    if not direct:
        weights = [lax.all_gather(w, ("dp", "chan"), axis=0, tiled=True) for w in weights]
        weights = [w.reshape(4, 2, 2, 2, -1, w.shape[1]) for w in weights]
    per = [w.shape[-2:] for w in weights]
    full = [(4, 2, 2, 2) + p for p in per]
    ff = per[1][1]
    shape = jax.ShapeDtypeStruct
    shapes = [shape((width, feats), BF16)] * 2 + [shape((1, chans), F32)] * 2
    shapes += [shape(x.shape, F32) for x in mode_parts] + [shape(x.shape, F32) for x in vectors]
    shapes += [shape(p, F32) for p in per] if direct else [shape(f, BF16) for f in full]
    dma, vm = pltpu.SemaphoreType.DMA, pltpu.VMEM
    sheet, grid = (32, 128), (groups, 128)
    scratch = [vm((nj, chans, width), BF16)] * 6 + [
        vm((packs, rows * PACK, 128), F32),
        vm((packs, 4, blocks * PACK, 128), F32),
        vm((width, feats), BF16), vm((width, ff), BF16), vm((width, ff), BF16), vm((width, 2 * feats), BF16),
        vm((width, feats), F32), vm((width, feats), F32), vm((width, feats), F32), vm((width, ff), F32),
        vm((n_dp,) + sheet, F32), vm((nj,) + sheet, F32), vm((n_dp,) + sheet, F32), vm((nj,) + sheet, F32),
        vm((n_dp, 4, mode_parts[0].shape[0], 128), F32),
        vm((n_dp, 5) + grid, F32), vm((n_dp, chans, 128), F32), vm((nj, 8, 128), F32),
        vm((5,) + grid, F32), vm(sheet, F32), vm(sheet, F32), vm((chans, 128), F32), vm((chans, 128), F32), vm((192, 128), F32),
        vm((18,) + grid, F32),
        vm((rows * PACK, 128), F32), vm((rows * PACK, 128), F32), vm((rows * PACK, 128), F32),
        vm((4, blocks * PACK, 128), F32),
        dma((8, 2)), dma((2, packs)), dma((2, packs)), dma((2, mb)), dma((2, packs)),
    ]
    if direct:
        half = [(r, k // 2) for r, k in per]
        scratch += [vm(f, BF16) for f in full] * 2
        scratch += [vm((4, 2, 2) + p, BF16) for p in per]
        scratch += [vm((4, 2) + p, BF16) for p in half] * 2
        scratch += [vm((4,) + p, BF16) for p in half] * 2
        scratch += [vm((4,) + p, BF16) for p in per]
        scratch += [dma((2, 42)), dma((2, 33))]
    vmem = pl.BlockSpec(memory_space=pltpu.VMEM)
    outs = pl.pallas_call(
        functools.partial(whole_kernel, (nj, chans, mb, h), n_dp, direct),
        out_shape=shapes,
        in_specs=[vmem] * 16,
        out_specs=[vmem] * len(shapes),
        scratch_shapes=scratch,
        compiler_params=pltpu.CompilerParams(collective_id=0, has_side_effects=True, vmem_limit_bytes=62 << 20),
        name="whole",
    )(tokens, cot, lengths, log_step, skip, *mode_parts, *vectors, *weights)
    if direct:
        return deliver(outs)
    outs, grads = outs[:12], outs[12:]
    grads = [lax.psum_scatter(g.reshape(-1, g.shape[-1]).astype(F32), ("dp", "chan"), scatter_dimension=0, tiled=True) for g in grads]
    return deliver(outs) + grads


def deliver_kernel(*refs):
    n = (len(refs) - 1) // 2
    sems = refs[-1]
    copies = [pltpu.make_async_copy(refs[k], refs[n + k], sems.at[k]) for k in range(n)]
    for copy in copies:
        copy.start()
    for copy in copies:
        copy.wait()


def deliver(arrays):
    anywhere = pl.BlockSpec(memory_space=pl.ANY)
    return list(pl.pallas_call(
        deliver_kernel,
        out_shape=[jax.ShapeDtypeStruct(x.shape, x.dtype) for x in arrays],
        in_specs=[pl.BlockSpec(memory_space=pltpu.VMEM)] * len(arrays),
        out_specs=[anywhere] * len(arrays),
        scratch_shapes=[pltpu.SemaphoreType.DMA((len(arrays),))],
        name="deliver",
    )(*arrays))


def on_device(
    tokens, cotangent, lengths, norm_gain, log_step, log_decay, frequency, readout_real, readout_imaginary,
    skip_gain, out_weight, out_bias, ffn_gain, in_weight, in_bias, back_weight,
):
    mb, rows, feats = tokens.shape
    nj, n_dp = lax.axis_size("chan"), lax.axis_size("dp")
    flat_rows = (mb * rows, feats)
    block_out, grad_tokens, g_ls, g_skip, g_ld, g_fr, g_rr, g_ri, g_bo, g_g1, g_g2, g_bi, g_out, g_in, g_back = whole(
        tokens.reshape(flat_rows), cotangent.reshape(flat_rows), lengths.T, log_step.reshape(1, -1), skip_gain.reshape(1, -1),
        [x.T for x in (log_decay, frequency, readout_real, readout_imaginary)],
        [x.reshape(1, -1) for x in (out_bias, norm_gain, ffn_gain, in_bias)],
        (out_weight, in_weight, back_weight), mb, n_dp, nj)
    return (
        block_out.reshape(tokens.shape), grad_tokens.reshape(tokens.shape), g_g1.reshape(-1), g_ls.reshape(-1),
        g_ld.T, g_fr.T, g_rr.T, g_ri.T, g_skip.reshape(-1), g_out, g_bo.reshape(-1), g_g2.reshape(-1), g_in, g_bi.reshape(-1), g_back,
    )


def solution(mesh):
    both = ("dp", "chan")
    rows, row, vec, chan, mode = P(None, both, None), P(both, None), P(both), P("chan"), P("chan", "dp")
    return jax.shard_map(
        on_device, mesh=mesh,
        in_specs=(rows, rows, P(None, "dp"), vec, chan, mode, mode, mode, mode, chan, row, vec, vec, row, vec, row),
        out_specs=(rows, rows, vec, chan, mode, mode, mode, mode, chan, row, vec, vec, row, vec, row),
        check_vma=False,
    )
```

```python
import functools
import jax
import ml_dtypes
import numpy as np
import jax.numpy as jnp
from jax import lax
from jax.experimental import pallas as pl
from jax.experimental.pallas import tpu as pltpu
from jax.sharding import PartitionSpec as P

SPAN = 128
FU = 2
SU = 2
PACK = 16
HI = lax.Precision.HIGHEST


def keep_row(span, i):
    return jnp.where((span & (i * SPAN)) == 0, 0.0, 1.0)


def cmul(ar, ai, br, bi):
    return ar * br - ai * bi, ar * bi + ai * br


def mode_rows(ls, ld, fr, rr, ri):
    dt = jnp.exp(ls)
    a_r = -jnp.exp(ld)
    a_i = fr
    t_r, t_i = dt * a_r, dt * a_i
    mag = jnp.exp(t_r)
    l_r, l_i = mag * jnp.cos(t_i), mag * jnp.sin(t_i)
    mod = a_r * a_r + a_i * a_i
    u_r = l_r - 1.0
    q_r = (u_r * a_r + l_i * a_i) / mod
    q_i = (l_i * a_r - u_r * a_i) / mod
    w_r, w_i = cmul(rr, ri, q_r, q_i)
    return dict(dt=dt, a_r=a_r, a_i=a_i, t_r=t_r, t_i=t_i, l_r=l_r, l_i=l_i, mod=mod,
                q_r=q_r, q_i=q_i, w_r=w_r, w_i=w_i)


def mode_prelude(modes_ref, pw_ref):
    m = mode_rows(modes_ref[0], modes_ref[1], modes_ref[2], modes_ref[3], modes_ref[4])
    r, i = m["l_r"], m["l_i"]
    for k in range(8):
        pw_ref[2 * k] = r
        pw_ref[2 * k + 1] = i
        r, i = cmul(r, i, r, i)
    pw_ref[16] = 2.0 * m["w_r"]
    pw_ref[17] = 2.0 * m["w_i"]


def group_rows(pw_ref, g):
    rows = [pw_ref[k, pl.ds(g, 1), :] for k in range(18)]
    return [jnp.broadcast_to(x, (8, 128)) for x in rows]


def power_table(rows, reverse):
    sub = lax.broadcasted_iota(jnp.int32, (8, 128), 0)
    if reverse:
        sub = 7 - sub
        r, i = jnp.ones((8, 128), jnp.float32), jnp.zeros((8, 128), jnp.float32)
    else:
        r, i = rows[0], rows[1]
    for k in range(3):
        bit = ((sub >> k) & 1) == 1
        fr = jnp.where(bit, rows[2 * k], 1.0)
        fi = jnp.where(bit, rows[2 * k + 1], 0.0)
        r, i = cmul(r, i, fr, fi)
    parts = [(r, i)]
    for k in range(3, 7):
        more = [cmul(a, b, rows[2 * k], rows[2 * k + 1]) for a, b in parts]
        parts = more + parts if reverse else parts + more
    return (jnp.concatenate([p[0] for p in parts], 0), jnp.concatenate([p[1] for p in parts], 0))


def nt(a, b, **kw):
    return lax.dot_general(a, b, (((1,), (1,)), ((), ())), preferred_element_type=jnp.float32, **kw)


def tn(a, b, **kw):
    return lax.dot_general(a, b, (((0,), (0,)), ((), ())), preferred_element_type=jnp.float32, **kw)


def nn(a, b, **kw):
    return jnp.dot(a, b, preferred_element_type=jnp.float32, **kw)


def kernel_rows(rd_r, w_r):
    t = lax.broadcasted_iota(jnp.int32, (SPAN, 128), 0)
    src = jnp.where(t == SPAN - 1, jnp.concatenate([w_r] * 16, 0), rd_r)
    pick = (lax.broadcasted_iota(jnp.int32, (8, 128), 1) // 32
            == lax.broadcasted_iota(jnp.int32, (8, 128), 0)).astype(jnp.float32)
    return pltpu.roll(nt(pick, src, precision=HI), 1, 1)


def toeplitz(row):
    base = pltpu.roll(jnp.broadcast_to(row, (8, 128)), 0, 1, stride=1, stride_axis=0)
    parts = [base] + [pltpu.roll(base, 8 * v, 1) for v in range(1, 16)]
    whole = jnp.concatenate(parts, 0)
    s = lax.broadcasted_iota(jnp.int32, (SPAN, 128), 0)
    t = lax.broadcasted_iota(jnp.int32, (SPAN, 128), 1)
    return jnp.where(t >= s, whole, 0.0).astype(jnp.bfloat16)


def wave_tables():
    angle = 2.0 * np.pi * np.outer(np.arange(SPAN), np.arange(SPAN)) / (2 * SPAN)
    turn = np.cos(np.pi * np.arange(SPAN))
    cosines, sines = np.cos(angle), np.sin(angle)
    there = np.concatenate([cosines, sines], 1)
    there[:, SPAN] = turn
    high = there.astype(ml_dtypes.bfloat16)
    low = (there - high.astype(np.float64)).astype(ml_dtypes.bfloat16)
    back = np.concatenate([2.0 * cosines, -2.0 * sines], 0)
    back[0] = 1.0
    back[SPAN] = turn
    return np.concatenate([high, low], 0), (back / (2 * SPAN)).astype(np.float32)


def lag_sums(xs, gy, rows, there, back):
    step = 8 * PACK
    table = there[...]

    def spectrum(x):
        x = x.astype(jnp.bfloat16)
        return nn(jnp.concatenate([x, x], 1), table)

    def one(n, sums):
        at = pl.ds(pl.multiple_of(n * step, step), step)
        u, g = spectrum(xs[at, :]), spectrum(gy[at, :])
        u_c, u_s, g_c, g_s = u[:, :128], u[:, 128:], g[:, :128], g[:, 128:]
        parts = (u_c * g_c, u_s * g_s, g_c * u_s - g_s * u_c)
        return tuple(x + jnp.sum(p.reshape(8, PACK, 128), axis=0) for x, p in zip(sums, parts))
    even, odd, cross = lax.fori_loop(0, rows // 8, one, (jnp.zeros((PACK, 128), jnp.float32),) * 3)
    ends = lax.broadcasted_iota(jnp.int32, (PACK, 128), 1) == 0
    real = even + jnp.where(ends, 0.0, odd)
    imag = jnp.where(ends, odd, cross)
    return nn(jnp.concatenate([real, imag], 1), back[...], precision=HI)


def lane_owner(rows):
    return lax.broadcasted_iota(jnp.int32, (rows, 128), 1) // 32


def fold(stack, rows):
    width = stack.shape[1]
    own = (lax.broadcasted_iota(jnp.int32, (rows, width), 1) // 32) & 3
    out = stack[:rows]
    for k in range(1, 4):
        out = jnp.where(own == k, stack[k * rows:(k + 1) * rows], out)
    return out


def spread(packed, rows):
    width = packed.shape[1]
    own = (lax.broadcasted_iota(jnp.int32, (rows, width), 1) // 32) & 3
    return jnp.concatenate([jnp.where(own == k, packed, 0.0) for k in range(4)], 0)


def gelu_pair(v):
    half = 0.5 * (1.0 + lax.erf(v * 0.7071067811865476))
    return v * half, half + v * jnp.exp(-0.5 * v * v) * 0.3989422804014327


def block_rows(r):
    return pl.ds(pl.multiple_of(r * PACK, PACK), PACK)


def unpack(src_ref, q, xs, nj, mb, h, blocks, gain):
    def body(j, _):
        for m in range(mb):
            for k in range(h):
                x = src_ref[j, block_rows(q), pl.ds((m * h + k) * 128, 128)]
                xs[block_rows(m * blocks + j * h + k), :] = x.astype(jnp.float32) * gain
        return 0
    lax.fori_loop(0, nj, body, 0)


def rows_of(pw_ref, k, q, mb):
    parts = [jnp.broadcast_to(pw_ref[k, pl.ds(q * 4 + g, 1), :], (mb, 128)) for g in range(4)]
    parts.append(jnp.zeros((PACK - 4 * mb, 128), jnp.float32))
    return jnp.concatenate(parts, 0)


def table_place(store, g, width, first=0):
    per = store.shape[1] // width
    g = g + first
    return store.at[pl.ds(pl.multiple_of(g // per * SPAN, SPAN), SPAN), pl.ds(pl.multiple_of(lax.rem(g, per) * width, width), width)]


def forward_tables(pw_ref, groups, early, toep):
    def one(g, _):
        rws = group_rows(pw_ref, g)
        p_r, p_i = power_table(rws, True)
        back = (SPAN - 1 - lax.broadcasted_iota(jnp.int32, (SPAN, 128), 0)).astype(jnp.float32)
        table_place(early, g, 512)[...] = jnp.concatenate([p_r, p_i, back * p_r, back * p_i], 1).astype(jnp.bfloat16)
        e_r, e_i = power_table(rws, False)
        w_r, w_i = jnp.concatenate([rws[16]] * 16, 0), jnp.concatenate([rws[17]] * 16, 0)
        r_r, r_i = cmul(e_r, e_i, w_r, w_i)
        table_place(early, g, 256, 2 * groups)[...] = jnp.concatenate([r_r, -r_i], 1).astype(jnp.bfloat16)
        krow = kernel_rows(r_r, rws[16])
        for k in range(4):
            toep[4 * g + k] = toeplitz(krow[k:k + 1])
        return 0
    lax.fori_loop(0, groups, one, 0, unroll=2)


def backward_tables(pw_ref, groups, state_tab, read_tab):
    def one(g, _):
        rws = group_rows(pw_ref, g)
        e_r, e_i = power_table(rws, False)
        ahead = (1 + lax.broadcasted_iota(jnp.int32, (SPAN, 128), 0)).astype(jnp.float32)
        state_tab[g] = jnp.concatenate([e_r, e_i, ahead * e_r, ahead * e_i], 1).astype(jnp.bfloat16)
        p_r, p_i = power_table(rws, True)
        w_r, w_i = jnp.concatenate([rws[16]] * 16, 0), jnp.concatenate([rws[17]] * 16, 0)
        r_r, r_i = cmul(p_r, p_i, w_r, w_i)
        read_tab[g] = jnp.concatenate([r_r, -r_i], 1).astype(jnp.bfloat16)
        return 0
    lax.fori_loop(0, groups, one, 0, unroll=2)


def channel_rows(box, c, rows):
    return box[pl.ds(c, rows, stride=PACK), :].astype(jnp.bfloat16)


def put_states(sc, s, g, mb, blocks):
    for a in range(4):
        for m in range(mb):
            sc[a, pl.ds(g * mb + m, blocks, stride=PACK), :] = s[m * blocks:(m + 1) * blocks, a * 128:(a + 1) * 128]


def get_carry(ref, g, mb, blocks):
    return jnp.concatenate([
        jnp.concatenate([ref[a, pl.ds(g * mb + m, blocks, stride=PACK), :] for m in range(mb)], 0) for a in range(2)], 1)


def forward_pack(dims, q, skip_ref, gain_ref, span, early, toep, u_ref, act_ref, slope_ref, carry_ref, pw_ref, xs, ys, sc, poll):
    nj, chans, mb, h = dims
    blocks = nj * h
    rows = mb * blocks
    unpack(u_ref, q, xs, nj, mb, h, blocks, gain_ref[block_rows(q), :])

    def states(g, _):
        x = jnp.concatenate([channel_rows(xs, 4 * g + k, rows) for k in range(4)], 0)
        put_states(sc, fold(nn(x, table_place(early, q * 4 + g, 512)[...]), rows), g, mb, blocks)
        return 0
    lax.fori_loop(0, 4, states, 0, unroll=FU)
    h_r, h_i = rows_of(pw_ref, 14, q, mb), rows_of(pw_ref, 15, q, mb)

    def step(i, c):
        at = block_rows(i)
        keep = keep_row(span, i)
        c = [x * keep for x in c]
        s = [sc[a, at, :] for a in range(4)]
        for a in range(4):
            carry_ref[q, a, at, :] = c[a]
        z_r, z_i = cmul(c[0], c[1], h_r, h_i)
        d_r, d_i = cmul(c[2] + SPAN * c[0], c[3] + SPAN * c[1], h_r, h_i)
        return (z_r + s[0], z_i + s[1], d_r + s[2], d_i + s[3])
    zero = jnp.zeros((PACK, 128), jnp.float32)
    lax.fori_loop(0, blocks, step, (zero,) * 4, unroll=SU)
    poll(f'f{q}a')

    def outputs(g, _):
        c = get_carry(carry_ref.at[q], g, mb, blocks)
        across = nt(spread(c, rows).astype(jnp.bfloat16), table_place(early, q * 4 + g, 256, 2 * (chans // 4))[...])
        for k in range(4):
            y = across[k * rows:(k + 1) * rows] + nn(channel_rows(xs, 4 * g + k, rows), toep[q * PACK + 4 * g + k])
            ys[pl.ds(4 * g + k, rows, stride=PACK), :] = y
        return 0
    lax.fori_loop(0, 4, outputs, 0, unroll=FU)
    poll(f'f{q}b')
    skip = skip_ref[block_rows(q), :]

    def finish(j, _):
        for m in range(mb):
            for k in range(h):
                r = m * blocks + j * h + k
                v = ys[block_rows(r), :] + skip * xs[block_rows(r), :]
                a, d = gelu_pair(v)
                act_ref[j, block_rows(q), pl.ds((m * h + k) * 128, 128)] = a.astype(jnp.bfloat16)
                slope_ref[q, block_rows(r), :] = d
        return 0
    lax.fori_loop(0, nj, finish, 0)


def backward_pack(dims, q, skip_ref, gain_ref, span, state_tab, read_tab, toep, waves, u_ref, ga_ref, slope_ref, carry_ref, gn_ref, zw_ref, ng_ref, pw_ref, xs, gy, gx, sc, lags, poll):
    nj, chans, mb, h = dims
    blocks = nj * h
    rows = mb * blocks
    unpack(u_ref, q, xs, nj, mb, h, blocks, gain_ref[block_rows(q), :])

    def start(j, _):
        for m in range(mb):
            for k in range(h):
                r = m * blocks + j * h + k
                x = ga_ref[j, block_rows(q), pl.ds((m * h + k) * 128, 128)]
                gy[block_rows(r), :] = x.astype(jnp.float32) * slope_ref[q, block_rows(r), :]
        return 0
    lax.fori_loop(0, nj, start, 0)
    lags[...] = lag_sums(xs, gy, rows, *waves)
    poll(f'b{q}a')

    def states(g, _):
        gg = q * 4 + g
        ups = [channel_rows(gy, 4 * g + k, rows) for k in range(4)]
        lag = jnp.concatenate([lags[pl.ds(4 * g, 4), :], jnp.zeros((4, 128), jnp.float32)], 0)
        own8 = lax.broadcasted_iota(jnp.int32, (8, 128), 1) // 32 == lax.broadcasted_iota(jnp.int32, (8, 128), 0)
        lag0 = jnp.sum(jnp.where(own8, jnp.broadcast_to(lag[:, 0:1], (8, 128)), 0.0), axis=0, keepdims=True)
        lane = lax.broadcasted_iota(jnp.int32, (8, 128), 1)
        later = jnp.where(lane == 127, 0.0, pltpu.roll(lag, 127, 1))
        top = later.astype(jnp.bfloat16)
        low = (later - top.astype(jnp.float32)).astype(jnp.bfloat16)
        s = nn(jnp.concatenate(ups + [top, low], 0), state_tab[gg])
        near = s[4 * rows:4 * rows + 8] + s[4 * rows + 8:]
        near = jnp.sum(jnp.where(jnp.concatenate([own8] * 4, 1), near, 0.0), axis=0, keepdims=True)
        zw_ref[0, pl.ds(gg, 1), :] = near[:, 0:128] + lag0
        for a in range(1, 4):
            zw_ref[a, pl.ds(gg, 1), :] = near[:, a * 128:(a + 1) * 128]
        zw_ref[4, pl.ds(gg, 1), :] = lag0
        put_states(sc, fold(s[:4 * rows], rows), g, mb, blocks)
        return 0
    lax.fori_loop(0, 4, states, 0, unroll=FU)
    h_r, h_i = rows_of(pw_ref, 14, q, mb), rows_of(pw_ref, 15, q, mb)

    def step(n, c):
        i = blocks - 1 - n
        at = block_rows(i)
        a_r, a_i, z_r, z_i, w_r, w_i = c
        q_ = [sc[a, at, :] for a in range(4)]
        f = [carry_ref[q, a, at, :] for a in range(4)]
        d = cmul(q_[0], q_[1], f[0], f[1])
        e1 = cmul(q_[2], q_[3], f[0], f[1])
        e2 = cmul(q_[0], q_[1], f[2], f[3])
        sc[0, at, :] = a_r
        sc[1, at, :] = a_i
        keep = keep_row(span, i)
        n_r, n_i = cmul(a_r, a_i, h_r, h_i)
        return ((n_r + q_[0]) * keep, (n_i + q_[1]) * keep, z_r + d[0], z_i + d[1], w_r + e1[0] + e2[0], w_i + e1[1] + e2[1])
    zero = jnp.zeros((PACK, 128), jnp.float32)
    out = lax.fori_loop(0, blocks, step, (zero,) * 6, unroll=SU)
    for a in range(4):
        for g in range(4):
            add = jnp.sum(out[2 + a][g * mb:(g + 1) * mb], axis=0, keepdims=True)
            zw_ref[a, pl.ds(q * 4 + g, 1), :] += add
    poll(f'b{q}b')

    def outputs(g, _):
        across = nt(spread(get_carry(sc, g, mb, blocks), rows).astype(jnp.bfloat16), read_tab[q * 4 + g])
        for k in range(4):
            y = across[k * rows:(k + 1) * rows] + nt(channel_rows(gy, 4 * g + k, rows), toep[q * PACK + 4 * g + k])
            gx[pl.ds(4 * g + k, rows, stride=PACK), :] = y
        return 0
    lax.fori_loop(0, 4, outputs, 0, unroll=FU)
    poll(f'b{q}c')
    skip = skip_ref[block_rows(q), :]

    def finish(j, total):
        for m in range(mb):
            for k in range(h):
                r = m * blocks + j * h + k
                v = (gx[block_rows(r), :] + skip * gy[block_rows(r), :]).astype(jnp.bfloat16)
                cols = pl.ds((m * h + k) * 128, 128)
                gn_ref[j, block_rows(q), cols] = v
                total = total + v.astype(jnp.float32) * u_ref[j, block_rows(q), cols].astype(jnp.float32)
        return total
    ng_ref[block_rows(q), :] = lax.fori_loop(0, nj, finish, jnp.zeros((PACK, 128), jnp.float32))


def mode_gradients(modes, zw):
    m = mode_rows(*modes)
    z_r, z_i, v_r, v_i = zw[0], zw[1], zw[2], zw[3]
    rr, ri = modes[3], modes[4]
    g_rr = 2.0 * (z_r * m["q_r"] - z_i * m["q_i"])
    g_ri = -2.0 * (z_r * m["q_i"] + z_i * m["q_r"])
    k_r, k_i = cmul(rr, ri, m["a_r"] / m["mod"], -m["a_i"] / m["mod"])
    s_r, s_i = cmul(k_r, k_i, m["l_r"], m["l_i"])
    h1 = cmul(z_r, z_i, s_r, s_i)
    h2 = cmul(m["w_r"], m["w_i"], v_r, v_i)
    h_r, h_i = h1[0] + h2[0], h1[1] + h2[1]
    zc = cmul(z_r, z_i, m["w_r"], m["w_i"])
    za = cmul(zc[0], zc[1], m["a_r"] / m["mod"], -m["a_i"] / m["mod"])
    j_r, j_i = h_r * m["dt"] - za[0], h_i * m["dt"] - za[1]
    g_ls = 2.0 * (h_r * m["t_r"] - h_i * m["t_i"])
    return g_ls, 2.0 * m["a_r"] * j_r, -2.0 * j_i, g_rr, g_ri


def keep_rows(lengths, blocks, mb):
    at = jnp.arange(blocks, dtype=jnp.int32)[:, None] * SPAN
    keep = (at % lengths[None, :] != 0).astype(jnp.float32)
    rows = jnp.concatenate([keep] * 4 + [jnp.zeros((blocks, PACK - 4 * mb), jnp.float32)], 1)
    return jnp.broadcast_to(rows[:, :, None], (blocks, PACK, 128))


MESH = pl.DeviceIdType.MESH
F32, BF16 = jnp.float32, jnp.bfloat16


def layer_stats(v):
    average = jnp.mean(v, axis=-1, keepdims=True)
    centred = v - average
    spread = jnp.mean(centred * centred, axis=-1, keepdims=True)
    scale = lax.rsqrt(spread + 1e-05)
    return centred * scale, scale


def layer_back(q, n, scale):
    return scale * (q - jnp.mean(q, axis=-1, keepdims=True) - n * jnp.mean(q * n, axis=-1, keepdims=True))


def column_sum(x):
    return jnp.sum(x, axis=0, keepdims=True)


def peers(count, me):
    return [lax.rem(me + k, count) for k in range(1, count)]


def greet(n_dp, n_chan, d, c):
    barrier = pltpu.get_barrier_semaphore()
    for p in peers(n_dp, d):
        pl.semaphore_signal(barrier, inc=1, device_id=(p, c), device_id_type=MESH)
    for p in peers(n_chan, c):
        pl.semaphore_signal(barrier, inc=1, device_id=(d, p), device_id_type=MESH)


def be_greeted(n_dp, n_chan):
    pl.semaphore_wait(pltpu.get_barrier_semaphore(), n_dp + n_chan - 2)


def send(src, dst, send_sem, recv_sem, to):
    copy = pltpu.make_async_remote_copy(src_ref=src, dst_ref=dst, send_sem=send_sem, recv_sem=recv_sem, device_id=to, device_id_type=MESH)
    copy.start()
    return copy


def settle(whole, send_sem, recv_sem, here):
    pltpu.make_async_remote_copy(src_ref=whole, dst_ref=whole, send_sem=send_sem, recv_sem=recv_sem, device_id=here, device_id_type=MESH).wait()


class Exchange:
    def __init__(self, box, sems, count, me, to, here):
        self.box, self.sems, self.count, self.me, self.to, self.here = box, sems, count, me, to, here

    def start(self):
        for p in peers(self.count, self.me):
            send(self.box.at[self.me], self.box.at[self.me], self.sems.at[0], self.sems.at[1], self.to(p))

    def wait(self):
        settle(self.box.at[pl.ds(0, self.count - 1)], self.sems.at[0], self.sems.at[1], self.here)

    def total(self):
        return sum(self.box[k] for k in range(self.count))


class Copies:
    def __init__(self, sems):
        self.sems = sems
        self.used = 0
        self.unsent = []

    def put(self, src, dst, to):
        n = self.used
        self.used += 1
        copy = send(src, dst, self.sems.at[0, n], self.sems.at[1, n], to)
        self.unsent.append(copy)
        return copy

    def finish(self):
        for copy in self.unsent:
            copy.wait_send()


def arrive(copies):
    for copy in copies:
        copy.wait_recv()


class Place:
    def __init__(self, d, c):
        self.d, self.c = d, c
        self.a, self.b, self.core = c // 4, lax.rem(c // 2, 2), lax.rem(c, 2)

    def at(self, a, b, core):
        return (self.d, a * 4 + b * 2 + core)

    @property
    def over_a(self):
        return self.at(1 - self.a, self.b, self.core)

    @property
    def over_b(self):
        return self.at(self.a, 1 - self.b, self.core)

    @property
    def twin(self):
        return self.at(self.a, self.b, 1 - self.core)


class Part:
    def __init__(self, rows, low, high):
        self.rows, self.low, self.high = rows, low, high
        self.all = pl.ds(low.start, low.size + high.size)


def parts_of(w_out, w_in, w_back):
    def cut(w, rows, first, cols):
        return Part(rows, pl.ds(first, cols // 2), pl.ds(first + cols // 2, cols // 2))
    r, k = w_out.shape[-2:]
    some = [(0, cut(w_out, pl.ds(0, r), 0, k))]
    r, k = w_in.shape[-2:]
    some += [(1, cut(w_in, pl.ds(0, r), n * (k // 2), k // 2)) for n in range(2)]
    r, k = w_back.shape[-2:]
    some += [(2, cut(w_back, pl.ds(n * (r // 2), r // 2), 0, k)) for n in range(2)]
    return some


class Gather:
    def __init__(self, w, part, dp_first, copies, here, n_dp):
        self.w, self.part, self.copies, self.here, self.n_dp = w, part, copies, here, n_dp
        self.step, self.side, self.at = [], [], 0
        self.stages = [self.dp_first, self.hop] if dp_first else [self.first, self.dp_second]
        self.stages += [self.last, self.twin, self.done]

    def advance(self):
        self.stages[self.at]()
        self.at += 1

    def same(self, ref, to):
        return self.copies.put(ref, ref, to)

    def low(self, d, a, b, core):
        return self.w.at[d, a, b, core, self.part.rows, self.part.low]

    def high(self, d, a, b, core):
        return self.w.at[d, a, b, core, self.part.rows, self.part.high]

    def first(self):
        i = self.here
        self.step = [self.same(self.low(i.d, i.a, i.b, i.core), i.over_b), self.same(self.high(i.d, i.a, i.b, i.core), i.over_a)]

    def dp_second(self):
        i = self.here
        arrive(self.step)
        self.step = []
        for p in peers(self.n_dp, i.d):
            self.step.append(self.same(self.low(i.d, i.a, slice(None), i.core), (p, i.c)))
            self.step.append(self.same(self.high(i.d, slice(None), i.b, i.core), (p, i.c)))

    def dp_first(self):
        i = self.here
        own = self.w.at[i.d, i.a, i.b, i.core, self.part.rows, self.part.all]
        self.step = [self.same(own, (p, i.c)) for p in peers(self.n_dp, i.d)]

    def hop(self):
        i, every = self.here, slice(None)
        arrive(self.step)
        self.step = [self.same(self.low(every, i.a, i.b, i.core), i.over_b), self.same(self.high(every, i.a, i.b, i.core), i.over_a)]

    def last(self):
        i, every = self.here, slice(None)
        arrive(self.step)
        low, high = self.low(every, i.a, every, i.core), self.high(every, every, i.b, i.core)
        self.step = [self.same(low, i.over_a), self.same(high, i.over_b)]
        self.side = [self.same(low, i.twin), self.same(high, i.twin)]

    def twin(self):
        i, every = self.here, slice(None)
        arrive(self.step)
        self.side += [self.same(self.low(every, 1 - i.a, every, i.core), i.twin), self.same(self.high(every, every, 1 - i.b, i.core), i.twin)]

    def done(self):
        arrive(self.side)


class Scatter:
    def __init__(self, g, part, dp_last, boxes, out, copies, here, n_dp):
        self.g, self.part, self.out, self.copies, self.here, self.n_dp = g, part, out, copies, here, n_dp
        self.box, self.low_box, self.high_box, *self.more = boxes
        self.step, self.at = [], 0
        self.stages = [self.to_twin, self.add_twin]
        self.stages += [self.hop, self.dp_last, self.done_last] if dp_last else [self.dp, self.hop_last, self.done]

    def advance(self):
        self.stages[self.at]()
        self.at += 1

    def put(self, src, dst, to):
        self.step.append(self.copies.put(src, dst, to))

    def arrived(self):
        arrive(self.step)
        self.step = []

    def to_twin(self):
        i, every = self.here, slice(None)
        self.put(self.g.at[every, every, every, 1 - i.core, self.part.rows, self.part.all], self.box, i.twin)

    def add_twin(self):
        i, part, box = self.here, self.part, self.box
        self.arrived()
        half = box.shape[-1] // 2

        def add(n, _):
            for a in range(2):
                for b in range(2):
                    own = self.g[n, a, b, i.core, part.rows, part.all]
                    box[n, a, b] = (box[n, a, b].astype(F32) + own.astype(F32)).astype(BF16)
            return 0
        lax.fori_loop(0, box.shape[0], add, 0)
        self.put(box.at[:, 1 - i.a, :, :, pl.ds(0, half)], self.low_box, i.over_a)
        self.put(box.at[:, :, 1 - i.b, :, pl.ds(half, half)], self.high_box, i.over_b)

    def add_hop(self):
        i, box, low_box, high_box = self.here, self.box, self.low_box, self.high_box
        self.arrived()
        half = box.shape[-1] // 2

        def add(n, _):
            for k in range(2):
                low_box[n, k] = (low_box[n, k].astype(F32) + box[n, i.a, k, :, :half].astype(F32)).astype(BF16)
                high_box[n, k] = (high_box[n, k].astype(F32) + box[n, k, i.b, :, half:].astype(F32)).astype(BF16)
            return 0
        lax.fori_loop(0, box.shape[0], add, 0)

    def hop(self):
        i = self.here
        low2, high2, _low3, _high3 = self.more
        self.add_hop()
        self.put(self.low_box.at[:, 1 - i.b], low2, i.over_b)
        self.put(self.high_box.at[:, 1 - i.a], high2, i.over_a)

    def dp_last(self):
        i = self.here
        low2, high2, low3, high3 = self.more
        self.arrived()
        for n in range(self.n_dp):
            low2[n] = (low2[n].astype(F32) + self.low_box[n, i.b].astype(F32)).astype(BF16)
            high2[n] = (high2[n].astype(F32) + self.high_box[n, i.a].astype(F32)).astype(BF16)
        for p in peers(self.n_dp, i.d):
            self.put(low2.at[p], low3.at[i.d], (p, i.c))
            self.put(high2.at[p], high3.at[i.d], (p, i.c))

    def done_last(self):
        i = self.here
        low2, high2, low3, high3 = self.more
        self.arrived()
        for own, box, cols in ((low2, low3, self.part.low), (high2, high3, self.part.high)):
            total = own[i.d].astype(F32)
            for p in peers(self.n_dp, i.d):
                total = total + box[p].astype(F32)
            self.out[self.part.rows, cols] = total

    def dp(self):
        i = self.here
        low2, high2, _low3, _high3 = self.more
        self.add_hop()
        for p in peers(self.n_dp, i.d):
            self.put(self.low_box.at[p], low2.at[i.d], (p, i.c))
            self.put(self.high_box.at[p], high2.at[i.d], (p, i.c))

    def hop_last(self):
        i = self.here
        low2, high2, low3, high3 = self.more
        self.arrived()
        for first, box, other, own, cols, to in (
            (self.low_box, low2, low3, i.b, self.part.low, i.over_b), (self.high_box, high2, high3, i.a, self.part.high, i.over_a),
        ):
            def total(k):
                x = first[i.d, k].astype(F32)
                for p in peers(self.n_dp, i.d):
                    x = x + box[p, k].astype(F32)
                return x
            self.out[self.part.rows, cols] = total(own)
            other[0] = total(1 - own).astype(BF16)
            self.put(other.at[0], other.at[1], to)

    def done(self):
        _low2, _high2, low3, high3 = self.more
        self.arrived()
        for box, cols in ((low3, self.part.low), (high3, self.part.high)):
            self.out[self.part.rows, cols] += box[1].astype(F32)


def scatter_boxes(size, dp_last):
    r, k = size
    half = (r, k // 2)
    boxes = [(4, 2, 2, r, k), (4, 2) + half, (4, 2) + half]
    return boxes + ([(4,) + half] * 4 if dp_last else [(4, 2) + half] * 2 + [(2,) + half] * 2)


def wide(vec_ref, first, count):
    return jnp.concatenate([vec_ref[first + k:first + k + 1, :] for k in range(count)], 1)


def add_wide(vec_ref, first, row):
    for k in range(row.shape[1] // 128):
        vec_ref[first + k:first + k + 1, :] += row[:, k * 128:(k + 1) * 128]


def put_own(vec_ref, first, own, shard, shards):
    size = own.shape[1]
    rows = size * shards // 128
    while own.shape[1] < 128:
        own = jnp.concatenate([own, own], 1)
    index = 128 * lax.broadcasted_iota(jnp.int32, (rows, 128), 0) + lax.broadcasted_iota(jnp.int32, (rows, 128), 1)
    inside = (index >= shard * size) & (index < (shard + 1) * size)
    vec_ref[first:first + rows, :] = jnp.where(inside, jnp.broadcast_to(own, (rows, 128)), 0.0)


def pick_own(vec_ref, first, size, shard):
    start = shard * size
    row = vec_ref[pl.ds(first + start // 128, 1), :]
    row = pltpu.roll(jnp.broadcast_to(row, (8, 128)), lax.rem(128 - lax.rem(start, 128), 128), 1)
    return row[0:1, :size]


def to_column(row):
    return jnp.broadcast_to(row, (128, row.shape[1])).T


def padded(x, lanes=128):
    if x.shape[1] == lanes:
        return x
    return jnp.concatenate([x, jnp.zeros((x.shape[0], lanes - x.shape[1]), x.dtype)], 1)


def lane_pick(groups, k):
    lane = lax.broadcasted_iota(jnp.int32, (groups, 128), 1)
    return (lane == 4 * lax.broadcasted_iota(jnp.int32, (groups, 128), 0) + k).astype(F32)


def spread_modes(rows, modes):
    groups = modes.shape[1]
    for k in range(4):
        part = nt(lane_pick(groups, k), rows, precision=HI)
        for a in range(modes.shape[0]):
            modes[a, :, k * 32:(k + 1) * 32] = part[:, a * 32:(a + 1) * 32]


def collect_modes(arrays):
    groups = arrays[0].shape[0]
    total = None
    for k in range(4):
        part = jnp.concatenate([x[:, k * 32:(k + 1) * 32] for x in arrays], 1)
        part = tn(part, lane_pick(groups, k), precision=HI)
        total = part if total is None else total + part
    return total


def flat(x):
    return x.reshape(-1, x.shape[-1])


def row_block(m, t):
    return pl.ds(pl.multiple_of(m * t, t), t)


def dense_up(m, t, tokens, act, w_out, w_in, vec, keeps):
    middle, gate_ref, gated_ref, second, _hidden, _slopes = keeps
    at = row_block(m, t)
    feats = tokens.shape[1]
    project = tn(act[:, :, at].reshape(feats, t), flat(w_out[...])) + wide(vec, 0, 2 * feats // 128)
    gate = jax.nn.sigmoid(project[:, feats:])
    gated = project[:, :feats] * gate
    total = tokens[at, :].astype(F32) + gated
    gate_ref[at, :] = gate
    gated_ref[at, :] = gated
    middle[at, :] = total
    n, _scale = layer_stats(total)
    after = (n * wide(vec, 12, feats // 128)).astype(BF16)
    second[at, :] = after
    dense_hidden(m, t, (0, 1), w_in, vec, keeps)


def dense_hidden(m, t, tiles, w_in, vec, keeps):
    _middle, _gate_ref, _gated_ref, second, hidden, slopes = keeps
    at = row_block(m, t)
    tile = w_in.shape[-1] // 4
    after = second[at, :]
    for f in tiles:
        cols = slice(f * tile, (f + 1) * tile)
        before = nn(after, flat(w_in[:, :, :, :, :, cols])) + wide(vec, 16 + f * tile // 128, tile // 128)
        high, slope = gelu_pair(before)
        hidden[at, cols] = high.astype(BF16)
        slopes[at, cols] = slope


def dense_down(m, t, cot, wholes, vec, block_out, keeps, gb, gp, snd, sums):
    w_out, w_in, w_back = wholes
    middle, gate_ref, gated_ref, second, hidden, slopes = keeps
    at = row_block(m, t)
    feats = cot.shape[1]
    tile = w_in.shape[-1] // 4
    up = cot[at, :]
    total = middle[at, :]
    n, scale = layer_stats(total)
    gain = wide(vec, 12, feats // 128)
    back = jnp.zeros((t, feats), F32)
    for f in range(4):
        cols = slice(f * tile, (f + 1) * tile)
        wb = flat(w_back[f])
        low = (slopes[at, cols] * nt(up, wb)).astype(BF16)
        gb[at, cols] = low
        add_wide(sums, 16 + f * tile // 128, column_sum(low.astype(F32)))
        total = total + nn(hidden[at, cols], wb)
        back = back + nt(low, flat(w_in[:, :, :, :, :, cols]))
    block_out[at, :] = total.astype(BF16)
    add_wide(sums, 12, column_sum(back * n))
    grad = up.astype(F32) + layer_back(back * gain, n, scale)
    middle[at, :] = grad
    gate = gate_ref[at, :]
    first = (grad * gate).astype(BF16)
    last = (grad * gated_ref[at, :] * (1.0 - gate)).astype(BF16)
    gp[at, :feats] = first
    gp[at, feats:] = last
    add_wide(sums, 0, column_sum(first.astype(F32)))
    add_wide(sums, feats // 128, column_sum(last.astype(F32)))
    both = jnp.concatenate([first, last], 1)
    snd[:, :, at] = nt(flat(w_out[...]), both).astype(BF16).reshape(snd.shape[:2] + (t,))


def shaped(x, g):
    return x.astype(BF16).reshape(g.shape[1:])


def outer_products(left, right, g):
    size = left.shape[1] // 4
    def one(n, _):
        g[n] = shaped(tn(left[:, row_block(n, size)], right[...]), g)
        return 0
    lax.fori_loop(0, 4, one, 0)


PART_NAMES = ("o", "i", "j", "b", "c")
GATHER_DP_FIRST = (False, False, False, False, True)
SCATTER_DP_LAST = (True, False, True, False, False)
SCHEDULE = {
    "greeted": "gc go gi gj gb",
    "sent": "go gi gc",
    "tables": "go gj",
    "f0c": "gb",
    "f1b": "gi",
    "f1c": "go",
    "f3c": "gj gc gi",
    "act": "go gi",
    "up0": "gb",
    "up2": "gj gj",
    "hid1": "gc",
    "g_back": "sb sc gb gc gb",
    "pre0": "sb sc",
    "g_in": "si sj sb",
    "g_out": "so sc si sj so",
    "b0d": "si sb sc",
    "b1a": "sj",
    "b1d": "so",
    "b2d": "sj si",
    "b3b": "so",
    "tail": "sb sc si",
    "rows": "sj so",
}


def whole_kernel(dims, n_dp, direct, *refs):
    nj, chans, mb, h = dims
    refs = list(refs)
    def take(n):
        out = refs[:n]
        del refs[:n]
        return out
    tokens_in, cot_in, lengths, log_step, skip_row, *mode_parts = take(9)
    vectors = take(4)
    waves = take(2)
    given = take(3)
    block_out_to, grad_tokens_to = take(2)
    g_step, g_skip, *g_modes = take(6)
    g_vectors = take(4)
    results_to = take(3)
    tokens, cot, block_out, grad_tokens = take(4)
    u, snd, act, out, ga, gn, slope, carry = take(8)
    second, hidden, gb, gp = take(4)
    keeps = take(4)
    middle = keeps[0]
    keeps = keeps[:3] + [second, hidden] + keeps[3:]
    vec_dp, vec_chan, vec2_dp, vec2_chan, modes_dp, zw_dp, ng_dp, ng_chan = take(8)
    modes, vec, sums, skip, gain, mode_rows_box = take(6)
    pw, xs, ys, gy, sc, lags, toep, state_tab, read_tab = take(9)
    box_sems, in_sems, out_sems, back_sems, gn_sems, own_sems = take(6)
    d, c = lax.axis_index("dp"), lax.axis_index("chan")
    here = (d, c)
    shards, shard = n_dp * nj, d * nj + c
    packs = chans // PACK
    groups = modes.shape[1]
    width = tokens.shape[0]
    t = width // mb
    feats = nj * chans
    over_dp, over_chan = (lambda p: (p, c)), (lambda p: (d, p))

    def along_dp(box, n):
        return Exchange(box, box_sems.at[n], n_dp, d, over_dp, here)

    def along_chan(box, n):
        return Exchange(box, box_sems.at[n], nj, c, over_chan, here)
    vec_first, vec_second = along_dp(vec_dp, 0), along_chan(vec_chan, 1)
    modes_all = along_dp(modes_dp, 2)
    sums_first, sums_second = along_chan(vec2_chan, 3), along_dp(vec2_dp, 4)
    zw_all, ng_first, ng_second = along_dp(zw_dp, 5), along_dp(ng_dp, 6), along_chan(ng_chan, 7)
    if direct:
        wholes, grads = take(3), take(3)
        results = take(3)
        places = parts_of(*wholes)
        boxes = [take(7) for _ in places]
        place = Place(d, c)
        gather_copies, scatter_copies = Copies(refs[0]), Copies(refs[1])
        parts = {}
        for (k, part), dp_first, dp_last, name, each in zip(places, GATHER_DP_FIRST, SCATTER_DP_LAST, PART_NAMES, boxes):
            parts["g" + name] = Gather(wholes[k], part, dp_first, gather_copies, place, n_dp)
            parts["s" + name] = Scatter(grads[k], part, dp_last, each, results[k], scatter_copies, place, n_dp)
    else:
        wholes, grads = given, results_to
    g_out, g_in, g_back = grads

    def poll(point):
        if direct:
            for name in SCHEDULE.get(point, "").split():
                parts[name].advance()

    def fetch(src, dst, n):
        copy = pltpu.make_async_copy(src, dst, own_sems.at[n])
        copy.start()
        return copy
    fetched = [fetch(tokens_in, tokens, 0)]
    if direct:
        fetched += [fetch(own, w.at[d, place.a, place.b, place.core], 2 + k) for k, (own, w) in enumerate(zip(given, wholes))]
    fetched.append(fetch(cot_in, cot, 1))

    for k, (own, first) in enumerate(zip(vectors, (0, 8, 12, 16))):
        put_own(vec_dp.at[d], first, own[...].astype(F32), shard, shards)
    for a in range(4):
        modes_dp[d, a] = padded(mode_parts[a][...])
    greet(n_dp, nj, d, c)
    fetched[0].wait()

    def normalize(m, _):
        at = row_block(m, t)
        n, _scale = layer_stats(tokens[at, :].astype(F32))
        snd[:, :, at] = n.T.astype(BF16).reshape(nj, chans, t)
        return 0
    lax.fori_loop(0, mb, normalize, 0)
    be_greeted(n_dp, nj)
    vec_first.start()
    modes_all.start()
    if direct:
        for copy in fetched[1:4]:
            copy.wait()
    poll("greeted")

    def share(box, where, sems, q):
        for p in peers(nj, c):
            send(box.at[p, block_rows(q)], where.at[c, block_rows(q)], sems.at[0, q], sems.at[1, q], (d, p))
        where[c, block_rows(q), :] = box[c, block_rows(q), :]

    def shared(where, sems, q):
        settle(where.at[pl.ds(0, nj - 1), block_rows(q)], sems.at[0, q], sems.at[1, q], here)

    for q in range(packs):
        share(snd, u, in_sems, q)
    poll("sent")
    sums[...] = jnp.zeros(sums.shape, F32)
    sc[...] = jnp.zeros(sc.shape, F32)
    skip[...] = to_column(skip_row[...])
    long = lengths[...] - 1
    row = lax.broadcasted_iota(jnp.int32, (PACK, 128), 0)
    span = jnp.zeros((PACK, 128), jnp.int32)
    for m in range(mb):
        span = jnp.where(lax.rem(row, mb) == m, jnp.broadcast_to(long[:, m:m + 1], (PACK, 128)), span)
    vec_first.wait()
    vec_chan[c] = vec_first.total()
    vec_second.start()
    modes_all.wait()
    kinds = [jnp.broadcast_to(padded(log_step[...]), (32, 128))]
    kinds += [jnp.concatenate([modes_dp[p, a] for p in range(n_dp)], 0) for a in range(4)]
    spread_modes(jnp.concatenate(kinds, 0), modes)
    mode_prelude(modes, pw)
    forward_tables(pw, groups, gb, toep)
    poll("tables")
    backward_tables(pw, groups, state_tab, read_tab)
    vec_second.wait()
    vec[...] = vec_second.total()
    for k in range(nj):
        @pl.when(c == k)
        def _():
            first = k * chans
            row = vec[8 + first // 128:9 + first // 128, :]
            gain[...] = to_column(row[:, first % 128:first % 128 + chans])

    for q in range(packs):
        shared(u, in_sems, q)
        forward_pack(dims, q, skip, gain, span, gb, toep, u, out, slope, carry, pw, xs, ys, sc, poll)
        share(out, act, out_sems, q)
        poll(f'f{q}c')
    for q in range(packs):
        shared(act, out_sems, q)
    poll("act")
    for m in range(mb):
        dense_up(m, t, tokens, act, wholes[0], wholes[1], vec, keeps)
        poll(f"up{m}")
    for m in range(mb):
        dense_hidden(m, t, (2, 3), wholes[1], vec, keeps)
        poll(f"hid{m}")
    fetched[-1].wait()
    outer_products(hidden, cot, g_back)
    poll("g_back")
    for m in range(mb):
        dense_down(m, t, cot, wholes, vec, block_out, keeps, gb, gp, snd, sums)
        poll(f"pre{m}")
        at = pl.ds(m * t, t)
        for p in peers(nj, c):
            send(snd.at[p, :, at], ga.at[c, :, at], back_sems.at[0, m], back_sems.at[1, m], (d, p))
        ga[c, :, at] = snd[c, :, at]
        poll(f"down{m}")
    written = [fetch(block_out, block_out_to, 5)]
    vec2_chan[c] = sums[...]
    sums_first.start()
    outer_products(second, gb, g_in)
    poll("g_in")
    def outer(n, _):
        g_out[n] = shaped(nn(flat(act[pl.ds(n * (nj // 4), nj // 4)]), gp[...]), g_out)
        return 0
    lax.fori_loop(0, 4, outer, 0)
    poll("g_out")
    for m in range(mb):
        settle(ga.at[pl.ds(0, nj - 1), :, pl.ds(m * t, t)], back_sems.at[0, m], back_sems.at[1, m], here)
    poll("ga")
    for q in range(packs):
        backward_pack(dims, q, skip, gain, span, state_tab, read_tab, toep, waves, u, ga, slope, carry, out, zw_dp.at[d], ng_dp.at[d], pw, xs, gy, ys, sc, lags, poll)
        share(out, gn, gn_sems, q)
        poll(f'b{q}d')
        if q == packs // 2:
            sums_first.wait()
            vec2_dp[d] = sums_first.total()
            sums_second.start()
    zw_all.start()
    ng_first.start()
    for q in range(packs):
        shared(gn, gn_sems, q)
    poll("tail")
    wide_gain = wide(vec, 8, feats // 128)
    for m in range(mb):
        at = row_block(m, t)
        n, scale = layer_stats(tokens[at, :].astype(F32))
        grad = gn[:, :, at].reshape(feats, t).astype(F32).T
        grad_tokens[at, :] = (middle[at, :] + layer_back(grad * wide_gain, n, scale)).astype(BF16)
        if m == 0:
            ng_first.wait()
            ng_chan[c, 0:1, :] = padded(column_sum(ng_first.total().T))
            ng_chan[c, 1:8, :] = jnp.zeros((7, 128), F32)
            ng_second.start()
    written.append(fetch(grad_tokens, grad_tokens_to, 6))
    zw_all.wait()
    zw = [sum(zw_dp[k, a] for k in range(n_dp)) for a in range(5)]
    found = list(mode_gradients([modes[a] for a in range(5)], zw)) + [zw[4]]
    mode_rows_box[...] = collect_modes(found)
    g_step[...] = column_sum(mode_rows_box[0:32, :])[:, :chans]
    g_skip[...] = mode_rows_box[160:161, :chans]
    for a in range(4):
        each = g_modes[a].shape[0]
        g_modes[a][...] = mode_rows_box[pl.ds(32 * (a + 1) + d * each, each), :chans]
    sums_second.wait()
    sums[...] = sums_second.total()
    for k, (first, own) in enumerate(zip((0, 8, 12, 16), g_vectors)):
        if k != 1:
            own[...] = pick_own(sums, first, own.shape[1], shard)
    poll("rows")
    if direct:
        written += [fetch(x, to, 7 + k) for k, (x, to) in enumerate(zip(results, results_to))]
    ng_second.wait()
    size = g_vectors[1].shape[1]
    start = shard * size
    row = ng_chan[start // chans]
    g_vectors[1][...] = pltpu.roll(row, lax.rem(128 - lax.rem(start, chans), 128), 1)[0:1, :size]
    if direct:
        gather_copies.finish()
        scatter_copies.finish()
        assert all(x.at == len(x.stages) for x in parts.values())
    for copy in written:
        copy.wait()


def whole(tokens, cot, lengths, log_step, skip, mode_parts, vectors, weights, mb, n_dp, nj):
    width, feats = tokens.shape
    chans = feats // nj
    t = width // mb
    h = t // SPAN
    blocks = nj * h
    rows = mb * blocks
    packs = chans // PACK
    groups = chans // 4
    direct = nj == 8 and n_dp == 4 and packs == 4 and all(w.shape[0] % 16 == 0 for w in weights)
    if not direct:
        weights = [lax.all_gather(w, ("dp", "chan"), axis=0, tiled=True) for w in weights]
        weights = [w.reshape(4, 2, 2, 2, -1, w.shape[1]) for w in weights]
    per = [w.shape[-2:] for w in weights]
    full = [(4, 2, 2, 2) + p for p in per]
    ff = per[1][1]
    shape = jax.ShapeDtypeStruct
    shapes = [shape((width, feats), BF16)] * 2 + [shape((1, chans), F32)] * 2
    shapes += [shape(x.shape, F32) for x in mode_parts] + [shape(x.shape, F32) for x in vectors]
    shapes += [shape(p, F32) for p in per] if direct else [shape(f, BF16) for f in full]
    dma, vm = pltpu.SemaphoreType.DMA, pltpu.VMEM
    sheet, grid = (32, 128), (groups, 128)
    scratch = [vm((width, feats), BF16)] * 4 + [vm((nj, chans, width), BF16)] * 6 + [
        vm((packs, rows * PACK, 128), F32),
        vm((packs, 4, blocks * PACK, 128), F32),
        vm((width, feats), BF16), vm((width, ff), BF16), vm((width, ff), BF16), vm((width, 2 * feats), BF16),
        vm((width, feats), F32), vm((width, feats), F32), vm((width, feats), F32), vm((width, ff), F32),
        vm((n_dp,) + sheet, F32), vm((nj,) + sheet, F32), vm((n_dp,) + sheet, F32), vm((nj,) + sheet, F32),
        vm((n_dp, 4, mode_parts[0].shape[0], 128), F32),
        vm((n_dp, 5) + grid, F32), vm((n_dp, chans, 128), F32), vm((nj, 8, 128), F32),
        vm((5,) + grid, F32), vm(sheet, F32), vm(sheet, F32), vm((chans, 128), F32), vm((chans, 128), F32), vm((192, 128), F32),
        vm((18,) + grid, F32),
        vm((rows * PACK, 128), F32), vm((rows * PACK, 128), F32), vm((rows * PACK, 128), F32),
        vm((4, blocks * PACK, 128), F32),
        vm((PACK, 128), F32), vm((chans, SPAN, 128), BF16), vm((groups, SPAN, 512), BF16), vm((groups, SPAN, 256), BF16),
        dma((8, 2)), dma((2, packs)), dma((2, packs)), dma((2, mb)), dma((2, packs)), dma((10,)),
    ]
    if direct:
        scratch += [vm(f, BF16) for f in full] * 2 + [vm(p, F32) for p in per]
        (r0, k0), (r1, k1), (r2, k2) = per
        sizes = [(r0, k0), (r1, k1 // 2), (r1, k1 // 2), (r2 // 2, k2), (r2 // 2, k2)]
        for size, dp_last in zip(sizes, SCATTER_DP_LAST):
            scratch += [vm(x, BF16) for x in scatter_boxes(size, dp_last)]
        scratch += [dma((2, 70)), dma((2, 55))]
    vmem, anywhere = pl.BlockSpec(memory_space=pltpu.VMEM), pl.BlockSpec(memory_space=pl.ANY)
    outs = pl.pallas_call(
        functools.partial(whole_kernel, (nj, chans, mb, h), n_dp, direct),
        out_shape=shapes,
        in_specs=[anywhere] * 2 + [vmem] * 13 + [anywhere if direct else vmem] * 3,
        out_specs=[anywhere] * 2 + [vmem] * 10 + [anywhere if direct else vmem] * 3,
        scratch_shapes=scratch,
        compiler_params=pltpu.CompilerParams(collective_id=0, has_side_effects=True, vmem_limit_bytes=63 << 20),
        name="whole",
    )(tokens, cot, lengths, log_step, skip, *mode_parts, *vectors, *(jnp.asarray(x) for x in wave_tables()), *weights)
    if direct:
        return deliver(outs)
    outs, grads = outs[:12], outs[12:]
    grads = [lax.psum_scatter(g.reshape(-1, g.shape[-1]).astype(F32), ("dp", "chan"), scatter_dimension=0, tiled=True) for g in grads]
    return deliver(outs) + grads


def deliver_kernel(*refs):
    n = (len(refs) - 1) // 3
    sems = refs[-1]
    first = [pltpu.make_async_copy(refs[k], refs[2 * n + k], sems.at[0, k]) for k in range(n)]
    last = [pltpu.make_async_copy(refs[2 * n + k], refs[n + k], sems.at[1, k]) for k in range(n)]
    for copy in first:
        copy.start()
    for one, two in zip(first[::-1], last[::-1]):
        one.wait()
        two.start()
    for copy in last:
        copy.wait()


def deliver(arrays):
    anywhere = pl.BlockSpec(memory_space=pl.ANY)
    return list(pl.pallas_call(
        deliver_kernel,
        out_shape=[jax.ShapeDtypeStruct(x.shape, x.dtype) for x in arrays],
        in_specs=[anywhere] * len(arrays),
        out_specs=[anywhere] * len(arrays),
        scratch_shapes=[pltpu.VMEM(x.shape, x.dtype) for x in arrays] + [pltpu.SemaphoreType.DMA((2, len(arrays)))],
        name="deliver",
    )(*arrays))


def on_device(
    tokens, cotangent, lengths, norm_gain, log_step, log_decay, frequency, readout_real, readout_imaginary,
    skip_gain, out_weight, out_bias, ffn_gain, in_weight, in_bias, back_weight,
):
    mb, rows, feats = tokens.shape
    nj, n_dp = lax.axis_size("chan"), lax.axis_size("dp")
    flat_rows = (mb * rows, feats)
    block_out, grad_tokens, g_ls, g_skip, g_ld, g_fr, g_rr, g_ri, g_bo, g_g1, g_g2, g_bi, g_out, g_in, g_back = whole(
        tokens.reshape(flat_rows), cotangent.reshape(flat_rows), lengths.T, log_step.reshape(1, -1), skip_gain.reshape(1, -1),
        [x.T for x in (log_decay, frequency, readout_real, readout_imaginary)],
        [x.reshape(1, -1) for x in (out_bias, norm_gain, ffn_gain, in_bias)],
        (out_weight, in_weight, back_weight), mb, n_dp, nj)
    return (
        block_out.reshape(tokens.shape), grad_tokens.reshape(tokens.shape), g_g1.reshape(-1), g_ls.reshape(-1),
        g_ld.T, g_fr.T, g_rr.T, g_ri.T, g_skip.reshape(-1), g_out, g_bo.reshape(-1), g_g2.reshape(-1), g_in, g_bi.reshape(-1), g_back,
    )


def solution(mesh):
    both = ("dp", "chan")
    rows, row, vec, chan, mode = P(None, both, None), P(both, None), P(both), P("chan"), P("chan", "dp")
    return jax.shard_map(
        on_device, mesh=mesh,
        in_specs=(rows, rows, P(None, "dp"), vec, chan, mode, mode, mode, mode, chan, row, vec, vec, row, vec, row),
        out_specs=(rows, rows, vec, chan, mode, mode, mode, mode, chan, row, vec, vec, row, vec, row),
        check_vma=False,
    )
```

```python
import functools
import jax
import ml_dtypes
import numpy as np
import jax.numpy as jnp
from jax import lax
from jax.experimental import pallas as pl
from jax.experimental.pallas import tpu as pltpu
from jax.sharding import PartitionSpec as P

SPAN = 128
FU = 2
SU = 2
PACK = 16
HI = lax.Precision.HIGHEST


def keep_row(span, i):
    return jnp.where((span & (i * SPAN)) == 0, 0.0, 1.0)


def cmul(ar, ai, br, bi):
    return ar * br - ai * bi, ar * bi + ai * br


def mode_rows(ls, ld, fr, rr, ri):
    dt = jnp.exp(ls)
    a_r = -jnp.exp(ld)
    a_i = fr
    t_r, t_i = dt * a_r, dt * a_i
    mag = jnp.exp(t_r)
    l_r, l_i = mag * jnp.cos(t_i), mag * jnp.sin(t_i)
    mod = a_r * a_r + a_i * a_i
    u_r = l_r - 1.0
    q_r = (u_r * a_r + l_i * a_i) / mod
    q_i = (l_i * a_r - u_r * a_i) / mod
    w_r, w_i = cmul(rr, ri, q_r, q_i)
    return dict(dt=dt, a_r=a_r, a_i=a_i, t_r=t_r, t_i=t_i, l_r=l_r, l_i=l_i, mod=mod,
                q_r=q_r, q_i=q_i, w_r=w_r, w_i=w_i)


def mode_prelude(modes_ref, pw_ref):
    m = mode_rows(modes_ref[0], modes_ref[1], modes_ref[2], modes_ref[3], modes_ref[4])
    r, i = m["l_r"], m["l_i"]
    for k in range(8):
        pw_ref[2 * k] = r
        pw_ref[2 * k + 1] = i
        r, i = cmul(r, i, r, i)
    pw_ref[16] = 2.0 * m["w_r"]
    pw_ref[17] = 2.0 * m["w_i"]


def group_rows(pw_ref, g):
    rows = [pw_ref[k, pl.ds(g, 1), :] for k in range(18)]
    return [jnp.broadcast_to(x, (8, 128)) for x in rows]


def power_table(rows, reverse):
    sub = lax.broadcasted_iota(jnp.int32, (8, 128), 0)
    if reverse:
        sub = 7 - sub
        r, i = jnp.ones((8, 128), jnp.float32), jnp.zeros((8, 128), jnp.float32)
    else:
        r, i = rows[0], rows[1]
    for k in range(3):
        bit = ((sub >> k) & 1) == 1
        fr = jnp.where(bit, rows[2 * k], 1.0)
        fi = jnp.where(bit, rows[2 * k + 1], 0.0)
        r, i = cmul(r, i, fr, fi)
    parts = [(r, i)]
    for k in range(3, 7):
        more = [cmul(a, b, rows[2 * k], rows[2 * k + 1]) for a, b in parts]
        parts = more + parts if reverse else parts + more
    return (jnp.concatenate([p[0] for p in parts], 0), jnp.concatenate([p[1] for p in parts], 0))


def nt(a, b, **kw):
    return lax.dot_general(a, b, (((1,), (1,)), ((), ())), preferred_element_type=jnp.float32, **kw)


def tn(a, b, **kw):
    return lax.dot_general(a, b, (((0,), (0,)), ((), ())), preferred_element_type=jnp.float32, **kw)


def nn(a, b, **kw):
    return jnp.dot(a, b, preferred_element_type=jnp.float32, **kw)


def kernel_rows(rd_r, w_r):
    t = lax.broadcasted_iota(jnp.int32, (SPAN, 128), 0)
    src = jnp.where(t == SPAN - 1, jnp.concatenate([w_r] * 16, 0), rd_r)
    pick = (lax.broadcasted_iota(jnp.int32, (8, 128), 1) // 32
            == lax.broadcasted_iota(jnp.int32, (8, 128), 0)).astype(jnp.float32)
    return pltpu.roll(nt(pick, src, precision=HI), 1, 1)


def toeplitz(row):
    base = pltpu.roll(jnp.broadcast_to(row, (8, 128)), 0, 1, stride=1, stride_axis=0)
    parts = [base] + [pltpu.roll(base, 8 * v, 1) for v in range(1, 16)]
    whole = jnp.concatenate(parts, 0)
    s = lax.broadcasted_iota(jnp.int32, (SPAN, 128), 0)
    t = lax.broadcasted_iota(jnp.int32, (SPAN, 128), 1)
    return jnp.where(t >= s, whole, 0.0).astype(jnp.bfloat16)


def wave_tables():
    angle = 2.0 * np.pi * np.outer(np.arange(SPAN), np.arange(SPAN)) / (2 * SPAN)
    turn = np.cos(np.pi * np.arange(SPAN))
    cosines, sines = np.cos(angle), np.sin(angle)
    there = np.concatenate([cosines, sines], 1)
    there[:, SPAN] = turn
    high = there.astype(ml_dtypes.bfloat16)
    low = (there - high.astype(np.float64)).astype(ml_dtypes.bfloat16)
    back = np.concatenate([2.0 * cosines, -2.0 * sines], 0)
    back[0] = 1.0
    back[SPAN] = turn
    return np.concatenate([high, low], 0), (back / (2 * SPAN)).astype(np.float32)


def lag_sums(xs, gy, rows, there, back):
    step = 8 * PACK
    table = there[...]

    def spectrum(x):
        x = x.astype(jnp.bfloat16)
        return nn(jnp.concatenate([x, x], 1), table)

    def one(n, sums):
        at = pl.ds(pl.multiple_of(n * step, step), step)
        u, g = spectrum(xs[at, :]), spectrum(gy[at, :])
        u_c, u_s, g_c, g_s = u[:, :128], u[:, 128:], g[:, :128], g[:, 128:]
        parts = (u_c * g_c, u_s * g_s, g_c * u_s - g_s * u_c)
        return tuple(x + jnp.sum(p.reshape(8, PACK, 128), axis=0) for x, p in zip(sums, parts))
    even, odd, cross = lax.fori_loop(0, rows // 8, one, (jnp.zeros((PACK, 128), jnp.float32),) * 3)
    ends = lax.broadcasted_iota(jnp.int32, (PACK, 128), 1) == 0
    real = even + jnp.where(ends, 0.0, odd)
    imag = jnp.where(ends, odd, cross)
    return nn(jnp.concatenate([real, imag], 1), back[...], precision=HI)


def lane_owner(rows):
    return lax.broadcasted_iota(jnp.int32, (rows, 128), 1) // 32


def fold(stack, rows):
    width = stack.shape[1]
    own = (lax.broadcasted_iota(jnp.int32, (rows, width), 1) // 32) & 3
    out = stack[:rows]
    for k in range(1, 4):
        out = jnp.where(own == k, stack[k * rows:(k + 1) * rows], out)
    return out


def spread(packed, rows):
    width = packed.shape[1]
    own = (lax.broadcasted_iota(jnp.int32, (rows, width), 1) // 32) & 3
    return jnp.concatenate([jnp.where(own == k, packed, 0.0) for k in range(4)], 0)


def gelu_pair(v):
    half = 0.5 * (1.0 + lax.erf(v * 0.7071067811865476))
    return v * half, half + v * jnp.exp(-0.5 * v * v) * 0.3989422804014327


def block_rows(r):
    return pl.ds(pl.multiple_of(r * PACK, PACK), PACK)


def unpack(src_ref, q, xs, nj, mb, h, blocks, gain):
    def body(j, _):
        for m in range(mb):
            for k in range(h):
                x = src_ref[j, block_rows(q), pl.ds((m * h + k) * 128, 128)]
                xs[block_rows(m * blocks + j * h + k), :] = x.astype(jnp.float32) * gain
        return 0
    lax.fori_loop(0, nj, body, 0)


def rows_of(pw_ref, k, q, mb):
    parts = [jnp.broadcast_to(pw_ref[k, pl.ds(q * 4 + g, 1), :], (mb, 128)) for g in range(4)]
    parts.append(jnp.zeros((PACK - 4 * mb, 128), jnp.float32))
    return jnp.concatenate(parts, 0)


def table_place(store, g, width, first=0):
    per = store.shape[1] // width
    g = g + first
    return store.at[pl.ds(pl.multiple_of(g // per * SPAN, SPAN), SPAN), pl.ds(pl.multiple_of(lax.rem(g, per) * width, width), width)]


def forward_tables(pw_ref, groups, early, toep):
    def one(g, _):
        rws = group_rows(pw_ref, g)
        p_r, p_i = power_table(rws, True)
        back = (SPAN - 1 - lax.broadcasted_iota(jnp.int32, (SPAN, 128), 0)).astype(jnp.float32)
        table_place(early, g, 512)[...] = jnp.concatenate([p_r, p_i, back * p_r, back * p_i], 1).astype(jnp.bfloat16)
        e_r, e_i = power_table(rws, False)
        w_r, w_i = jnp.concatenate([rws[16]] * 16, 0), jnp.concatenate([rws[17]] * 16, 0)
        r_r, r_i = cmul(e_r, e_i, w_r, w_i)
        table_place(early, g, 256, 2 * groups)[...] = jnp.concatenate([r_r, -r_i], 1).astype(jnp.bfloat16)
        krow = kernel_rows(r_r, rws[16])
        for k in range(4):
            toep[4 * g + k] = toeplitz(krow[k:k + 1])
        return 0
    lax.fori_loop(0, groups, one, 0, unroll=2)


def backward_tables(pw_ref, groups, state_tab, read_tab):
    def one(g, _):
        rws = group_rows(pw_ref, g)
        e_r, e_i = power_table(rws, False)
        ahead = (1 + lax.broadcasted_iota(jnp.int32, (SPAN, 128), 0)).astype(jnp.float32)
        state_tab[g] = jnp.concatenate([e_r, e_i, ahead * e_r, ahead * e_i], 1).astype(jnp.bfloat16)
        p_r, p_i = power_table(rws, True)
        w_r, w_i = jnp.concatenate([rws[16]] * 16, 0), jnp.concatenate([rws[17]] * 16, 0)
        r_r, r_i = cmul(p_r, p_i, w_r, w_i)
        read_tab[g] = jnp.concatenate([r_r, -r_i], 1).astype(jnp.bfloat16)
        return 0
    lax.fori_loop(0, groups, one, 0, unroll=2)


def channel_rows(box, c, rows):
    return box[pl.ds(c, rows, stride=PACK), :].astype(jnp.bfloat16)


def put_states(sc, s, g, mb, blocks):
    for a in range(4):
        for m in range(mb):
            sc[a, pl.ds(g * mb + m, blocks, stride=PACK), :] = s[m * blocks:(m + 1) * blocks, a * 128:(a + 1) * 128]


def get_carry(ref, g, mb, blocks):
    return jnp.concatenate([
        jnp.concatenate([ref[a, pl.ds(g * mb + m, blocks, stride=PACK), :] for m in range(mb)], 0) for a in range(2)], 1)


def forward_pack(dims, q, skip_ref, gain_ref, span, early, toep, u_ref, act_ref, slope_ref, carry_ref, pw_ref, xs, ys, sc, poll):
    nj, chans, mb, h = dims
    blocks = nj * h
    rows = mb * blocks
    unpack(u_ref, q, xs, nj, mb, h, blocks, gain_ref[block_rows(q), :])

    def states(g, _):
        x = jnp.concatenate([channel_rows(xs, 4 * g + k, rows) for k in range(4)], 0)
        put_states(sc, fold(nn(x, table_place(early, q * 4 + g, 512)[...]), rows), g, mb, blocks)
        return 0
    lax.fori_loop(0, 4, states, 0, unroll=FU)
    h_r, h_i = rows_of(pw_ref, 14, q, mb), rows_of(pw_ref, 15, q, mb)

    def step(i, c):
        at = block_rows(i)
        keep = keep_row(span, i)
        c = [x * keep for x in c]
        s = [sc[a, at, :] for a in range(4)]
        for a in range(4):
            carry_ref[q, a, at, :] = c[a]
        z_r, z_i = cmul(c[0], c[1], h_r, h_i)
        d_r, d_i = cmul(c[2] + SPAN * c[0], c[3] + SPAN * c[1], h_r, h_i)
        return (z_r + s[0], z_i + s[1], d_r + s[2], d_i + s[3])
    zero = jnp.zeros((PACK, 128), jnp.float32)
    lax.fori_loop(0, blocks, step, (zero,) * 4, unroll=SU)
    poll(f'f{q}a')

    def outputs(g, _):
        c = get_carry(carry_ref.at[q], g, mb, blocks)
        across = nt(spread(c, rows).astype(jnp.bfloat16), table_place(early, q * 4 + g, 256, 2 * (chans // 4))[...])
        for k in range(4):
            y = across[k * rows:(k + 1) * rows] + nn(channel_rows(xs, 4 * g + k, rows), toep[q * PACK + 4 * g + k])
            ys[pl.ds(4 * g + k, rows, stride=PACK), :] = y
        return 0
    lax.fori_loop(0, 4, outputs, 0, unroll=FU)
    poll(f'f{q}b')
    skip = skip_ref[block_rows(q), :]

    def finish(j, _):
        for m in range(mb):
            for k in range(h):
                r = m * blocks + j * h + k
                v = ys[block_rows(r), :] + skip * xs[block_rows(r), :]
                a, d = gelu_pair(v)
                act_ref[j, block_rows(q), pl.ds((m * h + k) * 128, 128)] = a.astype(jnp.bfloat16)
                slope_ref[q, block_rows(r), :] = d
        return 0
    lax.fori_loop(0, nj, finish, 0)


def backward_pack(dims, q, skip_ref, gain_ref, span, state_tab, read_tab, toep, waves, u_ref, ga_ref, slope_ref, carry_ref, gn_ref, zw_ref, ng_ref, pw_ref, xs, gy, gx, sc, lags, poll):
    nj, chans, mb, h = dims
    blocks = nj * h
    rows = mb * blocks
    unpack(u_ref, q, xs, nj, mb, h, blocks, gain_ref[block_rows(q), :])

    def start(j, _):
        for m in range(mb):
            for k in range(h):
                r = m * blocks + j * h + k
                x = ga_ref[j, block_rows(q), pl.ds((m * h + k) * 128, 128)]
                gy[block_rows(r), :] = x.astype(jnp.float32) * slope_ref[q, block_rows(r), :]
        return 0
    lax.fori_loop(0, nj, start, 0)
    lags[...] = lag_sums(xs, gy, rows, *waves)
    poll(f'b{q}a')

    def states(g, _):
        gg = q * 4 + g
        ups = [channel_rows(gy, 4 * g + k, rows) for k in range(4)]
        lag = jnp.concatenate([lags[pl.ds(4 * g, 4), :], jnp.zeros((4, 128), jnp.float32)], 0)
        own8 = lax.broadcasted_iota(jnp.int32, (8, 128), 1) // 32 == lax.broadcasted_iota(jnp.int32, (8, 128), 0)
        lag0 = jnp.sum(jnp.where(own8, jnp.broadcast_to(lag[:, 0:1], (8, 128)), 0.0), axis=0, keepdims=True)
        lane = lax.broadcasted_iota(jnp.int32, (8, 128), 1)
        later = jnp.where(lane == 127, 0.0, pltpu.roll(lag, 127, 1))
        top = later.astype(jnp.bfloat16)
        low = (later - top.astype(jnp.float32)).astype(jnp.bfloat16)
        s = nn(jnp.concatenate(ups + [top, low], 0), state_tab[gg])
        near = s[4 * rows:4 * rows + 8] + s[4 * rows + 8:]
        near = jnp.sum(jnp.where(jnp.concatenate([own8] * 4, 1), near, 0.0), axis=0, keepdims=True)
        zw_ref[0, pl.ds(gg, 1), :] = near[:, 0:128] + lag0
        for a in range(1, 4):
            zw_ref[a, pl.ds(gg, 1), :] = near[:, a * 128:(a + 1) * 128]
        zw_ref[4, pl.ds(gg, 1), :] = lag0
        put_states(sc, fold(s[:4 * rows], rows), g, mb, blocks)
        return 0
    lax.fori_loop(0, 4, states, 0, unroll=FU)
    h_r, h_i = rows_of(pw_ref, 14, q, mb), rows_of(pw_ref, 15, q, mb)

    def step(n, c):
        i = blocks - 1 - n
        at = block_rows(i)
        a_r, a_i, z_r, z_i, w_r, w_i = c
        q_ = [sc[a, at, :] for a in range(4)]
        f = [carry_ref[q, a, at, :] for a in range(4)]
        d = cmul(q_[0], q_[1], f[0], f[1])
        e1 = cmul(q_[2], q_[3], f[0], f[1])
        e2 = cmul(q_[0], q_[1], f[2], f[3])
        sc[0, at, :] = a_r
        sc[1, at, :] = a_i
        keep = keep_row(span, i)
        n_r, n_i = cmul(a_r, a_i, h_r, h_i)
        return ((n_r + q_[0]) * keep, (n_i + q_[1]) * keep, z_r + d[0], z_i + d[1], w_r + e1[0] + e2[0], w_i + e1[1] + e2[1])
    zero = jnp.zeros((PACK, 128), jnp.float32)
    out = lax.fori_loop(0, blocks, step, (zero,) * 6, unroll=SU)
    for a in range(4):
        for g in range(4):
            add = jnp.sum(out[2 + a][g * mb:(g + 1) * mb], axis=0, keepdims=True)
            zw_ref[a, pl.ds(q * 4 + g, 1), :] += add
    poll(f'b{q}b')

    def outputs(g, _):
        across = nt(spread(get_carry(sc, g, mb, blocks), rows).astype(jnp.bfloat16), read_tab[q * 4 + g])
        for k in range(4):
            y = across[k * rows:(k + 1) * rows] + nt(channel_rows(gy, 4 * g + k, rows), toep[q * PACK + 4 * g + k])
            gx[pl.ds(4 * g + k, rows, stride=PACK), :] = y
        return 0
    lax.fori_loop(0, 4, outputs, 0, unroll=FU)
    poll(f'b{q}c')
    skip = skip_ref[block_rows(q), :]

    def finish(j, total):
        for m in range(mb):
            for k in range(h):
                r = m * blocks + j * h + k
                v = (gx[block_rows(r), :] + skip * gy[block_rows(r), :]).astype(jnp.bfloat16)
                cols = pl.ds((m * h + k) * 128, 128)
                gn_ref[j, block_rows(q), cols] = v
                total = total + v.astype(jnp.float32) * u_ref[j, block_rows(q), cols].astype(jnp.float32)
        return total
    ng_ref[block_rows(q), :] = lax.fori_loop(0, nj, finish, jnp.zeros((PACK, 128), jnp.float32))


def mode_gradients(modes, zw):
    m = mode_rows(*modes)
    z_r, z_i, v_r, v_i = zw[0], zw[1], zw[2], zw[3]
    rr, ri = modes[3], modes[4]
    g_rr = 2.0 * (z_r * m["q_r"] - z_i * m["q_i"])
    g_ri = -2.0 * (z_r * m["q_i"] + z_i * m["q_r"])
    k_r, k_i = cmul(rr, ri, m["a_r"] / m["mod"], -m["a_i"] / m["mod"])
    s_r, s_i = cmul(k_r, k_i, m["l_r"], m["l_i"])
    h1 = cmul(z_r, z_i, s_r, s_i)
    h2 = cmul(m["w_r"], m["w_i"], v_r, v_i)
    h_r, h_i = h1[0] + h2[0], h1[1] + h2[1]
    zc = cmul(z_r, z_i, m["w_r"], m["w_i"])
    za = cmul(zc[0], zc[1], m["a_r"] / m["mod"], -m["a_i"] / m["mod"])
    j_r, j_i = h_r * m["dt"] - za[0], h_i * m["dt"] - za[1]
    g_ls = 2.0 * (h_r * m["t_r"] - h_i * m["t_i"])
    return g_ls, 2.0 * m["a_r"] * j_r, -2.0 * j_i, g_rr, g_ri


def keep_rows(lengths, blocks, mb):
    at = jnp.arange(blocks, dtype=jnp.int32)[:, None] * SPAN
    keep = (at % lengths[None, :] != 0).astype(jnp.float32)
    rows = jnp.concatenate([keep] * 4 + [jnp.zeros((blocks, PACK - 4 * mb), jnp.float32)], 1)
    return jnp.broadcast_to(rows[:, :, None], (blocks, PACK, 128))


MESH = pl.DeviceIdType.MESH
F32, BF16 = jnp.float32, jnp.bfloat16


def layer_stats(v):
    average = jnp.mean(v, axis=-1, keepdims=True)
    centred = v - average
    spread = jnp.mean(centred * centred, axis=-1, keepdims=True)
    scale = lax.rsqrt(spread + 1e-05)
    return centred * scale, scale


def layer_back(q, n, scale):
    return scale * (q - jnp.mean(q, axis=-1, keepdims=True) - n * jnp.mean(q * n, axis=-1, keepdims=True))


def column_sum(x):
    return jnp.sum(x, axis=0, keepdims=True)


def peers(count, me):
    return [lax.rem(me + k, count) for k in range(1, count)]


def greet(n_dp, n_chan, d, c):
    barrier = pltpu.get_barrier_semaphore()
    for p in peers(n_dp, d):
        pl.semaphore_signal(barrier, inc=1, device_id=(p, c), device_id_type=MESH)
    for p in peers(n_chan, c):
        pl.semaphore_signal(barrier, inc=1, device_id=(d, p), device_id_type=MESH)


def be_greeted(n_dp, n_chan):
    pl.semaphore_wait(pltpu.get_barrier_semaphore(), n_dp + n_chan - 2)


def send(src, dst, send_sem, recv_sem, to):
    copy = pltpu.make_async_remote_copy(src_ref=src, dst_ref=dst, send_sem=send_sem, recv_sem=recv_sem, device_id=to, device_id_type=MESH)
    copy.start()
    return copy


def settle(whole, send_sem, recv_sem, here):
    pltpu.make_async_remote_copy(src_ref=whole, dst_ref=whole, send_sem=send_sem, recv_sem=recv_sem, device_id=here, device_id_type=MESH).wait()


class Exchange:
    def __init__(self, box, sems, count, me, to, here):
        self.box, self.sems, self.count, self.me, self.to, self.here = box, sems, count, me, to, here

    def start(self):
        for p in peers(self.count, self.me):
            send(self.box.at[self.me], self.box.at[self.me], self.sems.at[0], self.sems.at[1], self.to(p))

    def wait(self):
        settle(self.box.at[pl.ds(0, self.count - 1)], self.sems.at[0], self.sems.at[1], self.here)

    def total(self):
        return sum(self.box[k] for k in range(self.count))


class Copies:
    def __init__(self, sems):
        self.sems = sems
        self.used = 0
        self.unsent = []

    def put(self, src, dst, to):
        n = self.used
        self.used += 1
        copy = send(src, dst, self.sems.at[0, n], self.sems.at[1, n], to)
        self.unsent.append(copy)
        return copy

    def finish(self):
        for copy in self.unsent:
            copy.wait_send()


def arrive(copies):
    for copy in copies:
        copy.wait_recv()


class Place:
    def __init__(self, d, c):
        self.d, self.c = d, c
        self.a, self.b, self.core = c // 4, lax.rem(c // 2, 2), lax.rem(c, 2)

    def at(self, a, b, core):
        return (self.d, a * 4 + b * 2 + core)

    @property
    def over_a(self):
        return self.at(1 - self.a, self.b, self.core)

    @property
    def over_b(self):
        return self.at(self.a, 1 - self.b, self.core)

    @property
    def twin(self):
        return self.at(self.a, self.b, 1 - self.core)


class Part:
    def __init__(self, rows, low, high):
        self.rows, self.low, self.high = rows, low, high
        self.all = pl.ds(low.start, low.size + high.size)


def parts_of(w_out, w_in, w_back):
    def cut(w, rows, first, cols):
        return Part(rows, pl.ds(first, cols // 2), pl.ds(first + cols // 2, cols // 2))
    r, k = w_out.shape[-2:]
    some = [(0, cut(w_out, pl.ds(0, r), 0, k))]
    r, k = w_in.shape[-2:]
    some += [(1, cut(w_in, pl.ds(0, r), n * (k // 2), k // 2)) for n in range(2)]
    r, k = w_back.shape[-2:]
    some += [(2, cut(w_back, pl.ds(n * (r // 2), r // 2), 0, k)) for n in range(2)]
    return some


class Gather:
    def __init__(self, w, part, dp_first, copies, here, n_dp):
        self.w, self.part, self.copies, self.here, self.n_dp = w, part, copies, here, n_dp
        self.step, self.side, self.at = [], [], 0
        self.stages = [self.dp_first, self.hop] if dp_first else [self.first, self.dp_second]
        self.stages += [self.last, self.twin, self.done]

    def advance(self):
        self.stages[self.at]()
        self.at += 1

    def same(self, ref, to):
        return self.copies.put(ref, ref, to)

    def low(self, d, a, b, core):
        return self.w.at[d, a, b, core, self.part.rows, self.part.low]

    def high(self, d, a, b, core):
        return self.w.at[d, a, b, core, self.part.rows, self.part.high]

    def first(self):
        i = self.here
        self.step = [self.same(self.low(i.d, i.a, i.b, i.core), i.over_b), self.same(self.high(i.d, i.a, i.b, i.core), i.over_a)]

    def dp_second(self):
        i = self.here
        arrive(self.step)
        self.step = []
        for p in peers(self.n_dp, i.d):
            self.step.append(self.same(self.low(i.d, i.a, slice(None), i.core), (p, i.c)))
            self.step.append(self.same(self.high(i.d, slice(None), i.b, i.core), (p, i.c)))

    def dp_first(self):
        i = self.here
        own = self.w.at[i.d, i.a, i.b, i.core, self.part.rows, self.part.all]
        self.step = [self.same(own, (p, i.c)) for p in peers(self.n_dp, i.d)]

    def hop(self):
        i, every = self.here, slice(None)
        arrive(self.step)
        self.step = [self.same(self.low(every, i.a, i.b, i.core), i.over_b), self.same(self.high(every, i.a, i.b, i.core), i.over_a)]

    def last(self):
        i, every = self.here, slice(None)
        arrive(self.step)
        low, high = self.low(every, i.a, every, i.core), self.high(every, every, i.b, i.core)
        self.step = [self.same(low, i.over_a), self.same(high, i.over_b)]
        self.side = [self.same(low, i.twin), self.same(high, i.twin)]

    def twin(self):
        i, every = self.here, slice(None)
        arrive(self.step)
        self.side += [self.same(self.low(every, 1 - i.a, every, i.core), i.twin), self.same(self.high(every, every, 1 - i.b, i.core), i.twin)]

    def done(self):
        arrive(self.side)


class Scatter:
    def __init__(self, g, part, dp_last, boxes, out, copies, here, n_dp):
        self.g, self.part, self.out, self.copies, self.here, self.n_dp = g, part, out, copies, here, n_dp
        self.box, self.low_box, self.high_box, *self.more = boxes
        self.step, self.at = [], 0
        self.stages = [self.to_twin, self.add_twin]
        self.stages += [self.hop, self.dp_last, self.done_last] if dp_last else [self.dp, self.hop_last, self.done]

    def advance(self):
        self.stages[self.at]()
        self.at += 1

    def put(self, src, dst, to):
        self.step.append(self.copies.put(src, dst, to))

    def arrived(self):
        arrive(self.step)
        self.step = []

    def to_twin(self):
        i, every = self.here, slice(None)
        self.put(self.g.at[every, every, every, 1 - i.core, self.part.rows, self.part.all], self.box, i.twin)

    def add_twin(self):
        i, part, box = self.here, self.part, self.box
        self.arrived()
        half = box.shape[-1] // 2

        def add(n, _):
            for a in range(2):
                for b in range(2):
                    own = self.g[n, a, b, i.core, part.rows, part.all]
                    box[n, a, b] = (box[n, a, b].astype(F32) + own.astype(F32)).astype(BF16)
            return 0
        lax.fori_loop(0, box.shape[0], add, 0)
        self.put(box.at[:, 1 - i.a, :, :, pl.ds(0, half)], self.low_box, i.over_a)
        self.put(box.at[:, :, 1 - i.b, :, pl.ds(half, half)], self.high_box, i.over_b)

    def add_hop(self):
        i, box, low_box, high_box = self.here, self.box, self.low_box, self.high_box
        self.arrived()
        half = box.shape[-1] // 2

        def add(n, _):
            for k in range(2):
                low_box[n, k] = (low_box[n, k].astype(F32) + box[n, i.a, k, :, :half].astype(F32)).astype(BF16)
                high_box[n, k] = (high_box[n, k].astype(F32) + box[n, k, i.b, :, half:].astype(F32)).astype(BF16)
            return 0
        lax.fori_loop(0, box.shape[0], add, 0)

    def hop(self):
        i = self.here
        low2, high2, _low3, _high3 = self.more
        self.add_hop()
        self.put(self.low_box.at[:, 1 - i.b], low2, i.over_b)
        self.put(self.high_box.at[:, 1 - i.a], high2, i.over_a)

    def dp_last(self):
        i = self.here
        low2, high2, low3, high3 = self.more
        self.arrived()
        for n in range(self.n_dp):
            low2[n] = (low2[n].astype(F32) + self.low_box[n, i.b].astype(F32)).astype(BF16)
            high2[n] = (high2[n].astype(F32) + self.high_box[n, i.a].astype(F32)).astype(BF16)
        for p in peers(self.n_dp, i.d):
            self.put(low2.at[p], low3.at[i.d], (p, i.c))
            self.put(high2.at[p], high3.at[i.d], (p, i.c))

    def done_last(self):
        i = self.here
        low2, high2, low3, high3 = self.more
        self.arrived()
        for own, box, cols in ((low2, low3, self.part.low), (high2, high3, self.part.high)):
            total = own[i.d].astype(F32)
            for p in peers(self.n_dp, i.d):
                total = total + box[p].astype(F32)
            self.out[self.part.rows, cols] = total

    def dp(self):
        i = self.here
        low2, high2, _low3, _high3 = self.more
        self.add_hop()
        for p in peers(self.n_dp, i.d):
            self.put(self.low_box.at[p], low2.at[i.d], (p, i.c))
            self.put(self.high_box.at[p], high2.at[i.d], (p, i.c))

    def hop_last(self):
        i = self.here
        low2, high2, low3, high3 = self.more
        self.arrived()
        for first, box, other, own, cols, to in (
            (self.low_box, low2, low3, i.b, self.part.low, i.over_b), (self.high_box, high2, high3, i.a, self.part.high, i.over_a),
        ):
            def total(k):
                x = first[i.d, k].astype(F32)
                for p in peers(self.n_dp, i.d):
                    x = x + box[p, k].astype(F32)
                return x
            self.out[self.part.rows, cols] = total(own)
            other[0] = total(1 - own).astype(BF16)
            self.put(other.at[0], other.at[1], to)

    def done(self):
        _low2, _high2, low3, high3 = self.more
        self.arrived()
        for box, cols in ((low3, self.part.low), (high3, self.part.high)):
            self.out[self.part.rows, cols] += box[1].astype(F32)


def scatter_boxes(size, dp_last):
    r, k = size
    half = (r, k // 2)
    boxes = [(4, 2, 2, r, k), (4, 2) + half, (4, 2) + half]
    return boxes + ([(4,) + half] * 4 if dp_last else [(4, 2) + half] * 2 + [(2,) + half] * 2)


def wide(vec_ref, first, count):
    return jnp.concatenate([vec_ref[first + k:first + k + 1, :] for k in range(count)], 1)


def add_wide(vec_ref, first, row):
    for k in range(row.shape[1] // 128):
        vec_ref[first + k:first + k + 1, :] += row[:, k * 128:(k + 1) * 128]


def put_own(vec_ref, first, own, shard, shards):
    size = own.shape[1]
    rows = size * shards // 128
    while own.shape[1] < 128:
        own = jnp.concatenate([own, own], 1)
    index = 128 * lax.broadcasted_iota(jnp.int32, (rows, 128), 0) + lax.broadcasted_iota(jnp.int32, (rows, 128), 1)
    inside = (index >= shard * size) & (index < (shard + 1) * size)
    vec_ref[first:first + rows, :] = jnp.where(inside, jnp.broadcast_to(own, (rows, 128)), 0.0)


def pick_own(vec_ref, first, size, shard):
    start = shard * size
    row = vec_ref[pl.ds(first + start // 128, 1), :]
    row = pltpu.roll(jnp.broadcast_to(row, (8, 128)), lax.rem(128 - lax.rem(start, 128), 128), 1)
    return row[0:1, :size]


def to_column(row):
    return jnp.broadcast_to(row, (128, row.shape[1])).T


def padded(x, lanes=128):
    if x.shape[1] == lanes:
        return x
    return jnp.concatenate([x, jnp.zeros((x.shape[0], lanes - x.shape[1]), x.dtype)], 1)


def lane_pick(groups, k):
    lane = lax.broadcasted_iota(jnp.int32, (groups, 128), 1)
    return (lane == 4 * lax.broadcasted_iota(jnp.int32, (groups, 128), 0) + k).astype(F32)


def spread_modes(rows, modes):
    groups = modes.shape[1]
    for k in range(4):
        part = nt(lane_pick(groups, k), rows, precision=HI)
        for a in range(modes.shape[0]):
            modes[a, :, k * 32:(k + 1) * 32] = part[:, a * 32:(a + 1) * 32]


def collect_modes(arrays):
    groups = arrays[0].shape[0]
    total = None
    for k in range(4):
        part = jnp.concatenate([x[:, k * 32:(k + 1) * 32] for x in arrays], 1)
        part = tn(part, lane_pick(groups, k), precision=HI)
        total = part if total is None else total + part
    return total


def flat(x):
    return x.reshape(-1, x.shape[-1])


def row_block(m, t):
    return pl.ds(pl.multiple_of(m * t, t), t)


def dense_up(m, t, tokens, act, w_out, w_in, vec, keeps):
    middle, gate_ref, gated_ref, second, _hidden, _slopes = keeps
    at = row_block(m, t)
    feats = tokens.shape[1]
    project = tn(act[:, :, at].reshape(feats, t), flat(w_out[...])) + wide(vec, 0, 2 * feats // 128)
    gate = jax.nn.sigmoid(project[:, feats:])
    gated = project[:, :feats] * gate
    total = tokens[at, :].astype(F32) + gated
    gate_ref[at, :] = gate
    gated_ref[at, :] = gated
    middle[at, :] = total
    n, _scale = layer_stats(total)
    after = (n * wide(vec, 12, feats // 128)).astype(BF16)
    second[at, :] = after
    dense_hidden(m, t, (0, 1), w_in, vec, keeps)


def dense_hidden(m, t, tiles, w_in, vec, keeps):
    _middle, _gate_ref, _gated_ref, second, hidden, slopes = keeps
    at = row_block(m, t)
    tile = w_in.shape[-1] // 4
    after = second[at, :]
    for f in tiles:
        cols = slice(f * tile, (f + 1) * tile)
        before = nn(after, flat(w_in[:, :, :, :, :, cols])) + wide(vec, 16 + f * tile // 128, tile // 128)
        high, slope = gelu_pair(before)
        hidden[at, cols] = high.astype(BF16)
        slopes[at, cols] = slope


def dense_down(m, t, cot, wholes, vec, block_out, keeps, gb, gp, snd, sums):
    w_out, w_in, w_back = wholes
    middle, gate_ref, gated_ref, second, hidden, slopes = keeps
    at = row_block(m, t)
    feats = cot.shape[1]
    tile = w_in.shape[-1] // 4
    up = cot[at, :]
    total = middle[at, :]
    n, scale = layer_stats(total)
    gain = wide(vec, 12, feats // 128)
    for f in range(4):
        cols = slice(f * tile, (f + 1) * tile)
        low = (slopes[at, cols] * nt(up, flat(w_back[f]))).astype(BF16)
        gb[at, cols] = low
        add_wide(sums, 16 + f * tile // 128, column_sum(low.astype(F32)))
    total = total + nn(hidden[at, :], flat(w_back[...]))
    back = nt(gb[at, :], flat(w_in[...]))
    block_out[at, :] = total.astype(BF16)
    add_wide(sums, 12, column_sum(back * n))
    grad = up.astype(F32) + layer_back(back * gain, n, scale)
    middle[at, :] = grad
    gate = gate_ref[at, :]
    first = (grad * gate).astype(BF16)
    last = (grad * gated_ref[at, :] * (1.0 - gate)).astype(BF16)
    gp[at, :feats] = first
    gp[at, feats:] = last
    add_wide(sums, 0, column_sum(first.astype(F32)))
    add_wide(sums, feats // 128, column_sum(last.astype(F32)))
    both = jnp.concatenate([first, last], 1)
    snd[:, :, at] = nt(flat(w_out[...]), both).astype(BF16).reshape(snd.shape[:2] + (t,))


def shaped(x, g):
    return x.astype(BF16).reshape(g.shape[1:])


def outer_products(left, right, g):
    size = left.shape[1] // 4
    def one(n, _):
        g[n] = shaped(tn(left[:, row_block(n, size)], right[...]), g)
        return 0
    lax.fori_loop(0, 4, one, 0)


PART_NAMES = ("o", "i", "j", "b", "c")
GATHER_DP_FIRST = (False, False, False, False, True)
SCATTER_DP_LAST = (True, False, True, False, False)
SCHEDULE = {
    "greeted": ("gc", "go", "gi", "gj", "gb"),
    "sent": ("go", "gi", "gc"),
    "tables": ("go", "gj"),
    "f0c": ("gb",),
    "f1b": ("gi",),
    "f1c": ("go",),
    "f3c": ("gj", "gc", "gi"),
    "act": ("go", "gi"),
    "up0": ("gb",),
    "up2": ("gj", "gj"),
    "hid1": ("gc",),
    "g_back": ("sb", "sc", "sb", "sc", "gb", "gc", "gb"),
    "g_in": ("si", "sj"),
    "g_out": ("si", "so", "sj", "so"),
    "b0d": ("si", "sb", "sc"),
    "b1a": ("sj",),
    "b1d": ("so",),
    "b2d": ("sj", "si"),
    "zw": ("so",),
    "tail": ("sb", "sc", "si"),
    "rows": ("sj", "so"),
    "down0": ("sb",),
    "down1": ("sc",),
}


def whole_kernel(dims, n_dp, direct, *refs):
    nj, chans, mb, h = dims
    refs = list(refs)
    def take(n):
        out = refs[:n]
        del refs[:n]
        return out
    tokens_in, cot_in, lengths, log_step, skip_row, *mode_parts = take(9)
    vectors = take(4)
    waves = take(2)
    given = take(3)
    block_out_to, grad_tokens_to = take(2)
    g_step, g_skip, *g_modes = take(6)
    g_vectors = take(4)
    results_to = take(3)
    tokens, cot, block_out, grad_tokens = take(4)
    u, snd, act, out, ga, gn, slope, carry = take(8)
    second, hidden, gb, gp = take(4)
    keeps = take(4)
    middle = keeps[0]
    keeps = keeps[:3] + [second, hidden] + keeps[3:]
    vec_dp, vec_chan, vec2_dp, vec2_chan, modes_dp, zw_dp, ng_dp, ng_chan = take(8)
    modes, vec, sums, skip, gain, mode_rows_box = take(6)
    pw, xs, ys, gy, sc, lags, toep, state_tab, read_tab = take(9)
    box_sems, in_sems, out_sems, back_sems, gn_sems, own_sems = take(6)
    d, c = lax.axis_index("dp"), lax.axis_index("chan")
    here = (d, c)
    shards, shard = n_dp * nj, d * nj + c
    packs = chans // PACK
    groups = modes.shape[1]
    width = tokens.shape[0]
    t = width // mb
    feats = nj * chans
    over_dp, over_chan = (lambda p: (p, c)), (lambda p: (d, p))

    def along_dp(box, n):
        return Exchange(box, box_sems.at[n], n_dp, d, over_dp, here)

    def along_chan(box, n):
        return Exchange(box, box_sems.at[n], nj, c, over_chan, here)
    vec_first, vec_second = along_dp(vec_dp, 0), along_chan(vec_chan, 1)
    modes_all = along_dp(modes_dp, 2)
    sums_first, sums_second = along_chan(vec2_chan, 3), along_dp(vec2_dp, 4)
    zw_all, ng_first, ng_second = along_dp(zw_dp, 5), along_dp(ng_dp, 6), along_chan(ng_chan, 7)
    if direct:
        wholes, grads = take(3), take(3)
        results = take(3)
        places = parts_of(*wholes)
        boxes = [take(7) for _ in places]
        place = Place(d, c)
        gather_copies, scatter_copies = Copies(refs[0]), Copies(refs[1])
        parts = {}
        for (k, part), dp_first, dp_last, name, each in zip(places, GATHER_DP_FIRST, SCATTER_DP_LAST, PART_NAMES, boxes):
            parts["g" + name] = Gather(wholes[k], part, dp_first, gather_copies, place, n_dp)
            parts["s" + name] = Scatter(grads[k], part, dp_last, each, results[k], scatter_copies, place, n_dp)
    else:
        wholes, grads = given, results_to
    g_out, g_in, g_back = grads

    def poll(point):
        if direct:
            for name in SCHEDULE.get(point, ()):
                parts[name].advance()

    def fetch(src, dst, n):
        copy = pltpu.make_async_copy(src, dst, own_sems.at[n])
        copy.start()
        return copy
    fetched = [fetch(tokens_in, tokens, 0)]
    if direct:
        fetched += [fetch(own, w.at[d, place.a, place.b, place.core], 2 + k) for k, (own, w) in enumerate(zip(given, wholes))]
    fetched.append(fetch(cot_in, cot, 1))

    for k, (own, first) in enumerate(zip(vectors, (0, 8, 12, 16))):
        put_own(vec_dp.at[d], first, own[...].astype(F32), shard, shards)
    for a in range(4):
        modes_dp[d, a] = padded(mode_parts[a][...])
    greet(n_dp, nj, d, c)
    fetched[0].wait()

    def normalize(m, _):
        at = row_block(m, t)
        n, _scale = layer_stats(tokens[at, :].astype(F32))
        snd[:, :, at] = n.T.astype(BF16).reshape(nj, chans, t)
        return 0
    lax.fori_loop(0, mb, normalize, 0)
    be_greeted(n_dp, nj)
    vec_first.start()
    modes_all.start()
    if direct:
        for copy in fetched[1:4]:
            copy.wait()
    poll("greeted")

    def share(box, where, sems, q):
        for p in peers(nj, c):
            send(box.at[p, block_rows(q)], where.at[c, block_rows(q)], sems.at[0, q], sems.at[1, q], (d, p))
        where[c, block_rows(q), :] = box[c, block_rows(q), :]

    def shared(where, sems, q):
        settle(where.at[pl.ds(0, nj - 1), block_rows(q)], sems.at[0, q], sems.at[1, q], here)

    for q in range(packs):
        share(snd, u, in_sems, q)
    poll("sent")
    sums[...] = jnp.zeros(sums.shape, F32)
    sc[...] = jnp.zeros(sc.shape, F32)
    skip[...] = to_column(skip_row[...])
    long = lengths[...] - 1
    row = lax.broadcasted_iota(jnp.int32, (PACK, 128), 0)
    span = jnp.zeros((PACK, 128), jnp.int32)
    for m in range(mb):
        span = jnp.where(lax.rem(row, mb) == m, jnp.broadcast_to(long[:, m:m + 1], (PACK, 128)), span)
    vec_first.wait()
    vec_chan[c] = vec_first.total()
    vec_second.start()
    modes_all.wait()
    kinds = [jnp.broadcast_to(padded(log_step[...]), (32, 128))]
    kinds += [jnp.concatenate([modes_dp[p, a] for p in range(n_dp)], 0) for a in range(4)]
    spread_modes(jnp.concatenate(kinds, 0), modes)
    mode_prelude(modes, pw)
    forward_tables(pw, groups, gb, toep)
    poll("tables")
    backward_tables(pw, groups, state_tab, read_tab)
    vec_second.wait()
    vec[...] = vec_second.total()
    for k in range(nj):
        @pl.when(c == k)
        def _():
            first = k * chans
            row = vec[8 + first // 128:9 + first // 128, :]
            gain[...] = to_column(row[:, first % 128:first % 128 + chans])

    for q in range(packs):
        shared(u, in_sems, q)
        forward_pack(dims, q, skip, gain, span, gb, toep, u, out, slope, carry, pw, xs, ys, sc, poll)
        share(out, act, out_sems, q)
        poll(f'f{q}c')
    for q in range(packs):
        shared(act, out_sems, q)
    poll("act")
    for m in range(mb):
        dense_up(m, t, tokens, act, wholes[0], wholes[1], vec, keeps)
        poll(f"up{m}")
    for m in range(mb):
        dense_hidden(m, t, (2, 3), wholes[1], vec, keeps)
        poll(f"hid{m}")
    fetched[-1].wait()
    outer_products(hidden, cot, g_back)
    poll("g_back")
    for m in range(mb):
        dense_down(m, t, cot, wholes, vec, block_out, keeps, gb, gp, snd, sums)
        poll(f"pre{m}")
        at = pl.ds(m * t, t)
        for p in peers(nj, c):
            send(snd.at[p, :, at], ga.at[c, :, at], back_sems.at[0, m], back_sems.at[1, m], (d, p))
        ga[c, :, at] = snd[c, :, at]
        poll(f"down{m}")
    written = [fetch(block_out, block_out_to, 5)]
    vec2_chan[c] = sums[...]
    sums_first.start()
    outer_products(second, gb, g_in)
    poll("g_in")
    def outer(n, _):
        g_out[n] = shaped(nn(flat(act[pl.ds(n * (nj // 4), nj // 4)]), gp[...]), g_out)
        return 0
    lax.fori_loop(0, 4, outer, 0)
    poll("g_out")
    for m in range(mb):
        settle(ga.at[pl.ds(0, nj - 1), :, pl.ds(m * t, t)], back_sems.at[0, m], back_sems.at[1, m], here)
    poll("ga")
    for q in range(packs):
        backward_pack(dims, q, skip, gain, span, state_tab, read_tab, toep, waves, u, ga, slope, carry, out, zw_dp.at[d], ng_dp.at[d], pw, xs, gy, ys, sc, lags, poll)
        share(out, gn, gn_sems, q)
        poll(f'b{q}d')
        if q == packs // 2:
            sums_first.wait()
            vec2_dp[d] = sums_first.total()
            sums_second.start()
    zw_all.start()
    ng_first.start()
    poll("zw")
    zw_all.wait()
    zw = [sum(zw_dp[k, a] for k in range(n_dp)) for a in range(5)]
    found = list(mode_gradients([modes[a] for a in range(5)], zw)) + [zw[4]]
    mode_rows_box[...] = collect_modes(found)
    g_step[...] = column_sum(mode_rows_box[0:32, :])[:, :chans]
    g_skip[...] = mode_rows_box[160:161, :chans]
    for a in range(4):
        each = g_modes[a].shape[0]
        g_modes[a][...] = mode_rows_box[pl.ds(32 * (a + 1) + d * each, each), :chans]
    ng_first.wait()
    ng_chan[c, 0:1, :] = padded(column_sum(ng_first.total().T))
    ng_chan[c, 1:8, :] = jnp.zeros((7, 128), F32)
    ng_second.start()
    for q in range(packs):
        shared(gn, gn_sems, q)
    poll("tail")
    if direct:
        written.append(fetch(results[2], results_to[2], 9))
    wide_gain = wide(vec, 8, feats // 128)
    for m in range(mb):
        at = row_block(m, t)
        n, scale = layer_stats(tokens[at, :].astype(F32))
        grad = gn[:, :, at].reshape(feats, t).astype(F32).T
        grad_tokens[at, :] = (middle[at, :] + layer_back(grad * wide_gain, n, scale)).astype(BF16)
    written.append(fetch(grad_tokens, grad_tokens_to, 6))
    sums_second.wait()
    sums[...] = sums_second.total()
    for k, (first, own) in enumerate(zip((0, 8, 12, 16), g_vectors)):
        if k != 1:
            own[...] = pick_own(sums, first, own.shape[1], shard)
    poll("rows")
    if direct:
        written += [fetch(x, to, 7 + k) for k, (x, to) in enumerate(zip(results[:2], results_to))]
    ng_second.wait()
    size = g_vectors[1].shape[1]
    start = shard * size
    row = ng_chan[start // chans]
    g_vectors[1][...] = pltpu.roll(row, lax.rem(128 - lax.rem(start, chans), 128), 1)[0:1, :size]
    if direct:
        gather_copies.finish()
        scatter_copies.finish()
        assert all(x.at == len(x.stages) for x in parts.values())
    for copy in written:
        copy.wait()


def whole(tokens, cot, lengths, log_step, skip, mode_parts, vectors, weights, mb, n_dp, nj):
    width, feats = tokens.shape
    chans = feats // nj
    t = width // mb
    h = t // SPAN
    blocks = nj * h
    rows = mb * blocks
    packs = chans // PACK
    groups = chans // 4
    direct = nj == 8 and n_dp == 4 and packs == 4 and all(w.shape[0] % 16 == 0 for w in weights)
    if not direct:
        weights = [lax.all_gather(w, ("dp", "chan"), axis=0, tiled=True) for w in weights]
        weights = [w.reshape(4, 2, 2, 2, -1, w.shape[1]) for w in weights]
    per = [w.shape[-2:] for w in weights]
    full = [(4, 2, 2, 2) + p for p in per]
    ff = per[1][1]
    shape = jax.ShapeDtypeStruct
    shapes = [shape((width, feats), BF16)] * 2 + [shape((1, chans), F32)] * 2
    shapes += [shape(x.shape, F32) for x in mode_parts] + [shape(x.shape, F32) for x in vectors]
    shapes += [shape(p, F32) for p in per] if direct else [shape(f, BF16) for f in full]
    dma, vm = pltpu.SemaphoreType.DMA, pltpu.VMEM
    sheet, grid = (32, 128), (groups, 128)
    scratch = [vm((width, feats), BF16)] * 4 + [vm((nj, chans, width), BF16)] * 6 + [
        vm((packs, rows * PACK, 128), F32),
        vm((packs, 4, blocks * PACK, 128), F32),
        vm((width, feats), BF16), vm((width, ff), BF16), vm((width, ff), BF16), vm((width, 2 * feats), BF16),
        vm((width, feats), F32), vm((width, feats), F32), vm((width, feats), F32), vm((width, ff), F32),
        vm((n_dp,) + sheet, F32), vm((nj,) + sheet, F32), vm((n_dp,) + sheet, F32), vm((nj,) + sheet, F32),
        vm((n_dp, 4, mode_parts[0].shape[0], 128), F32),
        vm((n_dp, 5) + grid, F32), vm((n_dp, chans, 128), F32), vm((nj, 8, 128), F32),
        vm((5,) + grid, F32), vm(sheet, F32), vm(sheet, F32), vm((chans, 128), F32), vm((chans, 128), F32), vm((192, 128), F32),
        vm((18,) + grid, F32),
        vm((rows * PACK, 128), F32), vm((rows * PACK, 128), F32), vm((rows * PACK, 128), F32),
        vm((4, blocks * PACK, 128), F32),
        vm((PACK, 128), F32), vm((chans, SPAN, 128), BF16), vm((groups, SPAN, 512), BF16), vm((groups, SPAN, 256), BF16),
        dma((8, 2)), dma((2, packs)), dma((2, packs)), dma((2, mb)), dma((2, packs)), dma((10,)),
    ]
    if direct:
        scratch += [vm(f, BF16) for f in full] * 2 + [vm(p, F32) for p in per]
        (r0, k0), (r1, k1), (r2, k2) = per
        sizes = [(r0, k0), (r1, k1 // 2), (r1, k1 // 2), (r2 // 2, k2), (r2 // 2, k2)]
        for size, dp_last in zip(sizes, SCATTER_DP_LAST):
            scratch += [vm(x, BF16) for x in scatter_boxes(size, dp_last)]
        scratch += [dma((2, 70)), dma((2, 55))]
    vmem, anywhere = pl.BlockSpec(memory_space=pltpu.VMEM), pl.BlockSpec(memory_space=pl.ANY)
    outs = pl.pallas_call(
        functools.partial(whole_kernel, (nj, chans, mb, h), n_dp, direct),
        out_shape=shapes,
        in_specs=[anywhere] * 2 + [vmem] * 13 + [anywhere if direct else vmem] * 3,
        out_specs=[anywhere] * 2 + [vmem] * 10 + [anywhere if direct else vmem] * 3,
        scratch_shapes=scratch,
        compiler_params=pltpu.CompilerParams(collective_id=0, has_side_effects=True, vmem_limit_bytes=63 << 20),
        name="whole",
    )(tokens, cot, lengths, log_step, skip, *mode_parts, *vectors, *(jnp.asarray(x) for x in wave_tables()), *weights)
    if direct:
        return deliver(outs)
    outs, grads = outs[:12], outs[12:]
    grads = [lax.psum_scatter(g.reshape(-1, g.shape[-1]).astype(F32), ("dp", "chan"), scatter_dimension=0, tiled=True) for g in grads]
    return deliver(outs) + grads


def deliver_kernel(*refs):
    n = (len(refs) - 1) // 2
    sems = refs[-1]
    copies = [pltpu.make_async_copy(refs[k], refs[n + k], sems.at[k]) for k in range(n)]
    for copy in copies:
        copy.start()
    for copy in copies:
        copy.wait()


def deliver(arrays):
    return list(pl.pallas_call(
        deliver_kernel,
        out_shape=[jax.ShapeDtypeStruct(x.shape, x.dtype) for x in arrays],
        in_specs=[pl.BlockSpec(memory_space=pltpu.VMEM)] * len(arrays),
        out_specs=[pl.BlockSpec(memory_space=pl.ANY)] * len(arrays),
        scratch_shapes=[pltpu.SemaphoreType.DMA((len(arrays),))],
        name="deliver",
    )(*arrays))


def on_device(
    tokens, cotangent, lengths, norm_gain, log_step, log_decay, frequency, readout_real, readout_imaginary,
    skip_gain, out_weight, out_bias, ffn_gain, in_weight, in_bias, back_weight,
):
    mb, rows, feats = tokens.shape
    nj, n_dp = lax.axis_size("chan"), lax.axis_size("dp")
    flat_rows = (mb * rows, feats)
    block_out, grad_tokens, g_ls, g_skip, g_ld, g_fr, g_rr, g_ri, g_bo, g_g1, g_g2, g_bi, g_out, g_in, g_back = whole(
        tokens.reshape(flat_rows), cotangent.reshape(flat_rows), lengths.T, log_step.reshape(1, -1), skip_gain.reshape(1, -1),
        [x.T for x in (log_decay, frequency, readout_real, readout_imaginary)],
        [x.reshape(1, -1) for x in (out_bias, norm_gain, ffn_gain, in_bias)],
        (out_weight, in_weight, back_weight), mb, n_dp, nj)
    return (
        block_out.reshape(tokens.shape), grad_tokens.reshape(tokens.shape), g_g1.reshape(-1), g_ls.reshape(-1),
        g_ld.T, g_fr.T, g_rr.T, g_ri.T, g_skip.reshape(-1), g_out, g_bo.reshape(-1), g_g2.reshape(-1), g_in, g_bi.reshape(-1), g_back,
    )


def solution(mesh):
    both = ("dp", "chan")
    rows, row, vec, chan, mode = P(None, both, None), P(both, None), P(both), P("chan"), P("chan", "dp")
    return jax.shard_map(
        on_device, mesh=mesh,
        in_specs=(rows, rows, P(None, "dp"), vec, chan, mode, mode, mode, mode, chan, row, vec, vec, row, vec, row),
        out_specs=(rows, rows, vec, chan, mode, mode, mode, mode, chan, row, vec, vec, row, vec, row),
        check_vma=False,
    )
```
